32 devices in a mesh: shot: 4 (over x, core), gx: 4 (over z), gy: 2 (over y).
Axes of the slice: x: 2, y: 2, z: 4, core: 2. Of those that a mesh axis runs over, the one named last changes fastest.
Arguments:
- velocity: bfloat16 [512, 64, 256], P(('shot', 'gx'), 'gy'), may hold values from 0.14941406 to 0.34960938
- epsilon: bfloat16 [512, 64, 256], P(('shot', 'gx'), 'gy'), may hold values from 0.049804688 to 0.29882812
- delta: bfloat16 [512, 64, 256], P(('shot', 'gx'), 'gy'), may hold values from 0.019897461 to 0.14941406
- anchors: int32 [4], replicated, may hold values from 0 to 384
- sources: int32 [4, 3], P('shot'), may hold values from 0 to 255, as said below
- wavelet: float32 [4, 4], P('shot'), may hold values from -8 to 8
- p_now: float32 [4, 128, 64, 256], P('shot', 'gx', 'gy'), may hold values from -6 to 6
- p_prev: float32 [4, 128, 64, 256], P('shot', 'gx', 'gy'), may hold values from -6 to 6
- q_now: float32 [4, 128, 64, 256], P('shot', 'gx', 'gy'), may hold values from -6 to 6
- q_prev: float32 [4, 128, 64, 256], P('shot', 'gx', 'gy'), may hold values from -6 to 6
Outputs:
- p_out: float32 [4, 128, 64, 256], P('shot', 'gx', 'gy')
- q_out: float32 [4, 128, 64, 256], P('shot', 'gx', 'gy')
The draws below stay inside these ranges and needn't reach their ends.
Inputs may be any that keep to these rules, and one draw needn't show every extreme that they name: `sources`: each source lies inside its aperture: x below 128, y below 64, z below 256; some source lies on the aperture's far end along its longest dimension, and some source has x equal to 0.
All inputs are finite; a program needn't handle non-finite values.
Results may differ from the reference program's by a relative error of at most 0.0003.
Values may be sent and summed in bfloat16 or wider, within the bound.
No kernel may reach another device: no remote copies, remote signals or barrier semaphores. Data moves between devices by JAX's collectives and lax.ppermute only.
A program may use at most 128 MiB of HBM per device.

```python
import math
import jax
import jax.numpy as jnp
from jax import lax

NZ = 256
STEPS = 4
AX = 128
AY = 64
MX = 512
N_SHOT = 4


def draw_sources(key, part):
    keys = jax.random.split(key, 5)
    largest = max(AX, max(AY, NZ))
    far_shot = jax.random.randint(keys[3], (), 0, N_SHOT)
    near_shot = (far_shot + jax.random.randint(keys[4], (), 1, max(N_SHOT, 2))) % N_SHOT
    shot_ids = jnp.arange(N_SHOT, dtype=jnp.int32)[:, None]
    columns = []
    for column_index, extent in enumerate((AX, AY, NZ)):
        column = jax.random.randint(keys[column_index], (N_SHOT, 1), 0, extent)
        if extent == largest:
            column = jnp.where(shot_ids == far_shot, extent - 1, column)
        if column_index == 0:
            column = jnp.where(shot_ids == near_shot, 0, column)
        columns.append(column)
    return jnp.concatenate(columns, 1).astype(jnp.int32)


def with_ends(entries, rng, least, top_value):
    spot = [jax.random.randint(jax.random.fold_in(rng, axis), (), 0, length) for axis, length in enumerate(entries.shape)]
    main_axis = entries.shape.index(max(entries.shape))
    next_to = spot[:main_axis] + [(spot[main_axis] + 1) % entries.shape[main_axis]] + spot[main_axis + 1:]
    return entries.at[tuple(spot)].set(least).at[tuple(next_to)].set(top_value)


def block_levels(stream_key, dims, cuts, least, high):
    loudness, own = 1.0, jax.random.fold_in(stream_key, 6)
    for dim, parts in cuts:
        draws = jnp.exp(jax.random.uniform(jax.random.fold_in(own, dim), (parts,), jnp.float32, least / len(cuts), high / len(cuts)))
        loudness = loudness * jnp.repeat(draws, dims[dim] // parts).reshape([-1 if axis == dim else 1 for axis in range(len(dims))])
    return loudness


def gaussian(rng, shape, scale, most, cuts=(), kind=jnp.bfloat16):
    loudness = block_levels(rng, shape, cuts, -0.22, 0.18) if cuts else 1.0
    values = jax.random.normal(rng, shape, jnp.float32) * scale * loudness
    return jnp.minimum(jnp.maximum(values, -most), most).astype(kind)


def setup_inputs(seed: int = 0) -> dict:
    arg_keys = jax.random.split(jax.random.key(seed), 11)
    return {
        "velocity": jnp.clip(jnp.exp(math.log(0.34960938) - 0.8500951 * jax.random.uniform(arg_keys[0], (MX, AY, NZ), jnp.float32) ** block_levels(arg_keys[0], (MX, AY, NZ), ((0, 16), (1, 2)), -0.2, 0.2)), 0.14941406, 0.34960938).astype(jnp.bfloat16),
        "epsilon": jnp.clip(jnp.exp(math.log(0.29882812) - 1.7917595 * jax.random.uniform(arg_keys[1], (MX, AY, NZ), jnp.float32) ** block_levels(arg_keys[1], (MX, AY, NZ), ((0, 16), (1, 2)), -0.2, 0.2)), 0.049804688, 0.29882812).astype(jnp.bfloat16),
        "delta": jnp.clip(jnp.exp(math.log(0.14941406) - 2.0161293 * jax.random.uniform(arg_keys[2], (MX, AY, NZ), jnp.float32) ** block_levels(arg_keys[2], (MX, AY, NZ), ((0, 16), (1, 2)), -0.2, 0.2)), 0.019897461, 0.14941406).astype(jnp.bfloat16),
        "anchors": with_ends(jax.random.randint(arg_keys[3], (N_SHOT,), 0, MX - AX + 1), jax.random.fold_in(arg_keys[3], 1), 0, MX - AX).astype(jnp.int32),
        "sources": draw_sources(jax.random.fold_in(arg_keys[10], 71), 0),
        "wavelet": gaussian(arg_keys[5], (N_SHOT, STEPS), 2.0, 8.0, ((0, 4),), jnp.float32),
        "p_now": gaussian(arg_keys[6], (N_SHOT, AX, AY, NZ), 1.0, 6.0, ((0, 4), (1, 4), (2, 2)), jnp.float32),
        "p_prev": gaussian(arg_keys[7], (N_SHOT, AX, AY, NZ), 1.0, 6.0, ((0, 4), (1, 4), (2, 2)), jnp.float32),
        "q_now": gaussian(arg_keys[8], (N_SHOT, AX, AY, NZ), 1.0, 6.0, ((0, 4), (1, 4), (2, 2)), jnp.float32),
        "q_prev": gaussian(arg_keys[9], (N_SHOT, AX, AY, NZ), 1.0, 6.0, ((0, 4), (1, 4), (2, 2)), jnp.float32),
    }


STENCIL_WEIGHTS = (-205.0 / 72.0, 8.0 / 5.0, -1.0 / 5.0, 8.0 / 315.0, -1.0 / 560.0)

def shifted_up(values, reach):
    filler = jnp.zeros(values.shape[:-1] + (reach,), values.dtype)
    return jnp.concatenate([values[..., reach:], filler], -1)

def shifted_down(values, reach):
    filler = jnp.zeros(values.shape[:-1] + (reach,), values.dtype)
    return jnp.concatenate([filler, values[..., :-reach]], -1)

def vertical_second(values):
    total = STENCIL_WEIGHTS[0] * values
    for reach in range(1, 5):
        total = total + STENCIL_WEIGHTS[reach] * (shifted_up(values, reach) + shifted_down(values, reach))
    return total

def horizontal_second(padded, x_count, y_count):
    x_total = STENCIL_WEIGHTS[0] * padded[4:4 + x_count, 4:4 + y_count]
    for reach in range(1, 5):
        x_total = x_total + STENCIL_WEIGHTS[reach] * (padded[4 + reach:4 + reach + x_count, 4:4 + y_count] + padded[4 - reach:4 - reach + x_count, 4:4 + y_count])
    y_total = STENCIL_WEIGHTS[0] * padded[4:4 + x_count, 4:4 + y_count]
    for reach in range(1, 5):
        y_total = y_total + STENCIL_WEIGHTS[reach] * (padded[4:4 + x_count, 4 + reach:4 + reach + y_count] + padded[4:4 + x_count, 4 - reach:4 - reach + y_count])
    return x_total + y_total

def update(padded_p, p_field, p_before, q_field, q_before, courant_sq, horiz_gain, cross_gain):
    laplace_h = horizontal_second(padded_p, p_field.shape[0], p_field.shape[1])
    depth_term = vertical_second(q_field)
    p_next = 2.0 * p_field - p_before + courant_sq * (horiz_gain * laplace_h + cross_gain * depth_term)
    q_next = 2.0 * q_field - q_before + courant_sq * (cross_gain * laplace_h + depth_term)
    return (p_next, q_next)

def reference(velocity, epsilon, delta, anchors, sources, wavelet, p_now, p_prev, q_now, q_prev):
    results_p = []
    results_q = []
    for shot_group in range(N_SHOT):
        anchor_row = anchors[shot_group].astype(jnp.int32)
        velocity_block = lax.dynamic_slice_in_dim(velocity, anchor_row, AX, 0).astype(jnp.float32)
        epsilon_block = lax.dynamic_slice_in_dim(epsilon, anchor_row, AX, 0).astype(jnp.float32)
        delta_block = lax.dynamic_slice_in_dim(delta, anchor_row, AX, 0).astype(jnp.float32)
        courant_sq = velocity_block * velocity_block
        horiz_gain = 1.0 + 2.0 * epsilon_block
        cross_gain = jnp.sqrt(1.0 + 2.0 * delta_block)
        p_field = p_now[shot_group]
        p_before = p_prev[shot_group]
        q_field = q_now[shot_group]
        q_before = q_prev[shot_group]
        for step_index in range(STEPS):
            padded = jnp.pad(p_field, ((4, 4), (4, 4), (0, 0)))
            p_next, q_next = update(padded, p_field, p_before, q_field, q_before, courant_sq, horiz_gain, cross_gain)
            p_next = p_next.at[sources[shot_group, 0], sources[shot_group, 1], sources[shot_group, 2]].add(wavelet[shot_group, step_index])
            p_before, p_field, q_before, q_field = (p_field, p_next, q_field, q_next)
        results_p.append(p_field)
        results_q.append(q_field)
    return (jnp.stack(results_p), jnp.stack(results_q))
```

```python
import functools

import jax
import jax.numpy as jnp
import numpy as np
from jax import lax
from jax.experimental import pallas as pl
from jax.experimental.pallas import tpu as pltpu
from jax.sharding import PartitionSpec as P

STEPS = 4
REACH = 4
SCALE = 5040.0
CENTER = -14350.0
OUTER = (8064.0, -1008.0, 128.0, -9.0)
BUCKET = 4
XT = 8
YPAD = 16
VMEM_LIMIT = 24 * 1024 * 1024


def shot_row(anchor, residue, period):
    return anchor // period + (residue < anchor % period).astype(jnp.int32)


def rotation_branches(n_gx, rows):
    def perm(block, by):
        by %= n_gx
        if by == 0:
            return block
        return lax.ppermute(block, "gx", [(i, (i - by) % n_gx) for i in range(n_gx)])

    def branch(turn, bucket):
        def aligned(block):
            moved = perm(block, turn)
            return jnp.concatenate([moved, jnp.zeros_like(moved[: BUCKET - 1])], 0)

        def split(block):
            k = BUCKET * (bucket - 1)
            return jnp.concatenate(
                [perm(block[k + 1 :], turn), perm(block[: k + BUCKET], turn + 1)], 0
            )

        return aligned if bucket == 0 else split

    return [branch(t, b) for t in range(n_gx) for b in range(rows // BUCKET + 1)]


def model_windows(anchors, fields):
    shot = lax.axis_index("shot")
    gx = lax.axis_index("gx")
    n_gx = lax.axis_size("gx")
    n_shot = lax.axis_size("shot")
    rows = fields[0].shape[0]
    period = n_gx * rows
    residue = gx * rows + jnp.arange(rows, dtype=jnp.int32)
    half, core = shot // 2, shot % 2
    anchor = anchors[shot]
    own = shot_row(anchor, residue, period)[:, None, None]
    far = shot_row(anchors[shot ^ 2], residue, period)[:, None, None]
    turn = (anchor // rows) % n_gx
    rest = anchor % rows
    index = turn * (rows // BUCKET + 1) + jnp.where(rest > 0, (rest - 1) // BUCKET + 1, 0)
    first = jnp.where(rest > 0, (rest - 1) % BUCKET, 0)
    branches = rotation_branches(n_gx, rows)

    beside = [(i, i ^ 1) for i in range(n_shot)]
    across = [(i, i ^ 2) for i in range(n_shot)]
    pairs = []
    for field in fields:
        other = lax.ppermute(field, "shot", beside)
        pairs.append((jnp.where(core == 0, field, other), jnp.where(core == 0, other, field)))
    to_send = [jnp.where(far % 2 == 1, odd, even) for even, odd in pairs]
    crossed, windows = [], []
    for k, (even, odd) in enumerate(pairs):
        send = to_send[k]
        if k >= 1:
            send, crossed[k - 1] = lax.optimization_barrier((send, crossed[k - 1]))
        if k >= 2:
            send, windows[k - 2] = lax.optimization_barrier((send, windows[k - 2]))
        crossed.append(lax.ppermute(send, "shot", across))
        if k >= 1:
            windows.append(rotate(index, branches, own, half, pairs[k - 1], crossed[k - 1]))
    windows.append(rotate(index, branches, own, half, pairs[-1], crossed[-1]))
    return windows, first


def rotate(index, branches, own, half, pair, crossed):
    even, odd = pair
    block = jnp.where(own // 2 == half, jnp.where(own % 2 == 1, odd, even), crossed)
    return lax.switch(index, branches, block)


def swaps(count):
    near = [(i, i ^ 1) for i in range(count) if i ^ 1 < count]
    off = [(i, i + 1) for i in range(1, count - 1, 2)]
    return near, off + [(b, a) for a, b in off]


def exchange(rims):
    got = []
    for rim, axis, which in zip(rims, ("gx", "gx", "gy", "gy"), (0, 1, 0, 1)):
        pairs = swaps(lax.axis_size(axis))[which]
        got.append(lax.ppermute(rim, axis, pairs) if pairs else jnp.zeros_like(rim))
    return got


def depth_matrix(nz):
    out = np.zeros((nz, nz), np.float32)
    for k, weight in enumerate(OUTER, 1):
        out += weight * (np.eye(nz, k=k, dtype=np.float32) + np.eye(nz, k=-k, dtype=np.float32))
    return out


def plane_matrix(ny, y_odd):
    width = ny + YPAD
    out = np.zeros((XT, ny, XT + 2 * REACH, width), np.float32)
    first, second = (-REACH, ny) if y_odd else (ny, -REACH)
    column = np.zeros((ny, width), np.float32)
    for y in range(ny):
        for k, weight in enumerate(OUTER, 1):
            for at in (y - k, y + k):
                if 0 <= at < ny:
                    column[y, at] += weight
                elif first <= at < first + REACH:
                    column[y, ny + at - first] += weight
                elif second <= at < second + REACH:
                    column[y, ny + REACH + at - second] += weight
    for x in range(XT):
        out[x, :, x + REACH, :] = column
        for k, weight in enumerate(OUTER, 1):
            for at in (x + REACH - k, x + REACH + k):
                out[x, np.arange(ny), at, np.arange(ny)] += weight
    return out.reshape(XT * ny, (XT + 2 * REACH) * width)


def split(values):
    high = values.astype(jnp.bfloat16)
    return high, (values - high.astype(jnp.float32)).astype(jnp.bfloat16)


def step_kernel(step, last, where_ref, wave_ref, *refs):
    p_ref, pb_ref, q_ref, qb_ref, xa_ref, xb_ref, ya_ref, yb_ref, dz_ref, dh_ref = refs[:10]
    refs = refs[10:]
    if step == 0:
        v_ref, e_ref, d_ref = refs[:3]
        po_ref, qo_ref, sxa_ref, sxb_ref, sya_ref, syb_ref, a_ref, b_ref, c_ref = refs[3:12]
        refs = refs[12:]
    else:
        a_ref, b_ref, c_ref = refs[:3]
        po_ref, qo_ref = refs[3:5]
        refs = refs[5:]
        if not last:
            sxa_ref, sxb_ref, sya_ref, syb_ref = refs[:4]
            refs = refs[4:]
    high_ref, low_ref = refs
    nx, ny, nz = p_ref.shape
    wide = ny + YPAD
    x_odd, y_odd, lx, ly, lz, inside, first = (where_ref[i] for i in range(7))
    f32 = jnp.float32

    for x in range(0, nx, XT):
        high, low = split(p_ref[x : x + XT])
        high_ref[REACH + x : REACH + x + XT, 0:ny] = high
        low_ref[REACH + x : REACH + x + XT, 0:ny] = low
        ends = jnp.concatenate(
            [ya_ref[x : x + XT], yb_ref[x : x + XT], jnp.zeros((XT, YPAD - 2 * REACH, nz), f32)], 1
        )
        high, low = split(ends)
        high_ref[REACH + x : REACH + x + XT, ny:wide] = high
        low_ref[REACH + x : REACH + x + XT, ny:wide] = low
    for ref, at in ((xa_ref, (1 - x_odd) * (nx + REACH)), (xb_ref, x_odd * (nx + REACH))):
        high, low = split(ref[...])
        high_ref[pl.ds(at, REACH), 0:ny] = high
        low_ref[pl.ds(at, REACH), 0:ny] = low
        high_ref[pl.ds(at, REACH), ny:wide] = jnp.zeros((REACH, YPAD, nz), jnp.bfloat16)
        low_ref[pl.ds(at, REACH), ny:wide] = jnp.zeros((REACH, YPAD, nz), jnp.bfloat16)

    dot = functools.partial(jnp.dot, preferred_element_type=f32)
    flat = (XT * ny, nz)
    for x in range(0, nx, XT):
        tile = slice(x, x + XT)
        if step == 0:
            rows = pl.ds(first + x, XT)
            vel = v_ref[rows].astype(f32)
            speed = vel * vel * f32(1.0 / SCALE)
            cross = jnp.sqrt(1.0 + 2.0 * d_ref[rows].astype(f32))
            a = (speed * (1.0 + 2.0 * e_ref[rows].astype(f32))).reshape(flat)
            b = (speed * cross).reshape(flat)
            c = speed.reshape(flat)
            a_ref[tile] = a.reshape(XT, ny, nz)
            b_ref[tile] = b.reshape(XT, ny, nz)
            c_ref[tile] = speed
        else:
            a, b, c = (ref[tile].reshape(flat) for ref in (a_ref, b_ref, c_ref))
        p = p_ref[tile].reshape(flat)
        q = q_ref[tile].reshape(flat)
        window = slice(x, x + XT + 2 * REACH)
        deep = ((XT + 2 * REACH) * wide, nz)
        across = (
            dot(dh_ref[...], high_ref[window].reshape(deep))
            + dot(dh_ref[...], low_ref[window].reshape(deep))
            + f32(2 * CENTER) * p
        )
        high, low = split(q)
        down = dot(high, dz_ref[...]) + dot(low, dz_ref[...]) + f32(CENTER) * q
        po_ref[tile] = (2.0 * p - pb_ref[tile].reshape(flat) + (a * across + b * down)).reshape(XT, ny, nz)
        qo_ref[tile] = (2.0 * q - qb_ref[tile].reshape(flat) + (b * across + c * down)).reshape(XT, ny, nz)

    @pl.when(inside == 1)
    def _():
        y_tile = pl.ds(pl.multiple_of(ly // 8 * 8, 8), 8)
        at_y = lax.broadcasted_iota(jnp.int32, (1, 8, nz), 1) == ly % 8
        at_z = lax.broadcasted_iota(jnp.int32, (1, 8, nz), 2) == lz
        old = po_ref[pl.ds(lx, 1), y_tile, :]
        po_ref[pl.ds(lx, 1), y_tile, :] = old + jnp.where(at_y & at_z, wave_ref[step], 0.0)

    if not last:
        sxa_ref[...] = po_ref[pl.ds((1 - x_odd) * (nx - REACH), REACH)]
        sxb_ref[...] = po_ref[pl.ds(x_odd * (nx - REACH), REACH)]
        for x in range(0, nx, XT):
            head = po_ref[x : x + XT, 0:REACH]
            tail = po_ref[x : x + XT, ny - REACH : ny]
            odd = jnp.broadcast_to(y_odd, head.shape) == 1
            sya_ref[x : x + XT] = jnp.where(odd, head, tail)
            syb_ref[x : x + XT] = jnp.where(odd, tail, head)


def run_step(step, last, where, wave, arrays):
    nx, ny, nz = arrays[0].shape
    whole = (nx, ny, nz)
    rims = [(REACH, ny, nz)] * 2 + [(nx, REACH, nz)] * 2
    vmem = pl.BlockSpec(memory_space=pltpu.VMEM)
    smem = pl.BlockSpec(memory_space=pltpu.SMEM)
    f32 = jnp.float32
    if last:
        out = [jax.ShapeDtypeStruct(whole, f32)] * 2
    else:
        out = [pltpu.VMEM(whole, f32)] * 2 + [jax.ShapeDtypeStruct(r, f32) for r in rims]
    if step == 0:
        out += [pltpu.VMEM(whole, f32)] * 3
    arrays = [pltpu.with_memory_space_constraint(a, pltpu.VMEM) for a in arrays]
    padded = (nx + 2 * REACH, ny + YPAD, nz)
    return pl.pallas_call(
        functools.partial(step_kernel, step, last),
        out_shape=out,
        in_specs=[smem, smem] + [vmem] * len(arrays),
        out_specs=[vmem] * len(out),
        scratch_shapes=[pltpu.VMEM(padded, jnp.bfloat16)] * 2,
        compiler_params=pltpu.CompilerParams(vmem_limit_bytes=VMEM_LIMIT),
        name=f"step_{step}",
    )(where, wave, *arrays)


def on_device(velocity, epsilon, delta, anchors, sources, wavelet, p_now, p_prev, q_now, q_prev):
    p, pb, q, qb = p_now[0], p_prev[0], q_now[0], q_prev[0]
    nx, ny, nz = p.shape
    gx, gy = lax.axis_index("gx"), lax.axis_index("gy")
    x_odd, y_odd = gx % 2, gy % 2
    rims = [
        lax.dynamic_slice_in_dim(p, (1 - x_odd) * (nx - REACH), REACH, 0),
        lax.dynamic_slice_in_dim(p, x_odd * (nx - REACH), REACH, 0),
        lax.dynamic_slice_in_dim(p, (1 - y_odd) * (ny - REACH), REACH, 1),
        lax.dynamic_slice_in_dim(p, y_odd * (ny - REACH), REACH, 1),
    ]
    rims = exchange(rims)
    windows, first = model_windows(anchors, (velocity, epsilon, delta))
    lx, ly, lz = sources[0, 0] - gx * nx, sources[0, 1] - gy * ny, sources[0, 2]
    inside = (lx >= 0) & (lx < nx) & (ly >= 0) & (ly < ny)
    place = [x_odd, y_odd, lx, ly, lz, inside, first]
    place = jnp.stack([jnp.asarray(v, jnp.int32) for v in place])
    wave = wavelet[0]
    dz = jnp.asarray(depth_matrix(nz), jnp.bfloat16)
    dh = jnp.where(
        y_odd == 1,
        jnp.asarray(plane_matrix(ny, True), jnp.bfloat16),
        jnp.asarray(plane_matrix(ny, False), jnp.bfloat16),
    )
    for step in range(STEPS):
        last = step == STEPS - 1
        coefs = windows if step == 0 else coefs
        out = run_step(step, last, place, wave, [p, pb, q, qb, *rims, dz, dh, *coefs])
        pb, qb = p, q
        p, q = out[:2]
        if not last:
            rims = exchange(out[2:6])
        if step == 0:
            coefs = out[6:9]
    return p[None], q[None]


def solution(mesh):
    model = P(("shot", "gx"), "gy", None)
    field = P("shot", "gx", "gy", None)
    return jax.shard_map(
        on_device,
        mesh=mesh,
        in_specs=(model, model, model, P(), P("shot", None), P("shot", None)) + (field,) * 4,
        out_specs=(field, field),
        check_vma=False,
    )
```

```python
import functools

import jax
import jax.numpy as jnp
import numpy as np
from jax import lax
from jax.experimental import pallas as pl
from jax.experimental.pallas import tpu as pltpu
from jax.sharding import PartitionSpec as P

STEPS = 4
REACH = 4
SCALE = 5040.0
CENTER = -14350.0
OUTER = (8064.0, -1008.0, 128.0, -9.0)
BUCKET = 8
XT = 8
VMEM_LIMIT = 16 * 1024 * 1024


def shot_row(anchor, residue, period):
    return anchor // period + (residue < anchor % period).astype(jnp.int32)


def rotation_branches(n_gx, rows):
    def perm(block, by):
        by %= n_gx
        if by == 0:
            return block
        return lax.ppermute(block, "gx", [(i, (i - by) % n_gx) for i in range(n_gx)])

    def branch(turn, bucket):
        def aligned(block):
            moved = perm(block, turn)
            return jnp.concatenate([moved, jnp.zeros_like(moved[: BUCKET - 1])], 0)

        def split(block):
            k = BUCKET * (bucket - 1)
            return jnp.concatenate(
                [perm(block[k + 1 :], turn), perm(block[: k + BUCKET], turn + 1)], 0
            )

        return aligned if bucket == 0 else split

    return [branch(t, b) for t in range(n_gx) for b in range(rows // BUCKET + 1)]


def model_windows(anchors, fields, beside_work):
    shot = lax.axis_index("shot")
    gx = lax.axis_index("gx")
    n_gx = lax.axis_size("gx")
    n_shot = lax.axis_size("shot")
    rows = fields[0].shape[0]
    period = n_gx * rows
    residue = gx * rows + jnp.arange(rows, dtype=jnp.int32)
    half, core = shot // 2, shot % 2
    anchor = anchors[shot]
    own = shot_row(anchor, residue, period)[:, None, None]
    far = shot_row(anchors[shot ^ 2], residue, period)[:, None, None]
    turn = (anchor // rows) % n_gx
    rest = anchor % rows
    index = turn * (rows // BUCKET + 1) + jnp.where(rest > 0, (rest - 1) // BUCKET + 1, 0)
    first = jnp.where(rest > 0, (rest - 1) % BUCKET, 0)
    branches = rotation_branches(n_gx, rows)

    beside = [(i, i ^ 1) for i in range(n_shot)]
    across = [(i, i ^ 2) for i in range(n_shot)]

    def select(which, field, other):
        return jnp.where(which % 2 == core, field, other)

    def turned(field, other, crossed):
        block = jnp.where(own // 2 == half, select(own, field, other), crossed)
        return lax.switch(index, branches, block)

    others = [lax.ppermute(field, "shot", beside) for field in fields]
    sends = [select(far, fields[0], others[0])]
    sends[0], rest_others = lax.optimization_barrier((sends[0], others[1:]))
    others = [others[0], *rest_others]
    sends += [select(far, f, o) for f, o in zip(fields[1:], others[1:])]
    crossed = [lax.ppermute(sends[0], "shot", across)]
    work = beside_work(index, first)
    sends[1], sends[2], crossed[0], work = lax.optimization_barrier((sends[1], sends[2], crossed[0], work))
    crossed.append(lax.ppermute(sends[1], "shot", across))
    windows = [turned(fields[0], others[0], crossed[0])]
    sends[2], crossed[1], windows[0] = lax.optimization_barrier((sends[2], crossed[1], windows[0]))
    crossed.append(lax.ppermute(sends[2], "shot", across))
    windows.append(turned(fields[1], others[1], crossed[1]))
    crossed[2], windows[1] = lax.optimization_barrier((crossed[2], windows[1]))
    windows.append(turned(fields[2], others[2], crossed[2]))
    return windows, work


def swaps(count):
    near = [(i, i ^ 1) for i in range(count) if i ^ 1 < count]
    off = [(i, i + 1) for i in range(1, count - 1, 2)]
    return near, off + [(b, a) for a, b in off]


def exchange(rims):
    got = []
    for rim, axis, which in zip(rims, ("gx", "gx", "gy", "gy"), (0, 1, 0, 1)):
        pairs = swaps(lax.axis_size(axis))[which]
        got.append(lax.ppermute(rim, axis, pairs) if pairs else jnp.zeros_like(rim))
    return got


def depth_matrix(nz):
    out = np.zeros((nz, nz), np.float32)
    for k, weight in enumerate(OUTER, 1):
        out += weight * (np.eye(nz, k=k, dtype=np.float32) + np.eye(nz, k=-k, dtype=np.float32))
    return out


def plane_matrix(ny):
    out = np.zeros((XT, ny, XT + 2 * REACH, ny), np.float32)
    column = depth_matrix(ny)
    for x in range(XT):
        out[x, :, x + REACH, :] = column
        for k, weight in enumerate(OUTER, 1):
            for at in (x + REACH - k, x + REACH + k):
                out[x, np.arange(ny), at, np.arange(ny)] += weight
    return out.reshape(XT * ny, (XT + 2 * REACH) * ny)


def side_matrix(nx):
    out = np.zeros((nx, 16, 2, nx, REACH), np.float32)
    for y in range(REACH):
        for k, weight in enumerate(OUTER, 1):
            if y - k < 0:
                out[np.arange(nx), y, 0, np.arange(nx), y - k + REACH] = weight
                out[np.arange(nx), 15 - y, 1, np.arange(nx), k - y - 1] = weight
    return out.reshape(nx * 16, 2 * nx * REACH)


def split(values):
    high = values.astype(jnp.bfloat16)
    return high, (values - high.astype(jnp.float32)).astype(jnp.bfloat16)


def dot(a, b):
    return jnp.dot(a, b, preferred_element_type=jnp.float32)


def neighbours(p_ref, q_ref, dh_ref, dz_ref, high_ref, low_ref, use):
    nx, ny, nz = p_ref.shape
    flat = (XT * ny, nz)
    for ref in (high_ref, low_ref):
        ref[0:REACH] = jnp.zeros((REACH, ny, nz), jnp.bfloat16)
        ref[nx + REACH :] = jnp.zeros((REACH, ny, nz), jnp.bfloat16)

    def cut(i, _):
        x = i * XT
        high, low = split(p_ref[pl.ds(x, XT)])
        high_ref[pl.ds(x + REACH, XT)] = high
        low_ref[pl.ds(x + REACH, XT)] = low
        return _

    lax.fori_loop(0, nx // XT, cut, None)

    def tile(i, _):
        x = i * XT
        rows = pl.ds(x, XT)
        p, q = p_ref[rows].reshape(flat), q_ref[rows].reshape(flat)
        window = pl.ds(x, XT + 2 * REACH)
        deep = ((XT + 2 * REACH) * ny, nz)
        across = dot(dh_ref[...], high_ref[window].reshape(deep))
        across += dot(dh_ref[...], low_ref[window].reshape(deep))
        high, low = split(q)
        down = dot(high, dz_ref[...]) + dot(low, dz_ref[...])
        use(rows, p, q, across + (2 * CENTER) * p, down + CENTER * q)
        return _

    lax.fori_loop(0, nx // XT, tile, None)


def rim_terms(where_ref, xa_ref, xb_ref, ya_ref, yb_ref, ds_ref, shape):
    nx, ny, nz = shape
    x_odd, y_odd = where_ref[0] == 1, where_ref[1] == 1
    xa, xb = xa_ref[...].reshape(REACH, ny, nz), xb_ref[...].reshape(REACH, ny, nz)
    below, above = jnp.where(x_odd, xa, xb), jnp.where(x_odd, xb, xa)
    near, far = [], []
    for i in range(REACH):
        near.append(sum(OUTER[i + REACH - h - 1] * below[h] for h in range(i, REACH)))
        far.append(sum(OUTER[REACH + h - i - 1] * above[h] for h in range(0, i + 1)))
    ya, yb = ya_ref[...], yb_ref[...]
    sides = jnp.concatenate([jnp.where(y_odd, ya, yb), jnp.where(y_odd, yb, ya)], 0)
    high, low = split(sides)
    side = dot(ds_ref[...], high) + dot(ds_ref[...], low)
    return jnp.stack(near), jnp.stack(far), side.reshape(nx, 16, nz)


def add_source(where_ref, wave_ref, step, p_ref):
    nz = p_ref.shape[2]
    lx, ly, lz, inside = (where_ref[i] for i in range(2, 6))

    @pl.when(inside == 1)
    def _():
        y_tile = pl.ds(pl.multiple_of(ly // 8 * 8, 8), 8)
        at_y = lax.broadcasted_iota(jnp.int32, (1, 8, nz), 1) == ly % 8
        at_z = lax.broadcasted_iota(jnp.int32, (1, 8, nz), 2) == lz
        old = p_ref[pl.ds(lx, 1), y_tile, :]
        p_ref[pl.ds(lx, 1), y_tile, :] = old + jnp.where(at_y & at_z, wave_ref[step], 0.0)


def put_rims(where_ref, p_ref, sxa_ref, sxb_ref, sya_ref, syb_ref):
    nx, ny, nz = p_ref.shape
    x_odd, y_odd = where_ref[0], where_ref[1]
    sxa_ref[...] = p_ref[pl.ds((1 - x_odd) * (nx - REACH), REACH)].reshape(REACH * ny, nz)
    sxb_ref[...] = p_ref[pl.ds(x_odd * (nx - REACH), REACH)].reshape(REACH * ny, nz)
    for x in range(0, nx, 2):
        head = jnp.concatenate([p_ref[x, 0:REACH], p_ref[x + 1, 0:REACH]], 0)
        tail = jnp.concatenate([p_ref[x, ny - REACH : ny], p_ref[x + 1, ny - REACH : ny]], 0)
        rows = slice(x * REACH, (x + 2) * REACH)
        sya_ref[rows] = jnp.where(y_odd == 1, head, tail)
        syb_ref[rows] = jnp.where(y_odd == 1, tail, head)


def open_kernel(where_ref, p_ref, pb_ref, q_ref, qb_ref, xa_ref, xb_ref, ya_ref, yb_ref, dh_ref, dz_ref, ds_ref,
                h_ref, z_ref, up_ref, uq_ref, high_ref, low_ref):
    shape = p_ref.shape
    nx, ny, nz = shape

    def use(rows, p, q, across, down):
        h_ref[rows] = across.reshape(XT, ny, nz)
        z_ref[rows] = down.reshape(XT, ny, nz)
        up_ref[rows] = 2.0 * p_ref[rows] - pb_ref[rows]
        uq_ref[rows] = 2.0 * q_ref[rows] - qb_ref[rows]

    neighbours(p_ref, q_ref, dh_ref, dz_ref, high_ref, low_ref, use)
    near, far, side = rim_terms(where_ref, xa_ref, xb_ref, ya_ref, yb_ref, ds_ref, shape)
    h_ref[0:REACH] += near
    h_ref[nx - REACH : nx] += far
    h_ref[:, 0:8] += side[:, 0:8]
    h_ref[:, ny - 8 : ny] += side[:, 8:16]


def first_kernel(where_ref, wave_ref, h_ref, z_ref, up_ref, uq_ref, v_ref, e_ref, d_ref,
                 p_ref, q_ref, a_ref, b_ref, c_ref, *rim_refs):
    nx, ny, nz = h_ref.shape
    f32 = jnp.float32
    first = where_ref[6]
    tile = 2

    def update(i, _):
        rows, model = pl.ds(i * tile, tile), pl.ds(first + i * tile, tile)
        vel = v_ref[model].astype(f32)
        c = vel * vel * f32(1.0 / SCALE)
        a = c * (1.0 + 2.0 * e_ref[model].astype(f32))
        b = c * jnp.sqrt(1.0 + 2.0 * d_ref[model].astype(f32))
        a_ref[rows], b_ref[rows], c_ref[rows] = a, b, c
        h, z = h_ref[rows], z_ref[rows]
        p_ref[rows] = up_ref[rows] + (a * h + b * z)
        q_ref[rows] = uq_ref[rows] + (b * h + c * z)
        return _

    lax.fori_loop(0, nx // tile, update, None)
    add_source(where_ref, wave_ref, 0, p_ref)
    put_rims(where_ref, p_ref, *rim_refs)


def inner_kernel(p_ref, pb_ref, q_ref, qb_ref, a_ref, b_ref, c_ref, dh_ref, dz_ref, po_ref, qo_ref, high_ref, low_ref):
    nx, ny, nz = p_ref.shape
    flat, block = (XT * ny, nz), (XT, ny, nz)

    def use(rows, p, q, across, down):
        a, b, c = (ref[rows].reshape(flat) for ref in (a_ref, b_ref, c_ref))
        po_ref[rows] = (2.0 * p - pb_ref[rows].reshape(flat) + (a * across + b * down)).reshape(block)
        qo_ref[rows] = (2.0 * q - qb_ref[rows].reshape(flat) + (b * across + c * down)).reshape(block)

    neighbours(p_ref, q_ref, dh_ref, dz_ref, high_ref, low_ref, use)


def rim_kernel(step, where_ref, wave_ref, p_in, q_in, a_ref, b_ref, xa_ref, xb_ref, ya_ref, yb_ref, ds_ref,
               p_ref, q_ref, *out_refs):
    nx, ny, nz = p_ref.shape
    near, far, side = rim_terms(where_ref, xa_ref, xb_ref, ya_ref, yb_ref, ds_ref, p_ref.shape)
    for rows, term in ((slice(0, REACH), near), (slice(nx - REACH, nx), far)):
        p_ref[rows] = p_in[rows] + a_ref[rows] * term
        q_ref[rows] = q_in[rows] + b_ref[rows] * term
    for cells, term in ((slice(0, 8), side[:, 0:8]), (slice(ny - 8, ny), side[:, 8:16])):
        p_ref[:, cells] += a_ref[:, cells] * term
        q_ref[:, cells] += b_ref[:, cells] * term
    add_source(where_ref, wave_ref, step, p_ref)
    if len(out_refs) == 4:
        put_rims(where_ref, p_ref, *out_refs)
    else:
        p_out, q_out, sem = out_refs
        copies = [pltpu.make_async_copy(p_ref, p_out, sem.at[0]), pltpu.make_async_copy(q_ref, q_out, sem.at[1])]
        for copy in copies:
            copy.start()
        for copy in copies:
            copy.wait()


def call(kernel, name, scalars, arrays, out, scratch=(), aliases=None, hbm_out=0):
    vmem = pl.BlockSpec(memory_space=pltpu.VMEM)
    smem = pl.BlockSpec(memory_space=pltpu.SMEM)
    arrays = [pltpu.with_memory_space_constraint(a, pltpu.VMEM) for a in arrays]
    return pl.pallas_call(
        kernel,
        out_shape=out,
        in_specs=[smem] * len(scalars) + [vmem] * len(arrays),
        out_specs=[vmem] * (len(out) - hbm_out) + [pl.BlockSpec(memory_space=pl.ANY)] * hbm_out,
        scratch_shapes=scratch,
        input_output_aliases=aliases or {},
        compiler_params=pltpu.CompilerParams(vmem_limit_bytes=VMEM_LIMIT),
        name=name,
    )(*scalars, *arrays)


def on_device(velocity, epsilon, delta, anchors, sources, wavelet, p_now, p_prev, q_now, q_prev):
    p, pb, q, qb = p_now[0], p_prev[0], q_now[0], q_prev[0]
    nx, ny, nz = p.shape
    gx, gy = lax.axis_index("gx"), lax.axis_index("gy")
    x_odd, y_odd = gx % 2, gy % 2
    f32 = jnp.float32
    block = pltpu.VMEM((nx, ny, nz), f32)
    rim_shapes = [jax.ShapeDtypeStruct((REACH * n, nz), f32) for n in (ny, ny, nx, nx)]
    padded = [pltpu.VMEM((nx + 2 * REACH, ny, nz), jnp.bfloat16)] * 2
    dz = jnp.asarray(depth_matrix(nz), jnp.bfloat16)
    dh = jnp.asarray(plane_matrix(ny), jnp.bfloat16)
    ds = jnp.asarray(side_matrix(nx), jnp.bfloat16)
    wave = wavelet[0]
    rims = [
        lax.dynamic_slice_in_dim(p, (1 - x_odd) * (nx - REACH), REACH, 0),
        lax.dynamic_slice_in_dim(p, x_odd * (nx - REACH), REACH, 0),
        lax.dynamic_slice_in_dim(p, (1 - y_odd) * (ny - REACH), REACH, 1),
        lax.dynamic_slice_in_dim(p, y_odd * (ny - REACH), REACH, 1),
    ]
    rims = exchange([rim.reshape(s.shape) for rim, s in zip(rims, rim_shapes)])

    def beside_work(index, first):
        lx, ly, lz = sources[0, 0] - gx * nx, sources[0, 1] - gy * ny, sources[0, 2]
        inside = (lx >= 0) & (lx < nx) & (ly >= 0) & (ly < ny)
        place = [x_odd, y_odd, lx, ly, lz, inside, first]
        place = jnp.stack([jnp.asarray(v, jnp.int32) for v in place])
        opened = call(open_kernel, "open", [place], [p, pb, q, qb, *rims, dh, dz, ds], [block] * 4, padded)
        return place, opened

    windows, (place, opened) = model_windows(anchors, (velocity, epsilon, delta), beside_work)
    pb, qb = p, q
    p, q, a, b, c, *rims = call(
        first_kernel, "first", [place, wave], [*opened, *windows], [block] * 5 + rim_shapes
    )
    for step in range(1, STEPS):
        rims = exchange(rims)
        p_new, q_new = call(inner_kernel, f"inner_{step}", [], [p, pb, q, qb, a, b, c, dh, dz], [block] * 2, padded)
        last = step == STEPS - 1
        whole = jax.ShapeDtypeStruct((nx, ny, nz), f32)
        out = call(
            functools.partial(rim_kernel, step),
            f"rims_{step}",
            [place, wave],
            [p_new, q_new, a, b, *rims, ds],
            [block] * 2 + ([whole] * 2 if last else rim_shapes),
            [pltpu.SemaphoreType.DMA((2,))] if last else [],
            {2: 0, 3: 1},
            2 if last else 0,
        )
        pb, qb = p, q
        p, q, *rims = out
    return rims[0][None], rims[1][None]


def solution(mesh):
    model = P(("shot", "gx"), "gy", None)
    field = P("shot", "gx", "gy", None)
    return jax.shard_map(
        on_device,
        mesh=mesh,
        in_specs=(model, model, model, P(), P("shot", None), P("shot", None)) + (field,) * 4,
        out_specs=(field, field),
        check_vma=False,
    )
```

```python
import functools

import jax
import jax.numpy as jnp
import numpy as np
from jax import lax
from jax.experimental import pallas as pl
from jax.experimental.pallas import tpu as pltpu
from jax.sharding import PartitionSpec as P

STEPS = 4
REACH = 4
SCALE = 5040.0
CENTER = -14350.0
OUTER = (8064.0, -1008.0, 128.0, -9.0)
BUCKET = 8
XT = 8
VMEM_LIMIT = 16 * 1024 * 1024


def row_group(anchor, gx, n_gx, rows):
    period = n_gx * rows
    group = lax.div(anchor, period)
    cut = lax.rem(anchor, period) - gx * rows
    return lambda i: jnp.where(i < cut, group + 1, group)


def pick_kernel(n_gx, ids_ref, anchors_ref, field_ref, other_ref, send_ref, *index_ref):
    rows = field_ref.shape[0]
    shot, gx = ids_ref[0], ids_ref[1]
    core = shot & 1
    group = row_group(anchors_ref[shot ^ 2], gx, n_gx, rows)
    for i in range(rows):
        send_ref[i] = jnp.where(group(i) & 1 == core, field_ref[i], other_ref[i])
    if index_ref:
        anchor = anchors_ref[shot]
        turn = lax.rem(lax.div(anchor, rows), n_gx)
        rest = lax.rem(anchor, rows)
        bucket = jnp.where(rest > 0, lax.div(rest - 1, BUCKET) + 1, 0)
        index_ref[0][0] = turn * (rows // BUCKET + 1) + bucket


def join_kernel(n_gx, ids_ref, anchors_ref, field_ref, other_ref, crossed_ref, block_ref):
    rows = field_ref.shape[0]
    shot, gx = ids_ref[0], ids_ref[1]
    core, half = shot & 1, shot >> 1
    group = row_group(anchors_ref[shot], gx, n_gx, rows)
    for i in range(rows):
        here = jnp.where(group(i) & 1 == core, field_ref[i], other_ref[i])
        block_ref[i] = jnp.where(group(i) >> 1 == half, here, crossed_ref[i])


def rotation_branches(n_gx, rows):
    def perm(block, by):
        by %= n_gx
        if by == 0:
            return block
        return lax.ppermute(block, "gx", [(i, (i - by) % n_gx) for i in range(n_gx)])

    def branch(turn, bucket):
        def aligned(block):
            moved = perm(block, turn)
            return jnp.concatenate([moved, jnp.zeros_like(moved[: BUCKET - 1])], 0)

        def split(block):
            k = BUCKET * (bucket - 1)
            return jnp.concatenate(
                [perm(block[k + 1 :], turn), perm(block[: k + BUCKET], turn + 1)], 0
            )

        return aligned if bucket == 0 else split

    return [branch(t, b) for t in range(n_gx) for b in range(rows // BUCKET + 1)]


def model_windows(ids, anchors, fields, rims, beside_work):
    n_gx = lax.axis_size("gx")
    n_shot = lax.axis_size("shot")
    rows = fields[0].shape[0]
    branches = rotation_branches(n_gx, rows)
    beside = [(i, i ^ 1) for i in range(n_shot)]
    across = [(i, i ^ 2) for i in range(n_shot)]
    like = jax.ShapeDtypeStruct(fields[0].shape, fields[0].dtype)

    others = [lax.ppermute(field, "shot", beside) for field in fields]
    picks = []
    for k, (field, other) in enumerate(zip(fields, others)):
        out = [like] + [jax.ShapeDtypeStruct((1,), jnp.int32)] * (k == 0)
        picks.append(call(functools.partial(pick_kernel, n_gx), f"pick_{k}", [ids, anchors], [field, *in_vmem(other)], out, smem_out=k == 0))
    index = picks[0][1][0]
    sends = [pick[0] for pick in picks]

    def turned(k, crossed):
        (block,) = call(
            functools.partial(join_kernel, n_gx), f"join_{k}", [ids, anchors], [fields[k], others[k], crossed], [like]
        )
        return lax.switch(index, branches, block)

    crossed = [lax.ppermute(sends[0], "shot", across)]
    sends[1], sends[2], crossed[0], rims = lax.optimization_barrier((sends[1], sends[2], crossed[0], rims))
    work = beside_work(rims)
    crossed[0], work = lax.optimization_barrier((crossed[0], work))
    crossed.append(lax.ppermute(sends[1], "shot", across))
    windows = [turned(0, crossed[0])]
    sends[2], crossed[1], windows[0] = lax.optimization_barrier((sends[2], crossed[1], windows[0]))
    crossed.append(lax.ppermute(sends[2], "shot", across))
    windows.append(turned(1, crossed[1]))
    crossed[2], windows[1] = lax.optimization_barrier((crossed[2], windows[1]))
    windows.append(turned(2, crossed[2]))
    return windows, work


def swaps(count):
    near = [(i, i ^ 1) for i in range(count) if i ^ 1 < count]
    off = [(i, i + 1) for i in range(1, count - 1, 2)]
    return near, off + [(b, a) for a, b in off]


def exchange(rims):
    got = []
    for rim, axis, which in zip(rims, ("gx", "gx", "gy", "gy"), (0, 1, 0, 1)):
        pairs = swaps(lax.axis_size(axis))[which]
        got.append(lax.ppermute(rim, axis, pairs) if pairs else jnp.zeros_like(rim))
    return got


def depth_matrix(nz):
    out = np.zeros((nz, nz), np.float32)
    for k, weight in enumerate(OUTER, 1):
        out += weight * (np.eye(nz, k=k, dtype=np.float32) + np.eye(nz, k=-k, dtype=np.float32))
    return out


def plane_matrix(ny):
    out = np.zeros((XT, ny, XT + 2 * REACH, ny), np.float32)
    column = depth_matrix(ny)
    for x in range(XT):
        out[x, :, x + REACH, :] = column
        for k, weight in enumerate(OUTER, 1):
            for at in (x + REACH - k, x + REACH + k):
                out[x, np.arange(ny), at, np.arange(ny)] += weight
    return out.reshape(XT * ny, (XT + 2 * REACH) * ny)


def side_matrix(nx):
    out = np.zeros((nx, 16, 2, nx, REACH), np.float32)
    for y in range(REACH):
        for k, weight in enumerate(OUTER, 1):
            if y - k < 0:
                out[np.arange(nx), y, 0, np.arange(nx), y - k + REACH] = weight
                out[np.arange(nx), 15 - y, 1, np.arange(nx), k - y - 1] = weight
    return out.reshape(nx * 16, 2 * nx * REACH)


def split(values):
    high = values.astype(jnp.bfloat16)
    return high, (values - high.astype(jnp.float32)).astype(jnp.bfloat16)


def dot(a, b):
    return jnp.dot(a, b, preferred_element_type=jnp.float32)


def neighbours(p_ref, q_ref, dh_ref, dz_ref, high_ref, low_ref, use):
    nx, ny, nz = p_ref.shape
    flat = (XT * ny, nz)
    for ref in (high_ref, low_ref):
        ref[0:REACH] = jnp.zeros((REACH, ny, nz), jnp.bfloat16)
        ref[nx + REACH :] = jnp.zeros((REACH, ny, nz), jnp.bfloat16)

    def cut(i, _):
        x = i * XT
        high, low = split(p_ref[pl.ds(x, XT)])
        high_ref[pl.ds(x + REACH, XT)] = high
        low_ref[pl.ds(x + REACH, XT)] = low
        return _

    lax.fori_loop(0, nx // XT, cut, None)

    def tile(i, _):
        x = i * XT
        rows = pl.ds(x, XT)
        p, q = p_ref[rows].reshape(flat), q_ref[rows].reshape(flat)
        window = pl.ds(x, XT + 2 * REACH)
        deep = ((XT + 2 * REACH) * ny, nz)
        across = dot(dh_ref[...], high_ref[window].reshape(deep))
        across += dot(dh_ref[...], low_ref[window].reshape(deep))
        high, low = split(q)
        down = dot(high, dz_ref[...]) + dot(low, dz_ref[...])
        use(i, rows, p, q, across + (2 * CENTER) * p, down + CENTER * q)
        return _

    lax.fori_loop(0, nx // XT, tile, None)


def rim_terms(ids_ref, xa_ref, xb_ref, ya_ref, yb_ref, ds_ref, shape):
    nx, ny, nz = shape
    x_odd, y_odd = ids_ref[1] % 2 == 1, ids_ref[2] % 2 == 1
    xa, xb = xa_ref[...].reshape(REACH, ny, nz), xb_ref[...].reshape(REACH, ny, nz)
    below, above = jnp.where(x_odd, xa, xb), jnp.where(x_odd, xb, xa)
    near, far = [], []
    for i in range(REACH):
        near.append(sum(OUTER[i + REACH - h - 1] * below[h] for h in range(i, REACH)))
        far.append(sum(OUTER[REACH + h - i - 1] * above[h] for h in range(0, i + 1)))
    ya, yb = ya_ref[...], yb_ref[...]
    sides = jnp.concatenate([jnp.where(y_odd, ya, yb), jnp.where(y_odd, yb, ya)], 0)
    high, low = split(sides)
    side = dot(ds_ref[...], high) + dot(ds_ref[...], low)
    return jnp.stack(near), jnp.stack(far), side.reshape(nx, 16, nz)


def add_source(ids_ref, sources_ref, wave_ref, step, p_ref):
    nx, ny, nz = p_ref.shape
    lx, ly, lz = sources_ref[0, 0] - ids_ref[1] * nx, sources_ref[0, 1] - ids_ref[2] * ny, sources_ref[0, 2]

    @pl.when((lx >= 0) & (lx < nx) & (ly >= 0) & (ly < ny))
    def _():
        y_tile = pl.ds(pl.multiple_of((ly >> 3) * 8, 8), 8)
        at_y = lax.broadcasted_iota(jnp.int32, (1, 8, nz), 1) == (ly & 7)
        at_z = lax.broadcasted_iota(jnp.int32, (1, 8, nz), 2) == lz
        old = p_ref[pl.ds(lx, 1), y_tile, :]
        p_ref[pl.ds(lx, 1), y_tile, :] = old + jnp.where(at_y & at_z, wave_ref[0, step], 0.0)


def put_rims(ids_ref, p_ref, sxa_ref, sxb_ref, sya_ref, syb_ref):
    nx, ny, nz = p_ref.shape
    x_odd, y_odd = ids_ref[1] % 2, ids_ref[2] % 2
    sxa_ref[...] = p_ref[pl.ds((1 - x_odd) * (nx - REACH), REACH)].reshape(REACH * ny, nz)
    sxb_ref[...] = p_ref[pl.ds(x_odd * (nx - REACH), REACH)].reshape(REACH * ny, nz)
    for x in range(0, nx, 2):
        head = jnp.concatenate([p_ref[x, 0:REACH], p_ref[x + 1, 0:REACH]], 0)
        tail = jnp.concatenate([p_ref[x, ny - REACH : ny], p_ref[x + 1, ny - REACH : ny]], 0)
        rows = slice(x * REACH, (x + 2) * REACH)
        sya_ref[rows] = jnp.where(y_odd == 1, head, tail)
        syb_ref[rows] = jnp.where(y_odd == 1, tail, head)


def edge_kernel(ids_ref, p_ref, *rim_refs):
    put_rims(ids_ref, p_ref, *rim_refs)


def open_kernel(ids_ref, p_ref, q_ref, xa_ref, xb_ref, ya_ref, yb_ref, dh_ref, dz_ref, ds_ref, pb_hbm, qb_hbm,
                h_hbm, z_hbm, up_hbm, uq_hbm,
                high_ref, low_ref, pb_ref, qb_ref, side_ref, h_ref, z_ref, up_ref, uq_ref, in_sem, out_sem):
    nx, ny, nz = p_ref.shape
    loads = [pltpu.make_async_copy(pb_hbm, pb_ref, in_sem.at[0]), pltpu.make_async_copy(qb_hbm, qb_ref, in_sem.at[1])]
    for load in loads:
        load.start()
    near, far, side = rim_terms(ids_ref, xa_ref, xb_ref, ya_ref, yb_ref, ds_ref, p_ref.shape)
    side_ref[...] = side
    for load in loads:
        load.wait()
    pairs = ((h_ref, h_hbm), (z_ref, z_hbm), (up_ref, up_hbm), (uq_ref, uq_hbm))

    def stores(i, rows):
        return [pltpu.make_async_copy(a.at[rows], b.at[rows], out_sem.at[k, i]) for k, (a, b) in enumerate(pairs)]

    def use(i, rows, p, q, across, down):
        h_ref[rows] = across.reshape(XT, ny, nz)
        z_ref[rows] = down.reshape(XT, ny, nz)
        up_ref[rows] = 2.0 * p_ref[rows] - pb_ref[rows]
        uq_ref[rows] = 2.0 * q_ref[rows] - qb_ref[rows]

        @pl.when(i == 0)
        def _():
            h_ref[0:REACH] += near

        @pl.when(i == nx // XT - 1)
        def _():
            h_ref[nx - REACH : nx] += far

        h_ref[rows, 0:8] += side_ref[rows, 0:8]
        h_ref[rows, ny - 8 : ny] += side_ref[rows, 8:16]
        for store in stores(i, rows):
            store.start()

    neighbours(p_ref, q_ref, dh_ref, dz_ref, high_ref, low_ref, use)

    def finish(i, _):
        for store in stores(i, pl.ds(i * XT, XT)):
            store.wait()
        return _

    lax.fori_loop(0, nx // XT, finish, None)


def first_kernel(ids_ref, anchors_ref, sources_ref, wave_ref, *refs):
    sources = refs[:7]
    p_ref, q_ref, a_ref, b_ref, c_ref = refs[7:12]
    rim_refs, held, sem = refs[12:16], refs[16:23], refs[23]
    h_ref, z_ref, up_ref, uq_ref, v_ref, e_ref, d_ref = held
    nx, ny, nz = p_ref.shape
    f32 = jnp.float32
    rest = lax.rem(anchors_ref[ids_ref[0]], nx)
    first = jnp.where(rest > 0, lax.rem(rest - 1, BUCKET), 0)

    def loads(i):
        out = []
        for k, (src, dst) in enumerate(zip(sources, held)):
            start = i * XT + (first if k >= 4 else 0)
            out.append(pltpu.make_async_copy(src.at[pl.ds(start, XT)], dst.at[pl.ds(i * XT, XT)], sem.at[k, i]))
        return out

    for i in range(nx // XT):
        for load in loads(i):
            load.start()

    def tile(i, _):
        for load in loads(i):
            load.wait()

        def update(j, _):
            rows = pl.ds(i * XT + 2 * j, 2)
            vel = v_ref[rows].astype(f32)
            c = vel * vel * f32(1.0 / SCALE)
            a = c * (1.0 + 2.0 * e_ref[rows].astype(f32))
            b = c * jnp.sqrt(1.0 + 2.0 * d_ref[rows].astype(f32))
            a_ref[rows], b_ref[rows], c_ref[rows] = a, b, c
            h, z = h_ref[rows], z_ref[rows]
            p_ref[rows] = up_ref[rows] + (a * h + b * z)
            q_ref[rows] = uq_ref[rows] + (b * h + c * z)
            return _

        return lax.fori_loop(0, XT // 2, update, _)

    lax.fori_loop(0, nx // XT, tile, None)
    add_source(ids_ref, sources_ref, wave_ref, 0, p_ref)
    put_rims(ids_ref, p_ref, *rim_refs)


def inner_kernel(p_ref, pb_ref, q_ref, qb_ref, a_ref, b_ref, c_ref, dh_ref, dz_ref, po_ref, qo_ref, high_ref, low_ref):
    nx, ny, nz = p_ref.shape
    flat, block = (XT * ny, nz), (XT, ny, nz)

    def use(i, rows, p, q, across, down):
        a, b, c = (ref[rows].reshape(flat) for ref in (a_ref, b_ref, c_ref))
        po_ref[rows] = (2.0 * p - pb_ref[rows].reshape(flat) + (a * across + b * down)).reshape(block)
        qo_ref[rows] = (2.0 * q - qb_ref[rows].reshape(flat) + (b * across + c * down)).reshape(block)

    neighbours(p_ref, q_ref, dh_ref, dz_ref, high_ref, low_ref, use)


def rim_kernel(step, ids_ref, sources_ref, wave_ref, p_in, q_in, a_ref, b_ref, xa_ref, xb_ref, ya_ref, yb_ref, ds_ref,
               p_ref, q_ref, *out_refs):
    nx, ny, nz = p_ref.shape
    near, far, side = rim_terms(ids_ref, xa_ref, xb_ref, ya_ref, yb_ref, ds_ref, p_ref.shape)
    for rows, term in ((slice(0, REACH), near), (slice(nx - REACH, nx), far)):
        p_ref[rows] = p_in[rows] + a_ref[rows] * term
        q_ref[rows] = q_in[rows] + b_ref[rows] * term
    for cells, term in ((slice(0, 8), side[:, 0:8]), (slice(ny - 8, ny), side[:, 8:16])):
        p_ref[:, cells] += a_ref[:, cells] * term
        q_ref[:, cells] += b_ref[:, cells] * term
    add_source(ids_ref, sources_ref, wave_ref, step, p_ref)
    if len(out_refs) == 4:
        put_rims(ids_ref, p_ref, *out_refs)
    else:
        p_out, q_out, sem = out_refs
        copies = [pltpu.make_async_copy(p_ref, p_out, sem.at[0]), pltpu.make_async_copy(q_ref, q_out, sem.at[1])]
        for copy in copies:
            copy.start()
        for copy in copies:
            copy.wait()


def call(kernel, name, scalars, arrays, out, scratch=(), aliases=None, hbm=(), hbm_out=0, smem_out=0):
    vmem = pl.BlockSpec(memory_space=pltpu.VMEM)
    smem = pl.BlockSpec(memory_space=pltpu.SMEM)
    anywhere = pl.BlockSpec(memory_space=pl.ANY)
    return pl.pallas_call(
        kernel,
        out_shape=out,
        in_specs=[smem] * len(scalars) + [vmem] * len(arrays) + [anywhere] * len(hbm),
        out_specs=[vmem] * (len(out) - hbm_out - smem_out) + [anywhere] * hbm_out + [smem] * smem_out,
        scratch_shapes=scratch,
        input_output_aliases=aliases or {},
        compiler_params=pltpu.CompilerParams(vmem_limit_bytes=VMEM_LIMIT),
        name=name,
    )(*scalars, *arrays, *hbm)


def in_vmem(*arrays):
    return [pltpu.with_memory_space_constraint(a, pltpu.VMEM) for a in arrays]


def in_hbm(*arrays):
    return [pltpu.with_memory_space_constraint(a, pltpu.HBM) for a in arrays]


def on_device(velocity, epsilon, delta, anchors, sources, wavelet, p_now, p_prev, q_now, q_prev):
    p, pb, q, qb = p_now[0], p_prev[0], q_now[0], q_prev[0]
    nx, ny, nz = p.shape
    f32, bf16 = jnp.float32, jnp.bfloat16
    ids = jnp.stack([lax.axis_index(name) for name in ("shot", "gx", "gy")])
    block = pltpu.VMEM((nx, ny, nz), f32)
    stored = pltpu.HBM((nx, ny, nz), f32)
    rim_shapes = [jax.ShapeDtypeStruct((REACH * n, nz), f32) for n in (ny, ny, nx, nx)]
    padded = [pltpu.VMEM((nx + 2 * REACH, ny, nz), bf16)] * 2
    dz = jnp.asarray(depth_matrix(nz), bf16)
    dh = jnp.asarray(plane_matrix(ny), bf16)
    ds = jnp.asarray(side_matrix(nx), bf16)
    tiles = nx // XT
    rims = exchange(call(edge_kernel, "edges", [ids], in_vmem(p), rim_shapes))

    def beside_work(rims):
        return call(
            open_kernel, "open", [ids], in_vmem(p, q, *rims, dh, dz, ds), [stored] * 4,
            padded + [block] * 2 + [pltpu.VMEM((nx, 16, nz), f32)] + [block] * 4
            + [pltpu.SemaphoreType.DMA((2,)), pltpu.SemaphoreType.DMA((4, tiles))],
            hbm=in_hbm(pb, qb), hbm_out=4,
        )

    windows, opened = model_windows(ids, anchors, (velocity, epsilon, delta), rims, beside_work)
    pb, qb = p, q
    p, q, a, b, c, *rims = call(
        first_kernel, "first", [ids, anchors, sources, wavelet], [], [block] * 5 + rim_shapes,
        [block] * 4 + [pltpu.VMEM((nx, ny, nz), bf16)] * 3 + [pltpu.SemaphoreType.DMA((7, tiles))],
        hbm=in_hbm(*opened) + windows,
    )
    for step in range(1, STEPS):
        rims = exchange(rims)
        p_new, q_new = call(
            inner_kernel, f"inner_{step}", [], in_vmem(p, pb, q, qb, a, b, c, dh, dz), [block] * 2, padded
        )
        last = step == STEPS - 1
        whole = jax.ShapeDtypeStruct((nx, ny, nz), f32)
        out = call(
            functools.partial(rim_kernel, step), f"rims_{step}", [ids, sources, wavelet],
            in_vmem(p_new, q_new, a, b, *rims, ds),
            [block] * 2 + ([whole] * 2 if last else rim_shapes),
            [pltpu.SemaphoreType.DMA((2,))] if last else [],
            {3: 0, 4: 1},
            hbm_out=2 if last else 0,
        )
        pb, qb = p, q
        p, q, *rims = out
    return rims[0][None], rims[1][None]


def solution(mesh):
    model = P(("shot", "gx"), "gy", None)
    field = P("shot", "gx", "gy", None)
    return jax.shard_map(
        on_device,
        mesh=mesh,
        in_specs=(model, model, model, P(), P("shot", None), P("shot", None)) + (field,) * 4,
        out_specs=(field, field),
        check_vma=False,
    )
```

```python
import functools

import jax
import jax.numpy as jnp
import numpy as np
from jax import lax
from jax.experimental import pallas as pl
from jax.experimental.pallas import tpu as pltpu
from jax.sharding import PartitionSpec as P

STEPS = 4
REACH = 4
SCALE = 5040.0
CENTER = -14350.0
OUTER = (8064.0, -1008.0, 128.0, -9.0)
BUCKET = 4
XT = 8
VMEM_LIMIT = 16 * 1024 * 1024


def row_group(anchor, gx, n_gx, rows):
    period = n_gx * rows
    group = lax.div(anchor, period)
    cut = lax.rem(anchor, period) - gx * rows
    return lambda i: jnp.where(i < cut, group + 1, group)


def pick_kernel(n_gx, ids_ref, anchors_ref, field_ref, other_ref, send_ref, here_ref):
    rows = field_ref.shape[0]
    shot, gx = ids_ref[0], ids_ref[1]
    core = shot & 1
    far = row_group(anchors_ref[shot ^ 2], gx, n_gx, rows)
    own = row_group(anchors_ref[shot], gx, n_gx, rows)
    for i in range(rows):
        field, other = field_ref[i], other_ref[i]
        send_ref[i] = jnp.where(far(i) & 1 == core, field, other)
        here_ref[i] = jnp.where(own(i) & 1 == core, field, other)


def join_kernel(n_gx, ids_ref, anchors_ref, *refs):
    *blocks, out_ref = refs
    rows = out_ref.shape[0]
    shot, gx = ids_ref[0], ids_ref[1]
    core, half = shot & 1, shot >> 1
    own = row_group(anchors_ref[shot], gx, n_gx, rows)
    for i in range(rows):
        here, across = blocks[0][i], blocks[1][i]
        if len(blocks) == 4:
            mine = own(i) & 1 == core
            here, across = jnp.where(mine, here, blocks[2][i]), jnp.where(mine, across, blocks[3][i])
        out_ref[i] = jnp.where(own(i) >> 1 == half, here, across)


def index_kernel(n_gx, rows, ids_ref, anchors_ref, index_ref):
    anchor = anchors_ref[ids_ref[0]]
    turn = lax.rem(lax.div(anchor, rows), n_gx)
    rest = lax.rem(anchor, rows)
    bucket = jnp.where(rest > 0, lax.div(rest - 1, BUCKET) + 1, 0)
    index_ref[0] = turn * (rows // BUCKET + 1) + bucket


def rotation_branches(n_gx, rows):
    def perm(block, by):
        by %= n_gx
        if by == 0:
            return block
        return lax.ppermute(block, "gx", [(i, (i - by) % n_gx) for i in range(n_gx)])

    def branch(turn, bucket):
        def aligned(block):
            moved = perm(block, turn)
            return jnp.concatenate([moved, jnp.zeros_like(moved[: BUCKET - 1])], 0)

        def split(block):
            k = BUCKET * (bucket - 1)
            return jnp.concatenate(
                [perm(block[k + 1 :], turn), perm(block[: k + BUCKET], turn + 1)], 0
            )

        return aligned if bucket == 0 else split

    return [branch(t, b) for t in range(n_gx) for b in range(rows // BUCKET + 1)]


def model_windows(ids, anchors, fields, rims):
    n_gx = lax.axis_size("gx")
    n_shot = lax.axis_size("shot")
    rows = fields[0].shape[0]
    branches = rotation_branches(n_gx, rows)
    beside = [(i, i ^ 1) for i in range(n_shot)]
    across = [(i, i ^ 2) for i in range(n_shot)]
    like = jax.ShapeDtypeStruct(fields[0].shape, fields[0].dtype)

    def turned(k, *blocks):
        (block,) = call(
            functools.partial(join_kernel, n_gx), f"join_{k}", [ids, anchors], in_vmem(*blocks), [like]
        )
        return lax.switch(index, branches, block)

    crossed = [lax.ppermute(fields[0], "shot", across)]
    (index,) = call(
        functools.partial(index_kernel, n_gx, rows), "index", [ids, anchors], [],
        [jax.ShapeDtypeStruct((1,), jnp.int32)], smem_out=1,
    )
    index = index[0]
    others = [lax.ppermute(field, "shot", beside) for field in fields]
    sends, heres = [None], [None]
    for k in (1, 2):
        send, here = call(
            functools.partial(pick_kernel, n_gx), f"pick_{k}", [ids, anchors], in_vmem(fields[k], others[k]), [like] * 2
        )
        sends.append(send)
        heres.append(here)
    sends[1], sends[2], crossed[0], rims = lax.optimization_barrier((sends[1], sends[2], crossed[0], rims))
    crossed.append(lax.ppermute(sends[1], "shot", across))
    far_other = lax.ppermute(crossed[0], "shot", beside)
    windows = [turned(0, fields[0], crossed[0], others[0], far_other)]
    sends[2], crossed[1], windows[0] = lax.optimization_barrier((sends[2], crossed[1], windows[0]))
    crossed.append(lax.ppermute(sends[2], "shot", across))
    windows.append(turned(1, heres[1], crossed[1]))
    crossed[2], windows[1] = lax.optimization_barrier((crossed[2], windows[1]))
    windows.append(turned(2, heres[2], crossed[2]))
    return windows, rims


def swaps(count):
    near = [(i, i ^ 1) for i in range(count) if i ^ 1 < count]
    off = [(i, i + 1) for i in range(1, count - 1, 2)]
    return near, off + [(b, a) for a, b in off]


def exchange(rims):
    got = []
    for rim, axis, which in zip(rims, ("gx", "gx", "gy", "gy"), (0, 1, 0, 1)):
        pairs = swaps(lax.axis_size(axis))[which]
        got.append(lax.ppermute(rim, axis, pairs) if pairs else jnp.zeros_like(rim))
    return got


def depth_matrix(nz):
    out = np.zeros((nz, nz), np.float32)
    for k, weight in enumerate(OUTER, 1):
        out += weight * (np.eye(nz, k=k, dtype=np.float32) + np.eye(nz, k=-k, dtype=np.float32))
    return out


def plane_matrix(ny):
    out = np.zeros((XT, ny, XT + 2 * REACH, ny), np.float32)
    column = depth_matrix(ny)
    for x in range(XT):
        out[x, :, x + REACH, :] = column
        for k, weight in enumerate(OUTER, 1):
            for at in (x + REACH - k, x + REACH + k):
                out[x, np.arange(ny), at, np.arange(ny)] += weight
    return out.reshape(XT * ny, (XT + 2 * REACH) * ny)


def side_matrix(nx):
    out = np.zeros((nx, 16, 2, nx, REACH), np.float32)
    for y in range(REACH):
        for k, weight in enumerate(OUTER, 1):
            if y - k < 0:
                out[np.arange(nx), y, 0, np.arange(nx), y - k + REACH] = weight
                out[np.arange(nx), 15 - y, 1, np.arange(nx), k - y - 1] = weight
    return out.reshape(nx * 16, 2 * nx * REACH)


def split(values):
    high = values.astype(jnp.bfloat16)
    return high, (values - high.astype(jnp.float32)).astype(jnp.bfloat16)


def dot(a, b):
    return jnp.dot(a, b, preferred_element_type=jnp.float32)


def neighbours(p_ref, q_ref, dh_ref, dz_ref, high_ref, low_ref, use):
    nx, ny, nz = p_ref.shape
    flat = (XT * ny, nz)
    for ref in (high_ref, low_ref):
        ref[0:REACH] = jnp.zeros((REACH, ny, nz), jnp.bfloat16)
        ref[nx + REACH :] = jnp.zeros((REACH, ny, nz), jnp.bfloat16)

    def cut(i, _):
        x = i * XT
        high, low = split(p_ref[pl.ds(x, XT)])
        high_ref[pl.ds(x + REACH, XT)] = high
        low_ref[pl.ds(x + REACH, XT)] = low
        return _

    lax.fori_loop(0, nx // XT, cut, None)

    def tile(i, _):
        x = i * XT
        rows = pl.ds(x, XT)
        p, q = p_ref[rows].reshape(flat), q_ref[rows].reshape(flat)
        window = pl.ds(x, XT + 2 * REACH)
        deep = ((XT + 2 * REACH) * ny, nz)
        across = dot(dh_ref[...], high_ref[window].reshape(deep))
        across += dot(dh_ref[...], low_ref[window].reshape(deep))
        high, low = split(q)
        down = dot(high, dz_ref[...]) + dot(low, dz_ref[...])
        use(i, rows, p, q, across + (2 * CENTER) * p, down + CENTER * q)
        return _

    lax.fori_loop(0, nx // XT, tile, None)


def rim_terms(ids_ref, xa_ref, xb_ref, ya_ref, yb_ref, ds_ref, shape):
    nx, ny, nz = shape
    x_odd, y_odd = ids_ref[1] % 2 == 1, ids_ref[2] % 2 == 1
    xa, xb = xa_ref[...].reshape(REACH, ny, nz), xb_ref[...].reshape(REACH, ny, nz)
    below, above = jnp.where(x_odd, xa, xb), jnp.where(x_odd, xb, xa)
    near, far = [], []
    for i in range(REACH):
        near.append(sum(OUTER[i + REACH - h - 1] * below[h] for h in range(i, REACH)))
        far.append(sum(OUTER[REACH + h - i - 1] * above[h] for h in range(0, i + 1)))
    ya, yb = ya_ref[...], yb_ref[...]
    sides = jnp.concatenate([jnp.where(y_odd, ya, yb), jnp.where(y_odd, yb, ya)], 0)
    high, low = split(sides)
    side = dot(ds_ref[...], high) + dot(ds_ref[...], low)
    return jnp.stack(near), jnp.stack(far), side.reshape(nx, 16, nz)


def add_source(ids_ref, sources_ref, wave_ref, step, p_ref):
    nx, ny, nz = p_ref.shape
    lx, ly, lz = sources_ref[0, 0] - ids_ref[1] * nx, sources_ref[0, 1] - ids_ref[2] * ny, sources_ref[0, 2]

    @pl.when((lx >= 0) & (lx < nx) & (ly >= 0) & (ly < ny))
    def _():
        y_tile = pl.ds(pl.multiple_of((ly >> 3) * 8, 8), 8)
        at_y = lax.broadcasted_iota(jnp.int32, (1, 8, nz), 1) == (ly & 7)
        at_z = lax.broadcasted_iota(jnp.int32, (1, 8, nz), 2) == lz
        old = p_ref[pl.ds(lx, 1), y_tile, :]
        p_ref[pl.ds(lx, 1), y_tile, :] = old + jnp.where(at_y & at_z, wave_ref[0, step], 0.0)


def put_rims(ids_ref, p_ref, sxa_ref, sxb_ref, sya_ref, syb_ref):
    nx, ny, nz = p_ref.shape
    x_odd, y_odd = ids_ref[1] % 2, ids_ref[2] % 2
    sxa_ref[...] = p_ref[pl.ds((1 - x_odd) * (nx - REACH), REACH)].reshape(REACH * ny, nz)
    sxb_ref[...] = p_ref[pl.ds(x_odd * (nx - REACH), REACH)].reshape(REACH * ny, nz)
    for x in range(0, nx, 2):
        head = jnp.concatenate([p_ref[x, 0:REACH], p_ref[x + 1, 0:REACH]], 0)
        tail = jnp.concatenate([p_ref[x, ny - REACH : ny], p_ref[x + 1, ny - REACH : ny]], 0)
        rows = slice(x * REACH, (x + 2) * REACH)
        sya_ref[rows] = jnp.where(y_odd == 1, head, tail)
        syb_ref[rows] = jnp.where(y_odd == 1, tail, head)


def edge_kernel(ids_ref, p_ref, q_ref, *rim_refs):
    put_rims(ids_ref, p_ref, *rim_refs)


def add_rims(terms, p_in, q_in, a_ref, b_ref, p_ref, q_ref):
    near, far, side = terms
    nx, ny, nz = p_ref.shape
    for rows, term in ((slice(0, REACH), near), (slice(nx - REACH, nx), far)):
        p_ref[rows] = p_in[rows] + a_ref[rows] * term
        q_ref[rows] = q_in[rows] + b_ref[rows] * term
    for cells, term in ((slice(0, 8), side[:, 0:8]), (slice(ny - 8, ny), side[:, 8:16])):
        p_ref[:, cells] += a_ref[:, cells] * term
        q_ref[:, cells] += b_ref[:, cells] * term


def first_kernel(ids_ref, anchors_ref, sources_ref, wave_ref, p0_ref, q0_ref, xa_ref, xb_ref, ya_ref, yb_ref,
                 dh_ref, dz_ref, ds_ref, v_ref, e_ref, d_ref, pb_hbm, qb_hbm,
                 p_ref, q_ref, a_ref, b_ref, c_ref, sxa_ref, sxb_ref, sya_ref, syb_ref,
                 high_ref, low_ref, pb_ref, qb_ref, sem):
    nx, ny, nz = p_ref.shape
    f32 = jnp.float32
    loads = [pltpu.make_async_copy(pb_hbm, pb_ref, sem.at[0]), pltpu.make_async_copy(qb_hbm, qb_ref, sem.at[1])]
    for load in loads:
        load.start()
    rest = lax.rem(anchors_ref[ids_ref[0]], nx)
    first = jnp.where(rest > 0, lax.rem(rest - 1, BUCKET), 0)
    half = XT // 2

    def products(i, _):
        rows, model = pl.ds(i * half, half), pl.ds(first + i * half, half)
        vel = v_ref[model].astype(f32)
        c = vel * vel * f32(1.0 / SCALE)
        a_ref[rows] = c * (1.0 + 2.0 * e_ref[model].astype(f32))
        b_ref[rows] = c * jnp.sqrt(1.0 + 2.0 * d_ref[model].astype(f32))
        c_ref[rows] = c
        return _

    lax.fori_loop(0, nx // half, products, None)
    for load in loads:
        load.wait()

    def use(i, rows, p, q, across, down):
        update(rows, p, q, across, down, pb_ref, qb_ref, a_ref, b_ref, c_ref, p_ref, q_ref)

    neighbours(p0_ref, q0_ref, dh_ref, dz_ref, high_ref, low_ref, use)
    terms = rim_terms(ids_ref, xa_ref, xb_ref, ya_ref, yb_ref, ds_ref, p_ref.shape)
    add_rims(terms, p_ref, q_ref, a_ref, b_ref, p_ref, q_ref)
    add_source(ids_ref, sources_ref, wave_ref, 0, p_ref)
    put_rims(ids_ref, p_ref, sxa_ref, sxb_ref, sya_ref, syb_ref)


def update(rows, p, q, across, down, pb_ref, qb_ref, a_ref, b_ref, c_ref, po_ref, qo_ref):
    flat = p.shape
    a, b, c, pb, qb = (ref[rows].reshape(flat) for ref in (a_ref, b_ref, c_ref, pb_ref, qb_ref))
    block = (XT,) + po_ref.shape[1:]
    po_ref[rows] = (2.0 * p - pb + (a * across + b * down)).reshape(block)
    qo_ref[rows] = (2.0 * q - qb + (b * across + c * down)).reshape(block)


def inner_kernel(p_ref, pb_ref, q_ref, qb_ref, a_ref, b_ref, c_ref, dh_ref, dz_ref, po_ref, qo_ref, high_ref, low_ref):
    def use(i, rows, p, q, across, down):
        update(rows, p, q, across, down, pb_ref, qb_ref, a_ref, b_ref, c_ref, po_ref, qo_ref)

    neighbours(p_ref, q_ref, dh_ref, dz_ref, high_ref, low_ref, use)


def rim_kernel(step, ids_ref, sources_ref, wave_ref, p_in, q_in, a_ref, b_ref, xa_ref, xb_ref, ya_ref, yb_ref, ds_ref,
               p_ref, q_ref, *out_refs):
    terms = rim_terms(ids_ref, xa_ref, xb_ref, ya_ref, yb_ref, ds_ref, p_ref.shape)
    add_rims(terms, p_in, q_in, a_ref, b_ref, p_ref, q_ref)
    add_source(ids_ref, sources_ref, wave_ref, step, p_ref)
    if len(out_refs) == 4:
        put_rims(ids_ref, p_ref, *out_refs)
    else:
        p_out, q_out, sem = out_refs
        copies = [pltpu.make_async_copy(p_ref, p_out, sem.at[0]), pltpu.make_async_copy(q_ref, q_out, sem.at[1])]
        for copy in copies:
            copy.start()
        for copy in copies:
            copy.wait()


def call(kernel, name, scalars, arrays, out, scratch=(), aliases=None, hbm=(), hbm_out=0, smem_out=0):
    vmem = pl.BlockSpec(memory_space=pltpu.VMEM)
    smem = pl.BlockSpec(memory_space=pltpu.SMEM)
    anywhere = pl.BlockSpec(memory_space=pl.ANY)
    return pl.pallas_call(
        kernel,
        out_shape=out,
        in_specs=[smem] * len(scalars) + [vmem] * len(arrays) + [anywhere] * len(hbm),
        out_specs=[vmem] * (len(out) - hbm_out - smem_out) + [anywhere] * hbm_out + [smem] * smem_out,
        scratch_shapes=scratch,
        input_output_aliases=aliases or {},
        compiler_params=pltpu.CompilerParams(vmem_limit_bytes=VMEM_LIMIT),
        name=name,
    )(*scalars, *arrays, *hbm)


def in_vmem(*arrays):
    return [pltpu.with_memory_space_constraint(a, pltpu.VMEM) for a in arrays]


def in_hbm(*arrays):
    return [pltpu.with_memory_space_constraint(a, pltpu.HBM) for a in arrays]


def on_device(velocity, epsilon, delta, anchors, sources, wavelet, p_now, p_prev, q_now, q_prev):
    p, pb, q, qb = p_now[0], p_prev[0], q_now[0], q_prev[0]
    nx, ny, nz = p.shape
    f32, bf16 = jnp.float32, jnp.bfloat16
    ids = jnp.stack([lax.axis_index(name) for name in ("shot", "gx", "gy")])
    block = pltpu.VMEM((nx, ny, nz), f32)
    rim_shapes = [jax.ShapeDtypeStruct((REACH * n, nz), f32) for n in (ny, ny, nx, nx)]
    padded = [pltpu.VMEM((nx + 2 * REACH, ny, nz), bf16)] * 2
    dz = jnp.asarray(depth_matrix(nz), bf16)
    dh = jnp.asarray(plane_matrix(ny), bf16)
    ds = jnp.asarray(side_matrix(nx), bf16)
    rims = exchange(call(edge_kernel, "edges", [ids], in_vmem(p, q), rim_shapes))
    windows, rims = model_windows(ids, anchors, (velocity, epsilon, delta), rims)
    p0, q0 = p, q
    p, q, a, b, c, *rims = call(
        first_kernel, "first", [ids, anchors, sources, wavelet], in_vmem(p0, q0, *rims, dh, dz, ds) + windows,
        [block] * 5 + rim_shapes, padded + [block] * 2 + [pltpu.SemaphoreType.DMA((2,))], hbm=in_hbm(pb, qb),
    )
    pb, qb = p0, q0
    for step in range(1, STEPS):
        rims = exchange(rims)
        p_new, q_new = call(
            inner_kernel, f"inner_{step}", [], in_vmem(p, pb, q, qb, a, b, c, dh, dz), [block] * 2, padded
        )
        last = step == STEPS - 1
        whole = jax.ShapeDtypeStruct((nx, ny, nz), f32)
        out = call(
            functools.partial(rim_kernel, step), f"rims_{step}", [ids, sources, wavelet],
            in_vmem(p_new, q_new, a, b, *rims, ds),
            [block] * 2 + ([whole] * 2 if last else rim_shapes),
            [pltpu.SemaphoreType.DMA((2,))] if last else [],
            {3: 0, 4: 1},
            hbm_out=2 if last else 0,
        )
        pb, qb = p, q
        p, q, *rims = out
    return rims[0][None], rims[1][None]


def solution(mesh):
    model = P(("shot", "gx"), "gy", None)
    field = P("shot", "gx", "gy", None)
    return jax.shard_map(
        on_device,
        mesh=mesh,
        in_specs=(model, model, model, P(), P("shot", None), P("shot", None)) + (field,) * 4,
        out_specs=(field, field),
        check_vma=False,
    )
```

```python
import functools

import jax
import jax.numpy as jnp
import numpy as np
from jax import lax
from jax.experimental import pallas as pl
from jax.experimental.pallas import tpu as pltpu
from jax.sharding import PartitionSpec as P

STEPS = 4
REACH = 4
SCALE = 5040.0
CENTER = -14350.0
OUTER = (8064.0, -1008.0, 128.0, -9.0)
BUCKET = 4
XT = 8
VMEM_LIMIT = 16 * 1024 * 1024


def row_group(anchor, gx, n_gx, rows):
    period = n_gx * rows
    group = lax.div(anchor, period)
    cut = lax.rem(anchor, period) - gx * rows
    return lambda i: jnp.where(i < cut, group + 1, group)


def pick_kernel(n_gx, ids_ref, anchors_ref, field_ref, other_ref, send_ref, here_ref):
    rows = field_ref.shape[0]
    shot, gx = ids_ref[0], ids_ref[1]
    core = shot & 1
    far = row_group(anchors_ref[shot ^ 2], gx, n_gx, rows)
    own = row_group(anchors_ref[shot], gx, n_gx, rows)
    for i in range(rows):
        field, other = field_ref[i], other_ref[i]
        send_ref[i] = jnp.where(far(i) & 1 == core, field, other)
        here_ref[i] = jnp.where(own(i) & 1 == core, field, other)


def join_kernel(n_gx, ids_ref, anchors_ref, *refs):
    *blocks, out_ref = refs
    rows = out_ref.shape[0]
    shot, gx = ids_ref[0], ids_ref[1]
    core, half = shot & 1, shot >> 1
    own = row_group(anchors_ref[shot], gx, n_gx, rows)
    for i in range(rows):
        here, across = blocks[0][i], blocks[1][i]
        if len(blocks) == 4:
            mine = own(i) & 1 == core
            here, across = jnp.where(mine, here, blocks[2][i]), jnp.where(mine, across, blocks[3][i])
        out_ref[i] = jnp.where(own(i) >> 1 == half, here, across)


def facts_kernel(n_gx, shape, ids_ref, anchors_ref, sources_ref, wavelet_ref, facts_ref, waves_ref, index_ref):
    nx, ny, nz = shape
    gx, gy = ids_ref[1], ids_ref[2]
    anchor = anchors_ref[ids_ref[0]]
    turn = lax.rem(lax.div(anchor, nx), n_gx)
    rest = lax.rem(anchor, nx)
    bucket = jnp.where(rest > 0, lax.div(rest - 1, BUCKET) + 1, 0)
    index_ref[0] = turn * (nx // BUCKET + 1) + bucket
    lx, ly = sources_ref[0, 0] - gx * nx, sources_ref[0, 1] - gy * ny
    cell = jnp.where((lx >= 0) & (lx < nx) & (ly >= 0) & (ly < ny), lx * ny + ly, -1)
    for k, fact in enumerate((gx & 1, gy & 1, cell, sources_ref[0, 2])):
        facts_ref[k : k + 1] = jnp.full((1, nz), fact, jnp.int32)
    for k in range(STEPS):
        waves_ref[k : k + 1] = jnp.full((1, nz), wavelet_ref[0, k], jnp.float32)


def rotation_branches(n_gx, rows):
    def perm(block, by):
        by %= n_gx
        if by == 0:
            return block
        return lax.ppermute(block, "gx", [(i, (i - by) % n_gx) for i in range(n_gx)])

    def branch(turn, bucket):
        def aligned(block):
            moved = perm(block, turn)
            return jnp.concatenate([moved, jnp.zeros_like(moved[: BUCKET - 1])], 0)

        def split(block):
            k = BUCKET * (bucket - 1)
            return jnp.concatenate(
                [perm(block[k + 1 :], turn), perm(block[: k + BUCKET], turn + 1)], 0
            )

        return aligned if bucket == 0 else split

    return [branch(t, b) for t in range(n_gx) for b in range(rows // BUCKET + 1)]


def model_windows(ids, anchors, fields, index, rims):
    n_gx = lax.axis_size("gx")
    n_shot = lax.axis_size("shot")
    branches = rotation_branches(n_gx, fields[0].shape[0])
    beside = [(i, i ^ 1) for i in range(n_shot)]
    across = [(i, i ^ 2) for i in range(n_shot)]
    like = jax.ShapeDtypeStruct(fields[0].shape, fields[0].dtype)

    def turned(k, *blocks):
        (block,) = call(
            functools.partial(join_kernel, n_gx), f"join_{k}", [ids, anchors], in_vmem(*blocks), [like]
        )
        return lax.switch(index, branches, block)

    crossed = [lax.ppermute(fields[0], "shot", across)]
    others = [lax.ppermute(field, "shot", beside) for field in fields]
    sends, heres = [None], [None]
    for k in (1, 2):
        send, here = call(
            functools.partial(pick_kernel, n_gx), f"pick_{k}", [ids, anchors], in_vmem(fields[k], others[k]), [like] * 2
        )
        sends.append(send)
        heres.append(here)
    sends[1], sends[2], crossed[0], rims, index = lax.optimization_barrier((sends[1], sends[2], crossed[0], rims, index))
    crossed.append(lax.ppermute(sends[1], "shot", across))
    far_other = lax.ppermute(crossed[0], "shot", beside)
    windows = [turned(0, fields[0], crossed[0], others[0], far_other)]
    sends[2], crossed[1], windows[0] = lax.optimization_barrier((sends[2], crossed[1], windows[0]))
    crossed.append(lax.ppermute(sends[2], "shot", across))
    windows.append(turned(1, heres[1], crossed[1]))
    crossed[2], windows[1] = lax.optimization_barrier((crossed[2], windows[1]))
    windows.append(turned(2, heres[2], crossed[2]))
    return windows, rims


def swaps(count):
    near = [(i, i ^ 1) for i in range(count)]
    off = [(i, i + 1) for i in range(1, count - 1, 2)]
    return [near] + [off + [(b, a) for a, b in off]] * bool(off)


def exchange(rims):
    sets = [("gx", pairs) for pairs in swaps(lax.axis_size("gx"))] + [("gy", pairs) for pairs in swaps(lax.axis_size("gy"))]
    return [lax.ppermute(rim, axis, pairs) for rim, (axis, pairs) in zip(rims, sets, strict=True)]


def depth_matrix(nz):
    out = np.zeros((nz, nz), np.float32)
    for k, weight in enumerate(OUTER, 1):
        out += weight * (np.eye(nz, k=k, dtype=np.float32) + np.eye(nz, k=-k, dtype=np.float32))
    return out


def plane_matrix(ny):
    out = np.zeros((XT, ny, XT + 2 * REACH, ny), np.float32)
    column = depth_matrix(ny)
    for x in range(XT):
        out[x, :, x + REACH, :] = column
        for k, weight in enumerate(OUTER, 1):
            for at in (x + REACH - k, x + REACH + k):
                out[x, np.arange(ny), at, np.arange(ny)] += weight
    return out.reshape(XT * ny, (XT + 2 * REACH) * ny)


def side_matrix(nx):
    out = np.zeros((nx, 16, 2, nx, REACH), np.float32)
    for y in range(REACH):
        for k, weight in enumerate(OUTER, 1):
            if y - k < 0:
                out[np.arange(nx), y, 0, np.arange(nx), y - k + REACH] = weight
                out[np.arange(nx), 15 - y, 1, np.arange(nx), k - y - 1] = weight
    return out.reshape(nx * 16, 2 * nx * REACH)


def split(values):
    high = values.astype(jnp.bfloat16)
    return high, (values - high.astype(jnp.float32)).astype(jnp.bfloat16)


def dot(a, b):
    return jnp.dot(a, b, preferred_element_type=jnp.float32)


def neighbours(p_ref, q_ref, dh_ref, dz_ref, high_ref, low_ref, use):
    nx, ny, nz = p_ref.shape
    flat = (XT * ny, nz)
    for ref in (high_ref, low_ref):
        ref[0:REACH] = jnp.zeros((REACH, ny, nz), jnp.bfloat16)
        ref[nx + REACH :] = jnp.zeros((REACH, ny, nz), jnp.bfloat16)

    def cut(i, _):
        x = i * XT
        high, low = split(p_ref[pl.ds(x, XT)])
        high_ref[pl.ds(x + REACH, XT)] = high
        low_ref[pl.ds(x + REACH, XT)] = low
        return _

    lax.fori_loop(0, nx // XT, cut, None)

    def tile(i, _):
        x = i * XT
        rows = pl.ds(x, XT)
        p, q = p_ref[rows].reshape(flat), q_ref[rows].reshape(flat)
        window = pl.ds(x, XT + 2 * REACH)
        deep = ((XT + 2 * REACH) * ny, nz)
        both = jnp.concatenate([high_ref[window].reshape(deep), low_ref[window].reshape(deep)], 0)
        across = dot(jnp.concatenate([dh_ref[...]] * 2, 1), both)
        down = dot(jnp.concatenate(split(q), 1), jnp.concatenate([dz_ref[...]] * 2, 0))
        use(i, rows, p, q, across + (2 * CENTER) * p, down + CENTER * q)
        return _

    lax.fori_loop(0, nx // XT, tile, None)


def rim_terms(facts_ref, rim_refs, ds_ref, shape):
    nx, ny, nz = shape
    xa_ref, xb_ref, ya_ref, *yb_ref = rim_refs
    x_odd = jnp.broadcast_to(facts_ref[0:1], (ny, nz)) == 1
    y_odd = jnp.broadcast_to(facts_ref[1:2], (nx * REACH, nz)) == 1
    below, above = [], []
    for i in range(REACH):
        xa, xb = xa_ref[i * ny : (i + 1) * ny], xb_ref[i * ny : (i + 1) * ny]
        below.append(jnp.where(x_odd, xa, xb))
        above.append(jnp.where(x_odd, xb, xa))
    near, far = [], []
    for i in range(REACH):
        near.append(sum(OUTER[i + REACH - h - 1] * below[h] for h in range(i, REACH)))
        far.append(sum(OUTER[REACH + h - i - 1] * above[h] for h in range(0, i + 1)))
    ya = ya_ref[...]
    yb = yb_ref[0][...] if yb_ref else jnp.zeros_like(ya)
    sides = jnp.concatenate([jnp.where(y_odd, ya, yb), jnp.where(y_odd, yb, ya)], 0)
    side = dot(jnp.concatenate([ds_ref[...]] * 2, 1), jnp.concatenate(split(sides), 0))
    return jnp.stack(near), jnp.stack(far), side.reshape(nx, 16, nz)


def put_rims(facts_ref, low_ref, high_ref, head_ref, tail_ref, sxa_ref, sxb_ref, sya_ref, *syb_ref):
    _, ny, nz = low_ref.shape
    nx, cells, _ = head_ref.shape
    x_odd = jnp.broadcast_to(facts_ref[0:1], (ny, nz)) == 1
    y_odd = jnp.broadcast_to(facts_ref[1:2], (2 * REACH, nz)) == 1
    for i in range(REACH):
        low, high = low_ref[i], high_ref[i]
        rows = slice(i * ny, (i + 1) * ny)
        sxa_ref[rows] = jnp.where(x_odd, low, high)
        sxb_ref[rows] = jnp.where(x_odd, high, low)
    for x in range(0, nx, 2):
        head = jnp.concatenate([head_ref[x, 0:REACH], head_ref[x + 1, 0:REACH]], 0)
        tail = jnp.concatenate([tail_ref[x, cells - REACH : cells], tail_ref[x + 1, cells - REACH : cells]], 0)
        rows = slice(x * REACH, (x + 2) * REACH)
        sya_ref[rows] = jnp.where(y_odd, head, tail)
        if syb_ref:
            syb_ref[0][rows] = jnp.where(y_odd, tail, head)


def put_rims_of(facts_ref, p_ref, *rim_refs):
    nx, ny, _ = p_ref.shape
    low, high = p_ref.at[0:REACH], p_ref.at[nx - REACH : nx]
    put_rims(facts_ref, low, high, p_ref.at[:, 0:8], p_ref.at[:, ny - 8 : ny], *rim_refs)


def edge_kernel(facts_ref, p_hbm, *refs):
    *rim_refs, low_ref, high_ref, head_ref, tail_ref, sem = refs
    nx, ny, _ = p_hbm.shape
    parts = (p_hbm.at[0:REACH], p_hbm.at[nx - REACH : nx], p_hbm.at[:, 0:8], p_hbm.at[:, ny - 8 : ny])
    held = (low_ref, high_ref, head_ref, tail_ref)
    copies = [pltpu.make_async_copy(src, dst, sem.at[k]) for k, (src, dst) in enumerate(zip(parts, held))]
    for copy in copies:
        copy.start()
    for copy in copies:
        copy.wait()
    put_rims(facts_ref, *held, *rim_refs)


def add_rims(terms, p_in, q_in, a_ref, b_ref, p_ref, q_ref):
    near, far, side = terms
    nx, ny, nz = p_ref.shape
    for rows, term in ((slice(0, REACH), near), (slice(nx - REACH, nx), far)):
        p_ref[rows] = p_in[rows] + a_ref[rows] * term
        q_ref[rows] = q_in[rows] + b_ref[rows] * term
    for cells, term in ((slice(0, 8), side[:, 0:8]), (slice(ny - 8, ny), side[:, 8:16])):
        p_ref[:, cells] += a_ref[:, cells] * term
        q_ref[:, cells] += b_ref[:, cells] * term


def first_kernel(n_rims, ids_ref, anchors_ref, facts_ref, wave_ref, p0_ref, q0_ref, *refs):
    rim_refs, refs = refs[:n_rims], refs[n_rims:]
    dh_ref, dz_ref, ds_ref, v_ref, e_ref, d_ref, pb_hbm, qb_hbm, p_ref, q_ref, a_ref, b_ref, c_ref = refs[:13]
    send_refs, (high_ref, low_ref, pb_ref, qb_ref, sem) = refs[13 : 13 + n_rims], refs[13 + n_rims :]
    nx, ny, nz = p_ref.shape
    f32 = jnp.float32

    def loads(i):
        rows = pl.ds(i * XT, XT)
        pairs = ((pb_hbm, pb_ref), (qb_hbm, qb_ref))
        return [pltpu.make_async_copy(src.at[rows], dst.at[rows], sem.at[k, i]) for k, (src, dst) in enumerate(pairs)]

    for i in range(nx // XT):
        for load in loads(i):
            load.start()
    rest = lax.rem(anchors_ref[ids_ref[0]], nx)
    first = jnp.where(rest > 0, lax.rem(rest - 1, BUCKET), 0)

    def use(i, rows, p, q, across, down):
        model = pl.ds(first + i * XT, XT)
        c = v_ref[model].astype(f32)
        c = c * c * f32(1.0 / SCALE)
        a_ref[rows] = c * (1.0 + 2.0 * e_ref[model].astype(f32))
        b_ref[rows] = c * jnp.sqrt(1.0 + 2.0 * d_ref[model].astype(f32))
        c_ref[rows] = c
        for load in loads(i):
            load.wait()
        update(0, i, rows, p, q, across, down, facts_ref, wave_ref, pb_ref, qb_ref, a_ref, b_ref, c_ref, p_ref, q_ref)

    neighbours(p0_ref, q0_ref, dh_ref, dz_ref, high_ref, low_ref, use)
    terms = rim_terms(facts_ref, rim_refs, ds_ref, p_ref.shape)
    add_rims(terms, p_ref, q_ref, a_ref, b_ref, p_ref, q_ref)
    put_rims_of(facts_ref, p_ref, *send_refs)


def update(step, i, rows, p, q, across, down, facts_ref, wave_ref, pb_ref, qb_ref, a_ref, b_ref, c_ref, po_ref, qo_ref):
    flat = p.shape
    a, b, c, pb, qb = (ref[rows].reshape(flat) for ref in (a_ref, b_ref, c_ref, pb_ref, qb_ref))
    block = (XT,) + po_ref.shape[1:]
    at_row = lax.broadcasted_iota(jnp.int32, flat, 0) == jnp.broadcast_to(facts_ref[2:3] - i * flat[0], flat)
    at_z = lax.broadcasted_iota(jnp.int32, flat, 1) == jnp.broadcast_to(facts_ref[3:4], flat)
    source = jnp.where(at_row & at_z, jnp.broadcast_to(wave_ref[step : step + 1], flat), 0.0)
    po_ref[rows] = (2.0 * p - pb + (a * across + b * down) + source).reshape(block)
    qo_ref[rows] = (2.0 * q - qb + (b * across + c * down)).reshape(block)


def inner_kernel(step, facts_ref, wave_ref, p_ref, pb_ref, q_ref, qb_ref, a_ref, b_ref, c_ref, dh_ref, dz_ref,
                 po_ref, qo_ref, high_ref, low_ref):
    def use(i, rows, p, q, across, down):
        update(step, i, rows, p, q, across, down, facts_ref, wave_ref, pb_ref, qb_ref, a_ref, b_ref, c_ref, po_ref, qo_ref)

    neighbours(p_ref, q_ref, dh_ref, dz_ref, high_ref, low_ref, use)


def rim_kernel(n_rims, last, facts_ref, p_in, q_in, a_ref, b_ref, *refs):
    rim_refs, (ds_ref, p_ref, q_ref, *out_refs) = refs[:n_rims], refs[n_rims:]
    terms = rim_terms(facts_ref, rim_refs, ds_ref, p_ref.shape)
    add_rims(terms, p_in, q_in, a_ref, b_ref, p_ref, q_ref)
    if not last:
        put_rims_of(facts_ref, p_ref, *out_refs)
    else:
        p_out, q_out, sem = out_refs
        copies = [pltpu.make_async_copy(p_ref, p_out, sem.at[0]), pltpu.make_async_copy(q_ref, q_out, sem.at[1])]
        for copy in copies:
            copy.start()
        for copy in copies:
            copy.wait()


def call(kernel, name, scalars, arrays, out, scratch=(), aliases=None, hbm=(), hbm_out=0, smem_out=0):
    vmem = pl.BlockSpec(memory_space=pltpu.VMEM)
    smem = pl.BlockSpec(memory_space=pltpu.SMEM)
    anywhere = pl.BlockSpec(memory_space=pl.ANY)
    return pl.pallas_call(
        kernel,
        out_shape=out,
        in_specs=[smem] * len(scalars) + [vmem] * len(arrays) + [anywhere] * len(hbm),
        out_specs=[vmem] * (len(out) - hbm_out - smem_out) + [anywhere] * hbm_out + [smem] * smem_out,
        scratch_shapes=scratch,
        input_output_aliases=aliases or {},
        compiler_params=pltpu.CompilerParams(vmem_limit_bytes=VMEM_LIMIT),
        name=name,
    )(*scalars, *arrays, *hbm)


def in_vmem(*arrays):
    return [pltpu.with_memory_space_constraint(a, pltpu.VMEM) for a in arrays]


def in_hbm(*arrays):
    return [pltpu.with_memory_space_constraint(a, pltpu.HBM) for a in arrays]


def on_device(velocity, epsilon, delta, anchors, sources, wavelet, p_now, p_prev, q_now, q_prev):
    p, pb, q, qb = p_now[0], p_prev[0], q_now[0], q_prev[0]
    nx, ny, nz = p.shape
    f32, bf16 = jnp.float32, jnp.bfloat16
    ids = jnp.stack([lax.axis_index(name) for name in ("shot", "gx", "gy")])
    block = pltpu.VMEM((nx, ny, nz), f32)
    rim_shapes = [pltpu.VMEM((REACH * n, nz), f32) for axis, n in (("gx", ny), ("gy", nx)) for _ in swaps(lax.axis_size(axis))]
    padded = [pltpu.VMEM((nx + 2 * REACH, ny, nz), bf16)] * 2
    dz = jnp.asarray(depth_matrix(nz), bf16)
    dh = jnp.asarray(plane_matrix(ny), bf16)
    ds = jnp.asarray(side_matrix(nx), bf16)
    facts, waves, index = call(
        functools.partial(facts_kernel, lax.axis_size("gx"), p.shape), "facts", [ids, anchors, sources, wavelet], [],
        [pltpu.VMEM((8, nz), jnp.int32), pltpu.VMEM((STEPS, nz), f32), jax.ShapeDtypeStruct((1,), jnp.int32)],
        smem_out=1,
    )
    edges = call(
        edge_kernel, "edges", [], in_vmem(facts), rim_shapes,
        [pltpu.VMEM((REACH, ny, nz), f32)] * 2 + [pltpu.VMEM((nx, 8, nz), f32)] * 2 + [pltpu.SemaphoreType.DMA((4,))],
        hbm=in_hbm(p),
    )
    rims = exchange(edges)
    windows, rims = model_windows(ids, anchors, (velocity, epsilon, delta), index[0], rims)
    p0, q0 = p, q
    p, q, a, b, c, *rims = call(
        functools.partial(first_kernel, len(rims)), "first", [ids, anchors], in_vmem(facts, waves, p0, q0, *rims, dh, dz, ds) + windows,
        [block] * 5 + rim_shapes, padded + [block] * 2 + [pltpu.SemaphoreType.DMA((2, nx // XT))], hbm=in_hbm(pb, qb),
    )
    pb, qb = p0, q0
    for step in range(1, STEPS):
        rims = exchange(rims)
        p_new, q_new = call(
            functools.partial(inner_kernel, step), f"inner_{step}", [],
            in_vmem(facts, waves, p, pb, q, qb, a, b, c, dh, dz), [block] * 2, padded,
        )
        last = step == STEPS - 1
        whole = jax.ShapeDtypeStruct((nx, ny, nz), f32)
        out = call(
            functools.partial(rim_kernel, len(rims), last), f"rims_{step}", [], in_vmem(facts, p_new, q_new, a, b, *rims, ds),
            [block] * 2 + ([whole] * 2 if last else rim_shapes),
            [pltpu.SemaphoreType.DMA((2,))] if last else [],
            {1: 0, 2: 1},
            hbm_out=2 if last else 0,
        )
        pb, qb = p, q
        p, q, *rims = out
    return rims[0][None], rims[1][None]


def solution(mesh):
    model = P(("shot", "gx"), "gy", None)
    field = P("shot", "gx", "gy", None)
    return jax.shard_map(
        on_device,
        mesh=mesh,
        in_specs=(model, model, model, P(), P("shot", None), P("shot", None)) + (field,) * 4,
        out_specs=(field, field),
        check_vma=False,
    )
```

```python
import functools

import jax
import jax.numpy as jnp
import numpy as np
from jax import lax
from jax.experimental import pallas as pl
from jax.experimental.pallas import tpu as pltpu
from jax.sharding import PartitionSpec as P

STEPS = 4
REACH = 4
SCALE = 5040.0
CENTER = -14350.0
OUTER = (8064.0, -1008.0, 128.0, -9.0)
BUCKET = 4
XT = 8
VMEM_LIMIT = 16 * 1024 * 1024


def row_group(anchor, gx, n_gx, rows):
    period = n_gx * rows
    group = lax.div(anchor, period)
    cut = lax.rem(anchor, period) - gx * rows
    return lambda i: jnp.where(i < cut, group + 1, group)


def pick_kernel(n_gx, ids_ref, anchors_ref, field_ref, other_ref, send_ref, here_ref):
    rows = field_ref.shape[0]
    shot, gx = ids_ref[0], ids_ref[1]
    core = shot & 1
    far = row_group(anchors_ref[shot ^ 2], gx, n_gx, rows)
    own = row_group(anchors_ref[shot], gx, n_gx, rows)
    for i in range(rows):
        field, other = field_ref[i], other_ref[i]
        send_ref[i] = jnp.where(far(i) & 1 == core, field, other)
        here_ref[i] = jnp.where(own(i) & 1 == core, field, other)


def join_kernel(n_gx, whose, ids_ref, anchors_ref, *refs):
    *blocks, out_ref = refs
    rows = out_ref.shape[0]
    shot, gx = ids_ref[0], ids_ref[1]
    core, half = shot & 1, shot >> 1
    own = row_group(anchors_ref[shot ^ whose], gx, n_gx, rows)
    for i in range(rows):
        here, across = blocks[0][i], blocks[1][i]
        if len(blocks) == 4:
            mine = own(i) & 1 == core
            here, across = jnp.where(mine, here, blocks[2][i]), jnp.where(mine, across, blocks[3][i])
        out_ref[i] = jnp.where(own(i) >> 1 == half, here, across)


def facts_kernel(n_gx, shape, ids_ref, anchors_ref, sources_ref, wavelet_ref, facts_ref, waves_ref, *index_refs):
    nx, ny, nz = shape
    gx, gy = ids_ref[1], ids_ref[2]
    for k, index_ref in enumerate(index_refs):
        anchor = anchors_ref[ids_ref[0] ^ (2 * k)]
        turn = lax.rem(lax.div(anchor, nx), n_gx)
        rest = lax.rem(anchor, nx)
        bucket = jnp.where(rest > 0, lax.div(rest - 1, BUCKET) + 1, 0)
        index_ref[0] = turn * (nx // BUCKET + 1) + bucket
    lx, ly = sources_ref[0, 0] - gx * nx, sources_ref[0, 1] - gy * ny
    cell = jnp.where((lx >= 0) & (lx < nx) & (ly >= 0) & (ly < ny), lx * ny + ly, -1)
    for k, fact in enumerate((gx & 1, gy & 1, cell, sources_ref[0, 2])):
        facts_ref[k : k + 1] = jnp.full((1, nz), fact, jnp.int32)
    for k in range(STEPS):
        waves_ref[k : k + 1] = jnp.full((1, nz), wavelet_ref[0, k], jnp.float32)


def rotation_branches(n_gx, rows):
    def perm(block, by):
        by %= n_gx
        if by == 0:
            return block
        return lax.ppermute(block, "gx", [(i, (i - by) % n_gx) for i in range(n_gx)])

    def branch(turn, bucket):
        def aligned(block):
            moved = perm(block, turn)
            return jnp.concatenate([moved, jnp.zeros_like(moved[: BUCKET - 1])], 0)

        def split(block):
            k = BUCKET * (bucket - 1)
            return jnp.concatenate(
                [perm(block[k + 1 :], turn), perm(block[: k + BUCKET], turn + 1)], 0
            )

        return aligned if bucket == 0 else split

    return [branch(t, b) for t in range(n_gx) for b in range(rows // BUCKET + 1)]


def model_windows(ids, anchors, fields, index, rims):
    n_gx = lax.axis_size("gx")
    n_shot = lax.axis_size("shot")
    branches = rotation_branches(n_gx, fields[0].shape[0])
    beside = [(i, i ^ 1) for i in range(n_shot)]
    across = [(i, i ^ 2) for i in range(n_shot)]
    like = jax.ShapeDtypeStruct(fields[0].shape, fields[0].dtype)

    def turned(k, whose, *blocks):
        (block,) = call(
            functools.partial(join_kernel, n_gx, whose), f"join_{k}", [ids, anchors], in_vmem(*blocks), [like]
        )
        return lax.switch(index[whose // 2][0], branches, block)

    crossed = [lax.ppermute(fields[0], "shot", across)]
    others = [lax.ppermute(field, "shot", beside) for field in fields]
    sends, heres = [None], [None]
    for k in (1, 2):
        send, here = call(
            functools.partial(pick_kernel, n_gx), f"pick_{k}", [ids, anchors], in_vmem(fields[k], others[k]), [like] * 2
        )
        sends.append(send)
        heres.append(here)
    sends[1], sends[2], crossed[0], rims, index = lax.optimization_barrier((sends[1], sends[2], crossed[0], rims, index))
    crossed += [lax.ppermute(send, "shot", across) for send in sends[1:]]
    far_other = lax.ppermute(crossed[0], "shot", beside)
    windows = [turned(0, 2, fields[0], crossed[0], others[0], far_other)]
    crossed[1], windows[0] = lax.optimization_barrier((crossed[1], windows[0]))
    windows.append(turned(1, 0, heres[1], crossed[1]))
    crossed[2], windows[0], windows[1] = lax.optimization_barrier((crossed[2], windows[0], windows[1]))
    windows[0] = lax.ppermute(windows[0], "shot", across)
    windows.append(turned(2, 0, heres[2], crossed[2]))
    return windows, rims


def swaps(count):
    near = [(i, i ^ 1) for i in range(count)]
    off = [(i, i + 1) for i in range(1, count - 1, 2)]
    return [near] + [off + [(b, a) for a, b in off]] * bool(off)


def exchange(rims):
    sets = [("gx", pairs) for pairs in swaps(lax.axis_size("gx"))] + [("gy", pairs) for pairs in swaps(lax.axis_size("gy"))]
    return [lax.ppermute(rim, axis, pairs) for rim, (axis, pairs) in zip(rims, sets, strict=True)]


def depth_matrix(nz):
    out = np.zeros((nz, nz), np.float32)
    for k, weight in enumerate(OUTER, 1):
        out += weight * (np.eye(nz, k=k, dtype=np.float32) + np.eye(nz, k=-k, dtype=np.float32))
    return out


def plane_matrix(ny):
    out = np.zeros((XT, ny, XT + 2 * REACH, ny), np.float32)
    column = depth_matrix(ny)
    for x in range(XT):
        out[x, :, x + REACH, :] = column
        for k, weight in enumerate(OUTER, 1):
            for at in (x + REACH - k, x + REACH + k):
                out[x, np.arange(ny), at, np.arange(ny)] += weight
    return out.reshape(XT * ny, (XT + 2 * REACH) * ny)


def side_matrix(nx):
    out = np.zeros((nx, 16, 2, nx, REACH), np.float32)
    for y in range(REACH):
        for k, weight in enumerate(OUTER, 1):
            if y - k < 0:
                out[np.arange(nx), y, 0, np.arange(nx), y - k + REACH] = weight
                out[np.arange(nx), 15 - y, 1, np.arange(nx), k - y - 1] = weight
    return out.reshape(nx * 16, 2 * nx * REACH)


def split(values):
    high = values.astype(jnp.bfloat16)
    return high, (values - high.astype(jnp.float32)).astype(jnp.bfloat16)


def dot(a, b):
    return jnp.dot(a, b, preferred_element_type=jnp.float32)


def neighbours(p_ref, q_ref, dh_ref, dz_ref, high_ref, low_ref, use):
    nx, ny, nz = p_ref.shape
    flat = (XT * ny, nz)
    for ref in (high_ref, low_ref):
        ref[0:REACH] = jnp.zeros((REACH, ny, nz), jnp.bfloat16)
        ref[nx + REACH :] = jnp.zeros((REACH, ny, nz), jnp.bfloat16)

    def cut(i, _):
        x = i * XT
        high, low = split(p_ref[pl.ds(x, XT)])
        high_ref[pl.ds(x + REACH, XT)] = high
        low_ref[pl.ds(x + REACH, XT)] = low
        return _

    lax.fori_loop(0, nx // XT, cut, None)

    def tile(i, _):
        x = i * XT
        rows = pl.ds(x, XT)
        p, q = p_ref[rows].reshape(flat), q_ref[rows].reshape(flat)
        window = pl.ds(x, XT + 2 * REACH)
        deep = ((XT + 2 * REACH) * ny, nz)
        both = jnp.concatenate([high_ref[window].reshape(deep), low_ref[window].reshape(deep)], 0)
        across = dot(jnp.concatenate([dh_ref[...]] * 2, 1), both)
        down = dot(jnp.concatenate(split(q), 1), jnp.concatenate([dz_ref[...]] * 2, 0))
        use(i, rows, p, q, across + (2 * CENTER) * p, down + CENTER * q)
        return _

    lax.fori_loop(0, nx // XT, tile, None)


def rim_terms(facts_ref, rim_refs, ds_ref, shape):
    nx, ny, nz = shape
    xa_ref, xb_ref, ya_ref, *yb_ref = rim_refs
    x_odd = jnp.broadcast_to(facts_ref[0:1], (ny, nz)) == 1
    y_odd = jnp.broadcast_to(facts_ref[1:2], (nx * REACH, nz)) == 1
    below, above = [], []
    for i in range(REACH):
        xa, xb = xa_ref[i * ny : (i + 1) * ny], xb_ref[i * ny : (i + 1) * ny]
        below.append(jnp.where(x_odd, xa, xb))
        above.append(jnp.where(x_odd, xb, xa))
    near, far = [], []
    for i in range(REACH):
        near.append(sum(OUTER[i + REACH - h - 1] * below[h] for h in range(i, REACH)))
        far.append(sum(OUTER[REACH + h - i - 1] * above[h] for h in range(0, i + 1)))
    ya = ya_ref[...]
    yb = yb_ref[0][...] if yb_ref else jnp.zeros_like(ya)
    sides = jnp.concatenate([jnp.where(y_odd, ya, yb), jnp.where(y_odd, yb, ya)], 0)
    side = dot(jnp.concatenate([ds_ref[...]] * 2, 1), jnp.concatenate(split(sides), 0))
    return jnp.stack(near), jnp.stack(far), side.reshape(nx, 16, nz)


def put_rims(facts_ref, low_ref, high_ref, head_ref, tail_ref, sxa_ref, sxb_ref, sya_ref, *syb_ref):
    _, ny, nz = low_ref.shape
    nx, cells, _ = head_ref.shape
    x_odd = jnp.broadcast_to(facts_ref[0:1], (ny, nz)) == 1
    y_odd = jnp.broadcast_to(facts_ref[1:2], (2 * REACH, nz)) == 1
    for i in range(REACH):
        low, high = low_ref[i], high_ref[i]
        rows = slice(i * ny, (i + 1) * ny)
        sxa_ref[rows] = jnp.where(x_odd, low, high)
        sxb_ref[rows] = jnp.where(x_odd, high, low)
    for x in range(0, nx, 2):
        head = jnp.concatenate([head_ref[x, 0:REACH], head_ref[x + 1, 0:REACH]], 0)
        tail = jnp.concatenate([tail_ref[x, cells - REACH : cells], tail_ref[x + 1, cells - REACH : cells]], 0)
        rows = slice(x * REACH, (x + 2) * REACH)
        sya_ref[rows] = jnp.where(y_odd, head, tail)
        if syb_ref:
            syb_ref[0][rows] = jnp.where(y_odd, tail, head)


def put_rims_of(facts_ref, p_ref, *rim_refs):
    nx, ny, _ = p_ref.shape
    low, high = p_ref.at[0:REACH], p_ref.at[nx - REACH : nx]
    put_rims(facts_ref, low, high, p_ref.at[:, 0:8], p_ref.at[:, ny - 8 : ny], *rim_refs)


def edge_kernel(facts_ref, p_hbm, *refs):
    *rim_refs, low_ref, high_ref, head_ref, tail_ref, sem = refs
    nx, ny, _ = p_hbm.shape
    parts = (p_hbm.at[0:REACH], p_hbm.at[nx - REACH : nx], p_hbm.at[:, 0:8], p_hbm.at[:, ny - 8 : ny])
    held = (low_ref, high_ref, head_ref, tail_ref)
    copies = [pltpu.make_async_copy(src, dst, sem.at[k]) for k, (src, dst) in enumerate(zip(parts, held))]
    for copy in copies:
        copy.start()
    for copy in copies:
        copy.wait()
    put_rims(facts_ref, *held, *rim_refs)


def add_rims(terms, p_in, q_in, a_ref, b_ref, p_ref, q_ref):
    near, far, side = terms
    nx, ny, nz = p_ref.shape
    for rows, term in ((slice(0, REACH), near), (slice(nx - REACH, nx), far)):
        p_ref[rows] = p_in[rows] + a_ref[rows] * term
        q_ref[rows] = q_in[rows] + b_ref[rows] * term
    for cells, term in ((slice(0, 8), side[:, 0:8]), (slice(ny - 8, ny), side[:, 8:16])):
        p_ref[:, cells] += a_ref[:, cells] * term
        q_ref[:, cells] += b_ref[:, cells] * term


def first_kernel(n_rims, ids_ref, anchors_ref, facts_ref, wave_ref, p0_ref, q0_ref, *refs):
    rim_refs, refs = refs[:n_rims], refs[n_rims:]
    dh_ref, dz_ref, ds_ref, v_ref, e_ref, d_ref, pb_hbm, qb_hbm, p_ref, q_ref, a_ref, b_ref, c_ref = refs[:13]
    send_refs, (high_ref, low_ref, pb_ref, qb_ref, sem) = refs[13 : 13 + n_rims], refs[13 + n_rims :]
    nx, ny, nz = p_ref.shape
    f32 = jnp.float32

    def loads(i):
        rows = pl.ds(i * XT, XT)
        pairs = ((pb_hbm, pb_ref), (qb_hbm, qb_ref))
        return [pltpu.make_async_copy(src.at[rows], dst.at[rows], sem.at[k, i]) for k, (src, dst) in enumerate(pairs)]

    for i in range(nx // XT):
        for load in loads(i):
            load.start()
    rest = lax.rem(anchors_ref[ids_ref[0]], nx)
    first = jnp.where(rest > 0, lax.rem(rest - 1, BUCKET), 0)

    def use(i, rows, p, q, across, down):
        model = pl.ds(first + i * XT, XT)
        c = v_ref[model].astype(f32)
        c = c * c * f32(1.0 / SCALE)
        a_ref[rows] = c * (1.0 + 2.0 * e_ref[model].astype(f32))
        b_ref[rows] = c * jnp.sqrt(1.0 + 2.0 * d_ref[model].astype(f32))
        c_ref[rows] = c
        for load in loads(i):
            load.wait()
        update(0, i, rows, p, q, across, down, facts_ref, wave_ref, pb_ref, qb_ref, a_ref, b_ref, c_ref, p_ref, q_ref)

    neighbours(p0_ref, q0_ref, dh_ref, dz_ref, high_ref, low_ref, use)
    terms = rim_terms(facts_ref, rim_refs, ds_ref, p_ref.shape)
    add_rims(terms, p_ref, q_ref, a_ref, b_ref, p_ref, q_ref)
    put_rims_of(facts_ref, p_ref, *send_refs)


def update(step, i, rows, p, q, across, down, facts_ref, wave_ref, pb_ref, qb_ref, a_ref, b_ref, c_ref, po_ref, qo_ref):
    flat = p.shape
    a, b, c, pb, qb = (ref[rows].reshape(flat) for ref in (a_ref, b_ref, c_ref, pb_ref, qb_ref))
    block = (XT,) + po_ref.shape[1:]
    at_row = lax.broadcasted_iota(jnp.int32, flat, 0) == jnp.broadcast_to(facts_ref[2:3] - i * flat[0], flat)
    at_z = lax.broadcasted_iota(jnp.int32, flat, 1) == jnp.broadcast_to(facts_ref[3:4], flat)
    source = jnp.where(at_row & at_z, jnp.broadcast_to(wave_ref[step : step + 1], flat), 0.0)
    po_ref[rows] = (2.0 * p - pb + (a * across + b * down) + source).reshape(block)
    qo_ref[rows] = (2.0 * q - qb + (b * across + c * down)).reshape(block)


def inner_kernel(step, facts_ref, wave_ref, p_ref, pb_ref, q_ref, qb_ref, a_ref, b_ref, c_ref, dh_ref, dz_ref,
                 po_ref, qo_ref, high_ref, low_ref):
    def use(i, rows, p, q, across, down):
        update(step, i, rows, p, q, across, down, facts_ref, wave_ref, pb_ref, qb_ref, a_ref, b_ref, c_ref, po_ref, qo_ref)

    neighbours(p_ref, q_ref, dh_ref, dz_ref, high_ref, low_ref, use)


def rim_kernel(n_rims, last, facts_ref, p_in, q_in, a_ref, b_ref, *refs):
    rim_refs, (ds_ref, p_ref, q_ref, *out_refs) = refs[:n_rims], refs[n_rims:]
    terms = rim_terms(facts_ref, rim_refs, ds_ref, p_ref.shape)
    add_rims(terms, p_in, q_in, a_ref, b_ref, p_ref, q_ref)
    if not last:
        put_rims_of(facts_ref, p_ref, *out_refs)
    else:
        p_out, q_out, sem = out_refs
        copies = [pltpu.make_async_copy(p_ref, p_out, sem.at[0]), pltpu.make_async_copy(q_ref, q_out, sem.at[1])]
        for copy in copies:
            copy.start()
        for copy in copies:
            copy.wait()


def call(kernel, name, scalars, arrays, out, scratch=(), aliases=None, hbm=(), hbm_out=0, smem_out=0):
    vmem = pl.BlockSpec(memory_space=pltpu.VMEM)
    smem = pl.BlockSpec(memory_space=pltpu.SMEM)
    anywhere = pl.BlockSpec(memory_space=pl.ANY)
    return pl.pallas_call(
        kernel,
        out_shape=out,
        in_specs=[smem] * len(scalars) + [vmem] * len(arrays) + [anywhere] * len(hbm),
        out_specs=[vmem] * (len(out) - hbm_out - smem_out) + [anywhere] * hbm_out + [smem] * smem_out,
        scratch_shapes=scratch,
        input_output_aliases=aliases or {},
        compiler_params=pltpu.CompilerParams(vmem_limit_bytes=VMEM_LIMIT),
        name=name,
    )(*in_hbm(*scalars), *arrays, *hbm)


def in_vmem(*arrays):
    return [pltpu.with_memory_space_constraint(a, pltpu.VMEM) for a in arrays]


def in_hbm(*arrays):
    return [pltpu.with_memory_space_constraint(a, pltpu.HBM) for a in arrays]


def on_device(velocity, epsilon, delta, anchors, sources, wavelet, p_now, p_prev, q_now, q_prev):
    p, pb, q, qb = p_now[0], p_prev[0], q_now[0], q_prev[0]
    nx, ny, nz = p.shape
    f32, bf16 = jnp.float32, jnp.bfloat16
    ids = jnp.stack([lax.axis_index(name) for name in ("shot", "gx", "gy")])
    block = pltpu.VMEM((nx, ny, nz), f32)
    rim_shapes = [pltpu.VMEM((REACH * n, nz), f32) for axis, n in (("gx", ny), ("gy", nx)) for _ in swaps(lax.axis_size(axis))]
    padded = [pltpu.VMEM((nx + 2 * REACH, ny, nz), bf16)] * 2
    dz = jnp.asarray(depth_matrix(nz), bf16)
    dh = jnp.asarray(plane_matrix(ny), bf16)
    ds = jnp.asarray(side_matrix(nx), bf16)
    facts, waves, *index = call(
        functools.partial(facts_kernel, lax.axis_size("gx"), p.shape), "facts", [ids, anchors, sources, wavelet], [],
        [pltpu.VMEM((8, nz), jnp.int32), pltpu.VMEM((STEPS, nz), f32), *[jax.ShapeDtypeStruct((1,), jnp.int32)] * 2],
        smem_out=2,
    )
    edges = call(
        edge_kernel, "edges", [], in_vmem(facts), rim_shapes,
        [pltpu.VMEM((REACH, ny, nz), f32)] * 2 + [pltpu.VMEM((nx, 8, nz), f32)] * 2 + [pltpu.SemaphoreType.DMA((4,))],
        hbm=in_hbm(p),
    )
    rims = exchange(edges)
    windows, rims = model_windows(ids, anchors, (velocity, epsilon, delta), index, rims)
    p0, q0 = p, q
    p, q, a, b, c, *rims = call(
        functools.partial(first_kernel, len(rims)), "first", [ids, anchors], in_vmem(facts, waves, p0, q0, *rims, dh, dz, ds) + windows,
        [block] * 5 + rim_shapes, padded + [block] * 2 + [pltpu.SemaphoreType.DMA((2, nx // XT))], hbm=in_hbm(pb, qb),
    )
    pb, qb = p0, q0
    for step in range(1, STEPS):
        rims = exchange(rims)
        p_new, q_new = call(
            functools.partial(inner_kernel, step), f"inner_{step}", [],
            in_vmem(facts, waves, p, pb, q, qb, a, b, c, dh, dz), [block] * 2, padded,
        )
        last = step == STEPS - 1
        whole = jax.ShapeDtypeStruct((nx, ny, nz), f32)
        out = call(
            functools.partial(rim_kernel, len(rims), last), f"rims_{step}", [], in_vmem(facts, p_new, q_new, a, b, *rims, ds),
            [block] * 2 + ([whole] * 2 if last else rim_shapes),
            [pltpu.SemaphoreType.DMA((2,))] if last else [],
            {1: 0, 2: 1},
            hbm_out=2 if last else 0,
        )
        pb, qb = p, q
        p, q, *rims = out
    return rims[0][None], rims[1][None]


def solution(mesh):
    model = P(("shot", "gx"), "gy", None)
    field = P("shot", "gx", "gy", None)
    return jax.shard_map(
        on_device,
        mesh=mesh,
        in_specs=(model, model, model, P(), P("shot", None), P("shot", None)) + (field,) * 4,
        out_specs=(field, field),
        check_vma=False,
    )
```

```python
import functools

import jax
import jax.numpy as jnp
import numpy as np
from jax import lax
from jax.experimental import pallas as pl
from jax.experimental.pallas import tpu as pltpu
from jax.sharding import PartitionSpec as P

STEPS = 4
REACH = 4
SCALE = 5040.0
CENTER = -14350.0
OUTER = (8064.0, -1008.0, 128.0, -9.0)
BUCKET = 4
XT = 8
VMEM_LIMIT = 16 * 1024 * 1024


def row_group(anchor, gx, n_gx, rows):
    period = n_gx * rows
    group = lax.div(anchor, period)
    cut = lax.rem(anchor, period) - gx * rows
    return lambda i: jnp.where(i < cut, group + 1, group)


def pick_kernel(n_gx, ids_ref, anchors_ref, field_ref, other_ref, send_ref, here_ref):
    rows = field_ref.shape[0]
    shot, gx = ids_ref[0], ids_ref[1]
    core = shot & 1
    far = row_group(anchors_ref[shot ^ 2], gx, n_gx, rows)
    own = row_group(anchors_ref[shot], gx, n_gx, rows)
    for i in range(rows):
        field, other = field_ref[i], other_ref[i]
        send_ref[i] = jnp.where(far(i) & 1 == core, field, other)
        here_ref[i] = jnp.where(own(i) & 1 == core, field, other)


def join_kernel(n_gx, whose, ids_ref, anchors_ref, *refs):
    *blocks, out_ref = refs
    rows = out_ref.shape[0]
    shot, gx = ids_ref[0], ids_ref[1]
    core, half = shot & 1, shot >> 1
    own = row_group(anchors_ref[shot ^ whose], gx, n_gx, rows)
    for i in range(rows):
        here, across = blocks[0][i], blocks[1][i]
        if len(blocks) == 4:
            mine = own(i) & 1 == core
            here, across = jnp.where(mine, here, blocks[2][i]), jnp.where(mine, across, blocks[3][i])
        out_ref[i] = jnp.where(own(i) >> 1 == half, here, across)


def facts_kernel(n_gx, shape, ids_ref, anchors_ref, sources_ref, wavelet_ref, facts_ref, waves_ref, *index_refs):
    nx, ny, nz = shape
    gx, gy = ids_ref[1], ids_ref[2]
    for k, index_ref in enumerate(index_refs):
        anchor = anchors_ref[ids_ref[0] ^ (2 * k)]
        turn = lax.rem(lax.div(anchor, nx), n_gx)
        rest = lax.rem(anchor, nx)
        bucket = jnp.where(rest > 0, lax.div(rest - 1, BUCKET) + 1, 0)
        index_ref[0] = turn * (nx // BUCKET + 1) + bucket
    lx, ly = sources_ref[0, 0] - gx * nx, sources_ref[0, 1] - gy * ny
    cell = jnp.where((lx >= 0) & (lx < nx) & (ly >= 0) & (ly < ny), lx * ny + ly, -1)
    for k, fact in enumerate((gx & 1, gy & 1, cell, sources_ref[0, 2])):
        facts_ref[k : k + 1] = jnp.full((1, nz), fact, jnp.int32)
    for k in range(STEPS):
        waves_ref[k : k + 1] = jnp.full((1, nz), wavelet_ref[0, k], jnp.float32)


def rotation_branches(n_gx, rows):
    def perm(block, by):
        by %= n_gx
        if by == 0:
            return block
        return lax.ppermute(block, "gx", [(i, (i - by) % n_gx) for i in range(n_gx)])

    def branch(turn, bucket):
        def aligned(block):
            moved = perm(block, turn)
            return jnp.concatenate([moved, jnp.zeros_like(moved[: BUCKET - 1])], 0)

        def split(block):
            k = BUCKET * (bucket - 1)
            return jnp.concatenate(
                [perm(block[k + 1 :], turn), perm(block[: k + BUCKET], turn + 1)], 0
            )

        return aligned if bucket == 0 else split

    return [branch(t, b) for t in range(n_gx) for b in range(rows // BUCKET + 1)]


def model_windows(ids, anchors, fields, index, rims):
    n_gx = lax.axis_size("gx")
    n_shot = lax.axis_size("shot")
    branches = rotation_branches(n_gx, fields[0].shape[0])
    beside = [(i, i ^ 1) for i in range(n_shot)]
    across = [(i, i ^ 2) for i in range(n_shot)]
    like = jax.ShapeDtypeStruct(fields[0].shape, fields[0].dtype)

    def turned(k, whose, *blocks):
        (block,) = call(
            functools.partial(join_kernel, n_gx, whose), f"join_{k}", [ids, anchors], in_vmem(*blocks), [like]
        )
        return lax.switch(index[whose // 2][0], branches, block)

    crossed = [lax.ppermute(fields[0], "shot", across)]
    others = [lax.ppermute(field, "shot", beside) for field in fields]
    sends, heres = [None], [None]
    for k in (1, 2):
        send, here = call(
            functools.partial(pick_kernel, n_gx), f"pick_{k}", [ids, anchors], in_vmem(fields[k], others[k]), [like] * 2
        )
        sends.append(send)
        heres.append(here)
    sends[1], sends[2], crossed[0], rims, index = lax.optimization_barrier((sends[1], sends[2], crossed[0], rims, index))
    crossed += [lax.ppermute(send, "shot", across) for send in sends[1:]]
    far_other = lax.ppermute(crossed[0], "shot", beside)
    windows = [turned(0, 2, fields[0], crossed[0], others[0], far_other)]
    crossed[1], windows[0] = lax.optimization_barrier((crossed[1], windows[0]))
    windows.append(turned(1, 0, heres[1], crossed[1]))
    crossed[2], windows[0], windows[1] = lax.optimization_barrier((crossed[2], windows[0], windows[1]))
    windows[0] = lax.ppermute(windows[0], "shot", across)
    windows.append(turned(2, 0, heres[2], crossed[2]))
    return windows, rims


def swaps(count):
    near = [(i, i ^ 1) for i in range(count)]
    off = [(i, i + 1) for i in range(1, count - 1, 2)]
    return [near] + [off + [(b, a) for a, b in off]] * bool(off)


def exchange(rims):
    sets = [("gx", pairs) for pairs in swaps(lax.axis_size("gx"))] + [("gy", pairs) for pairs in swaps(lax.axis_size("gy"))]
    return [lax.ppermute(rim, axis, pairs) for rim, (axis, pairs) in zip(rims, sets, strict=True)]


def depth_matrix(nz):
    out = np.zeros((nz, nz), np.float32)
    for k, weight in enumerate(OUTER, 1):
        out += weight * (np.eye(nz, k=k, dtype=np.float32) + np.eye(nz, k=-k, dtype=np.float32))
    return out


def plane_matrix(ny):
    out = np.zeros((XT, ny, XT + 2 * REACH, ny), np.float32)
    column = depth_matrix(ny)
    for x in range(XT):
        out[x, :, x + REACH, :] = column
        for k, weight in enumerate(OUTER, 1):
            for at in (x + REACH - k, x + REACH + k):
                out[x, np.arange(ny), at, np.arange(ny)] += weight
    return out.reshape(XT * ny, (XT + 2 * REACH) * ny)


def side_matrix(nx):
    out = np.zeros((nx, 16, 2, nx, REACH), np.float32)
    for y in range(REACH):
        for k, weight in enumerate(OUTER, 1):
            if y - k < 0:
                out[np.arange(nx), y, 0, np.arange(nx), y - k + REACH] = weight
                out[np.arange(nx), 15 - y, 1, np.arange(nx), k - y - 1] = weight
    return out.reshape(nx * 16, 2 * nx * REACH)


def split(values):
    high = values.astype(jnp.bfloat16)
    return high, (values - high.astype(jnp.float32)).astype(jnp.bfloat16)


def dot(a, b):
    return jnp.dot(a, b, preferred_element_type=jnp.float32)


def neighbours(p_ref, q_ref, dh_ref, dz_ref, high_ref, low_ref, use, before=None):
    nx, ny, nz = p_ref.shape
    flat = (XT * ny, nz)
    for ref in (high_ref, low_ref):
        ref[0:REACH] = jnp.zeros((REACH, ny, nz), jnp.bfloat16)
        ref[nx + REACH :] = jnp.zeros((REACH, ny, nz), jnp.bfloat16)

    def cut(i, _):
        x = i * XT
        high, low = split(p_ref[pl.ds(x, XT)])
        high_ref[pl.ds(x + REACH, XT)] = high
        low_ref[pl.ds(x + REACH, XT)] = low
        return _

    lax.fori_loop(0, nx // XT, cut, None)

    def tile(i, _):
        if before:
            before(i)
        x = i * XT
        rows = pl.ds(x, XT)
        p, q = p_ref[rows].reshape(flat), q_ref[rows].reshape(flat)
        window = pl.ds(x, XT + 2 * REACH)
        deep = ((XT + 2 * REACH) * ny, nz)
        both = jnp.concatenate([high_ref[window].reshape(deep), low_ref[window].reshape(deep)], 0)
        across = dot(jnp.concatenate([dh_ref[...]] * 2, 1), both)
        down = dot(jnp.concatenate(split(q), 1), jnp.concatenate([dz_ref[...]] * 2, 0))
        use(i, rows, p, q, across + (2 * CENTER) * p, down + CENTER * q)
        return _

    lax.fori_loop(0, nx // XT, tile, None)


def rim_terms(facts_ref, rim_refs, ds_ref, shape):
    nx, ny, nz = shape
    xa_ref, xb_ref, ya_ref, *yb_ref = rim_refs
    x_odd = jnp.broadcast_to(facts_ref[0:1], (ny, nz)) == 1
    y_odd = jnp.broadcast_to(facts_ref[1:2], (nx * REACH, nz)) == 1
    below, above = [], []
    for i in range(REACH):
        xa, xb = xa_ref[i * ny : (i + 1) * ny], xb_ref[i * ny : (i + 1) * ny]
        below.append(jnp.where(x_odd, xa, xb))
        above.append(jnp.where(x_odd, xb, xa))
    near, far = [], []
    for i in range(REACH):
        near.append(sum(OUTER[i + REACH - h - 1] * below[h] for h in range(i, REACH)))
        far.append(sum(OUTER[REACH + h - i - 1] * above[h] for h in range(0, i + 1)))
    ya = ya_ref[...]
    yb = yb_ref[0][...] if yb_ref else jnp.zeros_like(ya)
    sides = jnp.concatenate([jnp.where(y_odd, ya, yb), jnp.where(y_odd, yb, ya)], 0)
    side = dot(jnp.concatenate([ds_ref[...]] * 2, 1), jnp.concatenate(split(sides), 0))
    return jnp.stack(near), jnp.stack(far), side.reshape(nx, 16, nz)


def put_rims(facts_ref, low_ref, high_ref, head_ref, tail_ref, sxa_ref, sxb_ref, sya_ref, *syb_ref):
    _, ny, nz = low_ref.shape
    nx, cells, _ = head_ref.shape
    x_odd = jnp.broadcast_to(facts_ref[0:1], (ny, nz)) == 1
    y_odd = jnp.broadcast_to(facts_ref[1:2], (2 * REACH, nz)) == 1
    for i in range(REACH):
        low, high = low_ref[i], high_ref[i]
        rows = slice(i * ny, (i + 1) * ny)
        sxa_ref[rows] = jnp.where(x_odd, low, high)
        sxb_ref[rows] = jnp.where(x_odd, high, low)
    for x in range(0, nx, 2):
        head = jnp.concatenate([head_ref[x, 0:REACH], head_ref[x + 1, 0:REACH]], 0)
        tail = jnp.concatenate([tail_ref[x, cells - REACH : cells], tail_ref[x + 1, cells - REACH : cells]], 0)
        rows = slice(x * REACH, (x + 2) * REACH)
        sya_ref[rows] = jnp.where(y_odd, head, tail)
        if syb_ref:
            syb_ref[0][rows] = jnp.where(y_odd, tail, head)


def put_rims_of(facts_ref, p_ref, *rim_refs):
    nx, ny, _ = p_ref.shape
    low, high = p_ref.at[0:REACH], p_ref.at[nx - REACH : nx]
    put_rims(facts_ref, low, high, p_ref.at[:, 0:8], p_ref.at[:, ny - 8 : ny], *rim_refs)


def edge_kernel(facts_ref, p_hbm, *refs):
    *rim_refs, low_ref, high_ref, head_ref, tail_ref, sem = refs
    nx, ny, _ = p_hbm.shape
    parts = (p_hbm.at[0:REACH], p_hbm.at[nx - REACH : nx], p_hbm.at[:, 0:8], p_hbm.at[:, ny - 8 : ny])
    held = (low_ref, high_ref, head_ref, tail_ref)
    copies = [pltpu.make_async_copy(src, dst, sem.at[k]) for k, (src, dst) in enumerate(zip(parts, held))]
    for copy in copies:
        copy.start()
    for copy in copies:
        copy.wait()
    put_rims(facts_ref, *held, *rim_refs)


def add_rims(terms, p_in, q_in, a_ref, b_ref, p_ref, q_ref):
    near, far, side = terms
    nx, ny, nz = p_ref.shape
    for rows, term in ((slice(0, REACH), near), (slice(nx - REACH, nx), far)):
        p_ref[rows] = p_in[rows] + a_ref[rows] * term
        q_ref[rows] = q_in[rows] + b_ref[rows] * term
    for cells, term in ((slice(0, 8), side[:, 0:8]), (slice(ny - 8, ny), side[:, 8:16])):
        p_ref[:, cells] += a_ref[:, cells] * term
        q_ref[:, cells] += b_ref[:, cells] * term


def first_kernel(n_rims, ids_ref, anchors_ref, facts_ref, wave_ref, p0_ref, q0_ref, dh_ref, dz_ref, ds_ref, *refs):
    sources, rims_hbm, refs = refs[:5], refs[5 : 5 + n_rims], refs[5 + n_rims :]
    p_ref, q_ref, a_ref, b_ref, c_ref = refs[:5]
    send_refs, refs = refs[5 : 5 + n_rims], refs[5 + n_rims :]
    high_ref, low_ref, pb_ref, qb_ref, v_ref, e_ref, d_ref = refs[:7]
    held, rim_refs, (sem, rim_sem) = refs[2:7], refs[7 : 7 + n_rims], refs[7 + n_rims :]
    nx, ny, nz = p_ref.shape
    f32 = jnp.float32

    def loads(i):
        out = []
        for k, (src, dst) in enumerate(zip(sources, held)):
            start = i * XT + (first if k >= 2 else 0)
            out.append(pltpu.make_async_copy(src.at[pl.ds(start, XT)], dst.at[pl.ds(i * XT, XT)], sem.at[k, i]))
        return out

    rest = lax.rem(anchors_ref[ids_ref[0]], nx)
    first = jnp.where(rest > 0, lax.rem(rest - 1, BUCKET), 0)
    for i in range(nx // XT):
        for load in loads(i):
            load.start()
    rim_loads = [pltpu.make_async_copy(src, dst, rim_sem.at[k]) for k, (src, dst) in enumerate(zip(rims_hbm, rim_refs))]
    for load in rim_loads:
        load.start()

    def arrive(i):
        for load in loads(i):
            load.wait()

    def use(i, rows, p, q, across, down):
        flat = p.shape
        c = v_ref[rows].reshape(flat).astype(f32)
        c = c * c * f32(1.0 / SCALE)
        a = c * (1.0 + 2.0 * e_ref[rows].reshape(flat).astype(f32))
        b = c * jnp.sqrt(1.0 + 2.0 * d_ref[rows].reshape(flat).astype(f32))
        for ref, value in ((a_ref, a), (b_ref, b), (c_ref, c)):
            ref[rows] = value.reshape((XT, ny, nz))
        update(0, i, rows, p, q, across, down, facts_ref, wave_ref, pb_ref, qb_ref, a, b, c, p_ref, q_ref)

    neighbours(p0_ref, q0_ref, dh_ref, dz_ref, high_ref, low_ref, use, arrive)
    for load in rim_loads:
        load.wait()
    terms = rim_terms(facts_ref, rim_refs, ds_ref, p_ref.shape)
    add_rims(terms, p_ref, q_ref, a_ref, b_ref, p_ref, q_ref)
    put_rims_of(facts_ref, p_ref, *send_refs)


def update(step, i, rows, p, q, across, down, facts_ref, wave_ref, pb_ref, qb_ref, a, b, c, po_ref, qo_ref):
    flat = p.shape
    pb, qb = pb_ref[rows].reshape(flat), qb_ref[rows].reshape(flat)
    block = (XT,) + po_ref.shape[1:]
    at_row = lax.broadcasted_iota(jnp.int32, flat, 0) == jnp.broadcast_to(facts_ref[2:3] - i * flat[0], flat)
    at_z = lax.broadcasted_iota(jnp.int32, flat, 1) == jnp.broadcast_to(facts_ref[3:4], flat)
    source = jnp.where(at_row & at_z, jnp.broadcast_to(wave_ref[step : step + 1], flat), 0.0)
    po_ref[rows] = (2.0 * p - pb + (a * across + b * down) + source).reshape(block)
    qo_ref[rows] = (2.0 * q - qb + (b * across + c * down)).reshape(block)


def inner_kernel(step, facts_ref, wave_ref, p_ref, pb_ref, q_ref, qb_ref, a_ref, b_ref, c_ref, dh_ref, dz_ref,
                 po_ref, qo_ref, high_ref, low_ref):
    def use(i, rows, p, q, across, down):
        a, b, c = (ref[rows].reshape(p.shape) for ref in (a_ref, b_ref, c_ref))
        update(step, i, rows, p, q, across, down, facts_ref, wave_ref, pb_ref, qb_ref, a, b, c, po_ref, qo_ref)

    neighbours(p_ref, q_ref, dh_ref, dz_ref, high_ref, low_ref, use)


def rim_kernel(n_rims, last, facts_ref, p_in, q_in, a_ref, b_ref, *refs):
    rim_refs, (ds_ref, p_ref, q_ref, *out_refs) = refs[:n_rims], refs[n_rims:]
    terms = rim_terms(facts_ref, rim_refs, ds_ref, p_ref.shape)
    add_rims(terms, p_in, q_in, a_ref, b_ref, p_ref, q_ref)
    if not last:
        put_rims_of(facts_ref, p_ref, *out_refs)
    else:
        p_out, q_out, sem = out_refs
        copies = [pltpu.make_async_copy(p_ref, p_out, sem.at[0]), pltpu.make_async_copy(q_ref, q_out, sem.at[1])]
        for copy in copies:
            copy.start()
        for copy in copies:
            copy.wait()


def call(kernel, name, scalars, arrays, out, scratch=(), aliases=None, hbm=(), hbm_out=0, smem_out=0):
    vmem = pl.BlockSpec(memory_space=pltpu.VMEM)
    smem = pl.BlockSpec(memory_space=pltpu.SMEM)
    anywhere = pl.BlockSpec(memory_space=pl.ANY)
    return pl.pallas_call(
        kernel,
        out_shape=out,
        in_specs=[smem] * len(scalars) + [vmem] * len(arrays) + [anywhere] * len(hbm),
        out_specs=[vmem] * (len(out) - hbm_out - smem_out) + [anywhere] * hbm_out + [smem] * smem_out,
        scratch_shapes=scratch,
        input_output_aliases=aliases or {},
        compiler_params=pltpu.CompilerParams(vmem_limit_bytes=VMEM_LIMIT),
        name=name,
    )(*in_hbm(*scalars), *arrays, *hbm)


def in_vmem(*arrays):
    return [pltpu.with_memory_space_constraint(a, pltpu.VMEM) for a in arrays]


def in_hbm(*arrays):
    return [pltpu.with_memory_space_constraint(a, pltpu.HBM) for a in arrays]


def on_device(velocity, epsilon, delta, anchors, sources, wavelet, p_now, p_prev, q_now, q_prev):
    p, pb, q, qb = p_now[0], p_prev[0], q_now[0], q_prev[0]
    nx, ny, nz = p.shape
    f32, bf16 = jnp.float32, jnp.bfloat16
    ids = jnp.stack([lax.axis_index(name) for name in ("shot", "gx", "gy")])
    block = pltpu.VMEM((nx, ny, nz), f32)
    rim_shapes = [pltpu.VMEM((REACH * n, nz), f32) for axis, n in (("gx", ny), ("gy", nx)) for _ in swaps(lax.axis_size(axis))]
    padded = [pltpu.VMEM((nx + 2 * REACH, ny, nz), bf16)] * 2
    dz = jnp.asarray(depth_matrix(nz), bf16)
    dh = jnp.asarray(plane_matrix(ny), bf16)
    ds = jnp.asarray(side_matrix(nx), bf16)
    facts, waves, *index = call(
        functools.partial(facts_kernel, lax.axis_size("gx"), p.shape), "facts", [ids, anchors, sources, wavelet], [],
        [pltpu.VMEM((8, nz), jnp.int32), pltpu.VMEM((STEPS, nz), f32), *[jax.ShapeDtypeStruct((1,), jnp.int32)] * 2],
        smem_out=2,
    )
    edges = call(
        edge_kernel, "edges", [], in_vmem(facts), rim_shapes,
        [pltpu.VMEM((REACH, ny, nz), f32)] * 2 + [pltpu.VMEM((nx, 8, nz), f32)] * 2 + [pltpu.SemaphoreType.DMA((4,))],
        hbm=in_hbm(p),
    )
    rims = exchange(edges)
    windows, rims = model_windows(ids, anchors, (velocity, epsilon, delta), index, rims)
    p0, q0 = p, q
    p, q, a, b, c, *rims = call(
        functools.partial(first_kernel, len(rims)), "first", [ids, anchors], in_vmem(facts, waves, p0, q0, dh, dz, ds),
        [block] * 5 + rim_shapes, padded + [block] * 2 + [pltpu.VMEM((nx, ny, nz), bf16)] * 3 + rim_shapes
        + [pltpu.SemaphoreType.DMA((5, nx // XT)), pltpu.SemaphoreType.DMA((len(rims),))],
        hbm=in_hbm(pb, qb) + windows + in_hbm(*rims),
    )
    pb, qb = p0, q0
    for step in range(1, STEPS):
        rims = exchange(rims)
        p_new, q_new = call(
            functools.partial(inner_kernel, step), f"inner_{step}", [],
            in_vmem(facts, waves, p, pb, q, qb, a, b, c, dh, dz), [block] * 2, padded,
        )
        last = step == STEPS - 1
        whole = jax.ShapeDtypeStruct((nx, ny, nz), f32)
        out = call(
            functools.partial(rim_kernel, len(rims), last), f"rims_{step}", [], in_vmem(facts, p_new, q_new, a, b, *rims, ds),
            [block] * 2 + ([whole] * 2 if last else rim_shapes),
            [pltpu.SemaphoreType.DMA((2,))] if last else [],
            {1: 0, 2: 1},
            hbm_out=2 if last else 0,
        )
        pb, qb = p, q
        p, q, *rims = out
    return rims[0][None], rims[1][None]


def solution(mesh):
    model = P(("shot", "gx"), "gy", None)
    field = P("shot", "gx", "gy", None)
    return jax.shard_map(
        on_device,
        mesh=mesh,
        in_specs=(model, model, model, P(), P("shot", None), P("shot", None)) + (field,) * 4,
        out_specs=(field, field),
        check_vma=False,
    )
```

```python
import functools

import jax
import jax.numpy as jnp
import numpy as np
from jax import lax
from jax.experimental import pallas as pl
from jax.experimental.pallas import tpu as pltpu
from jax.sharding import PartitionSpec as P

STEPS = 4
REACH = 4
SCALE = 5040.0
CENTER = -14350.0
OUTER = (8064.0, -1008.0, 128.0, -9.0)
BUCKET = 4
XT = 8
VMEM_LIMIT = 16 * 1024 * 1024


def row_group(anchor, gx, n_gx, rows):
    period = n_gx * rows
    group = lax.div(anchor, period)
    cut = lax.rem(anchor, period) - gx * rows
    return lambda i: jnp.where(i < cut, group + 1, group)


def pick_kernel(n_gx, ids_ref, anchors_ref, field_ref, other_ref, send_ref, here_ref):
    rows = field_ref.shape[0]
    shot, gx = ids_ref[0], ids_ref[1]
    core = shot & 1
    far = row_group(anchors_ref[shot ^ 2], gx, n_gx, rows)
    own = row_group(anchors_ref[shot], gx, n_gx, rows)
    for i in range(rows):
        field, other = field_ref[i], other_ref[i]
        send_ref[i] = jnp.where(far(i) & 1 == core, field, other)
        here_ref[i] = jnp.where(own(i) & 1 == core, field, other)


def join_kernel(n_gx, whose, ids_ref, anchors_ref, *refs):
    *blocks, out_ref = refs
    rows = out_ref.shape[0]
    shot, gx = ids_ref[0], ids_ref[1]
    core, half = shot & 1, shot >> 1
    own = row_group(anchors_ref[shot ^ whose], gx, n_gx, rows)
    for i in range(rows):
        here, across = blocks[0][i], blocks[1][i]
        if len(blocks) == 4:
            mine = own(i) & 1 == core
            here, across = jnp.where(mine, here, blocks[2][i]), jnp.where(mine, across, blocks[3][i])
        out_ref[i] = jnp.where(own(i) >> 1 == half, here, across)


def facts_kernel(n_gx, shape, ids_ref, anchors_ref, sources_ref, wavelet_ref, facts_ref, waves_ref, *index_refs):
    nx, ny, nz = shape
    gx, gy = ids_ref[1], ids_ref[2]
    for k, index_ref in enumerate(index_refs):
        anchor = anchors_ref[ids_ref[0] ^ (2 * k)]
        turn = lax.rem(lax.div(anchor, nx), n_gx)
        rest = lax.rem(anchor, nx)
        bucket = jnp.where(rest > 0, lax.div(rest - 1, BUCKET) + 1, 0)
        index_ref[0] = turn * (nx // BUCKET + 1) + bucket
    lx, ly = sources_ref[0, 0] - gx * nx, sources_ref[0, 1] - gy * ny
    cell = jnp.where((lx >= 0) & (lx < nx) & (ly >= 0) & (ly < ny), lx * ny + ly, -1)
    for k, fact in enumerate((gx & 1, gy & 1, cell, sources_ref[0, 2])):
        facts_ref[k : k + 1] = jnp.full((1, nz), fact, jnp.int32)
    for k in range(STEPS):
        waves_ref[k : k + 1] = jnp.full((1, nz), wavelet_ref[0, k], jnp.float32)


def rotation_branches(n_gx, rows):
    def perm(block, by):
        by %= n_gx
        if by == 0:
            return block
        return lax.ppermute(block, "gx", [(i, (i - by) % n_gx) for i in range(n_gx)])

    def branch(turn, bucket):
        def aligned(block):
            moved = perm(block, turn)
            return jnp.concatenate([moved, jnp.zeros_like(moved[: BUCKET - 1])], 0)

        def split(block):
            k = BUCKET * (bucket - 1)
            return jnp.concatenate(
                [perm(block[k + 1 :], turn), perm(block[: k + BUCKET], turn + 1)], 0
            )

        return aligned if bucket == 0 else split

    return [branch(t, b) for t in range(n_gx) for b in range(rows // BUCKET + 1)]


def model_windows(ids, anchors, fields, index, rims):
    n_gx = lax.axis_size("gx")
    n_shot = lax.axis_size("shot")
    branches = rotation_branches(n_gx, fields[0].shape[0])
    beside = [(i, i ^ 1) for i in range(n_shot)]
    across = [(i, i ^ 2) for i in range(n_shot)]
    like = jax.ShapeDtypeStruct(fields[0].shape, fields[0].dtype)

    def turned(k, whose, *blocks):
        (block,) = call(
            functools.partial(join_kernel, n_gx, whose), f"join_{k}", [ids, anchors], in_vmem(*blocks), [like]
        )
        return lax.switch(index[whose // 2][0], branches, block)

    crossed = [lax.ppermute(fields[0], "shot", across)]
    others = [lax.ppermute(field, "shot", beside) for field in fields]
    sends, heres = [None], [None]
    for k in (1, 2):
        send, here = call(
            functools.partial(pick_kernel, n_gx), f"pick_{k}", [ids, anchors], in_vmem(fields[k], others[k]), [like] * 2
        )
        sends.append(send)
        heres.append(here)
    sends[1], sends[2], crossed[0], rims, index = lax.optimization_barrier((sends[1], sends[2], crossed[0], rims, index))
    crossed += [lax.ppermute(send, "shot", across) for send in sends[1:]]
    far_other = lax.ppermute(crossed[0], "shot", beside)
    windows = [turned(0, 2, fields[0], crossed[0], others[0], far_other)]
    crossed[1], windows[0] = lax.optimization_barrier((crossed[1], windows[0]))
    windows.append(turned(1, 0, heres[1], crossed[1]))
    crossed[2], windows[0], windows[1] = lax.optimization_barrier((crossed[2], windows[0], windows[1]))
    windows[0] = lax.ppermute(windows[0], "shot", across)
    windows.append(turned(2, 0, heres[2], crossed[2]))
    return windows, rims


def swaps(count):
    near = [(i, i ^ 1) for i in range(count)]
    off = [(i, i + 1) for i in range(1, count - 1, 2)]
    return [near] + [off + [(b, a) for a, b in off]] * bool(off)


def exchange(rims):
    sets = [("gx", pairs) for pairs in swaps(lax.axis_size("gx"))] + [("gy", pairs) for pairs in swaps(lax.axis_size("gy"))]
    return [lax.ppermute(rim, axis, pairs) for rim, (axis, pairs) in zip(rims, sets, strict=True)]


def depth_matrix(nz):
    out = np.zeros((nz, nz), np.float32)
    for k, weight in enumerate(OUTER, 1):
        out += weight * (np.eye(nz, k=k, dtype=np.float32) + np.eye(nz, k=-k, dtype=np.float32))
    return out


def plane_matrix(ny):
    out = np.zeros((XT, ny, XT + 2 * REACH, ny), np.float32)
    column = depth_matrix(ny)
    for x in range(XT):
        out[x, :, x + REACH, :] = column
        for k, weight in enumerate(OUTER, 1):
            for at in (x + REACH - k, x + REACH + k):
                out[x, np.arange(ny), at, np.arange(ny)] += weight
    return out.reshape(XT * ny, (XT + 2 * REACH) * ny)


def side_matrix(nx):
    out = np.zeros((nx, 16, 2, REACH + 1, nx), np.float32)
    x = np.arange(nx)
    for cell in range(REACH):
        for plane in range(REACH + 1):
            reach = cell + plane % REACH
            if reach < REACH:
                out[x, cell, 0, plane, x] = OUTER[reach]
                out[x, 15 - cell, 1, plane, x] = OUTER[reach]
    return out.reshape(nx * 16, 2 * (REACH + 1) * nx)


def split(values):
    high = values.astype(jnp.bfloat16)
    return high, (values - high.astype(jnp.float32)).astype(jnp.bfloat16)


def dot(a, b):
    return jnp.dot(a, b, preferred_element_type=jnp.float32)


def neighbours(p_ref, q_ref, dh_ref, dz_ref, high_ref, low_ref, use, before=None):
    nx, ny, nz = p_ref.shape
    flat = (XT * ny, nz)
    for ref in (high_ref, low_ref):
        ref[0:REACH] = jnp.zeros((REACH, ny, nz), jnp.bfloat16)
        ref[nx + REACH :] = jnp.zeros((REACH, ny, nz), jnp.bfloat16)

    def cut(i, _):
        x = i * XT
        high, low = split(p_ref[pl.ds(x, XT)])
        high_ref[pl.ds(x + REACH, XT)] = high
        low_ref[pl.ds(x + REACH, XT)] = low
        return _

    lax.fori_loop(0, nx // XT, cut, None)

    def tile(i, _):
        if before:
            before(i)
        x = i * XT
        rows = pl.ds(x, XT)
        p, q = p_ref[rows].reshape(flat), q_ref[rows].reshape(flat)
        window = pl.ds(x, XT + 2 * REACH)
        deep = ((XT + 2 * REACH) * ny, nz)
        both = jnp.concatenate([high_ref[window].reshape(deep), low_ref[window].reshape(deep)], 0)
        across = dot(jnp.concatenate([dh_ref[...]] * 2, 1), both)
        down = dot(jnp.concatenate(split(q), 1), jnp.concatenate([dz_ref[...]] * 2, 0))
        use(i, rows, p, q, across + (2 * CENTER) * p, down + CENTER * q)
        return _

    lax.fori_loop(0, nx // XT, tile, None)


def rim_terms(facts_ref, rim_refs, ds_ref, shape):
    nx, ny, nz = shape
    xa_ref, xb_ref, ya_ref, *yb_ref = rim_refs
    x_odd = jnp.broadcast_to(facts_ref[0:1], (ny, nz)) == 1
    below, above = [], []
    for d in range(REACH):
        xa, xb = (ref[d * ny : (d + 1) * ny].astype(jnp.float32) for ref in (xa_ref, xb_ref))
        if d == 0:
            xa, xb = (v + ref[REACH * ny :].astype(jnp.float32) for v, ref in ((xa, xa_ref), (xb, xb_ref)))
        below.append(jnp.where(x_odd, xa, xb))
        above.append(jnp.where(x_odd, xb, xa))
    near, far = [], []
    for i in range(REACH):
        near.append(sum(OUTER[i + d] * below[d] for d in range(REACH - i)))
        far.insert(0, sum(OUTER[i + d] * above[d] for d in range(REACH - i)))
    ya = ya_ref[...]
    y_odd = jnp.broadcast_to(facts_ref[1:2].astype(jnp.float32).astype(ya.dtype), ya.shape)
    low_side, high_side = ya * y_odd, ya * (1 - y_odd)
    if yb_ref:
        yb = yb_ref[0][...]
        low_side, high_side = low_side + yb * (1 - y_odd), high_side + yb * y_odd
    side = dot(ds_ref[...], jnp.concatenate([low_side, high_side], 0))
    return jnp.stack(near), jnp.stack(far), side.reshape(nx, 16, nz)


def put_rims(facts_ref, low_ref, high_ref, head_ref, tail_ref, sxa_ref, sxb_ref, sya_ref, *syb_ref):
    _, ny, nz = low_ref.shape
    nx, cells, _ = head_ref.shape
    x_odd = jnp.broadcast_to(facts_ref[0:1], (ny, nz)) == 1
    y_odd = jnp.broadcast_to(facts_ref[1:2], (nx, nz)) == 1
    for d in range(REACH):
        low, high = low_ref[d], high_ref[REACH - 1 - d]
        put_plane(d, sxa_ref, jnp.where(x_odd, low, high))
        put_plane(d, sxb_ref, jnp.where(x_odd, high, low))
        head, tail = head_ref[:, d, :], tail_ref[:, cells - 1 - d, :]
        put_plane(d, sya_ref, jnp.where(y_odd, head, tail))
        if syb_ref:
            put_plane(d, syb_ref[0], jnp.where(y_odd, tail, head))


def put_plane(d, ref, plane):
    high, low = split(plane)
    count = plane.shape[0]
    ref[d * count : (d + 1) * count] = high
    if d == 0:
        ref[REACH * count :] = low


def put_rims_of(facts_ref, p_ref, *rim_refs):
    nx, ny, _ = p_ref.shape
    low, high = p_ref.at[0:REACH], p_ref.at[nx - REACH : nx]
    put_rims(facts_ref, low, high, p_ref, p_ref, *rim_refs)


def edge_kernel(facts_ref, p_hbm, *refs):
    *rim_refs, low_ref, high_ref, head_ref, tail_ref, sem = refs
    nx, ny, _ = p_hbm.shape
    parts = (p_hbm.at[0:REACH], p_hbm.at[nx - REACH : nx], p_hbm.at[:, 0:8], p_hbm.at[:, ny - 8 : ny])
    held = (low_ref, high_ref, head_ref, tail_ref)
    copies = [pltpu.make_async_copy(src, dst, sem.at[k]) for k, (src, dst) in enumerate(zip(parts, held))]
    for copy in copies:
        copy.start()
    for copy in copies:
        copy.wait()
    put_rims(facts_ref, *held, *rim_refs)


def add_rims(terms, p_in, q_in, a_ref, b_ref, p_ref, q_ref):
    near, far, side = terms
    nx, ny, nz = p_ref.shape
    for rows, term in ((slice(0, REACH), near), (slice(nx - REACH, nx), far)):
        p_ref[rows] = p_in[rows] + a_ref[rows] * term
        q_ref[rows] = q_in[rows] + b_ref[rows] * term
    for cells, term in ((slice(0, 8), side[:, 0:8]), (slice(ny - 8, ny), side[:, 8:16])):
        p_ref[:, cells] += a_ref[:, cells] * term
        q_ref[:, cells] += b_ref[:, cells] * term


def first_kernel(n_rims, ids_ref, anchors_ref, facts_ref, wave_ref, p0_ref, q0_ref, dh_ref, dz_ref, ds_ref, *refs):
    sources, rims_hbm, refs = refs[:5], refs[5 : 5 + n_rims], refs[5 + n_rims :]
    p_ref, q_ref, a_ref, b_ref, c_ref = refs[:5]
    send_refs, refs = refs[5 : 5 + n_rims], refs[5 + n_rims :]
    high_ref, low_ref, pb_ref, qb_ref, v_ref, e_ref, d_ref = refs[:7]
    held, rim_refs, (sem, rim_sem) = refs[2:7], refs[7 : 7 + n_rims], refs[7 + n_rims :]
    nx, ny, nz = p_ref.shape
    f32 = jnp.float32

    def loads(i):
        out = []
        for k, (src, dst) in enumerate(zip(sources, held)):
            start = i * XT + (first if k >= 2 else 0)
            out.append(pltpu.make_async_copy(src.at[pl.ds(start, XT)], dst.at[pl.ds(i * XT, XT)], sem.at[k, i]))
        return out

    rest = lax.rem(anchors_ref[ids_ref[0]], nx)
    first = jnp.where(rest > 0, lax.rem(rest - 1, BUCKET), 0)
    for i in range(nx // XT):
        for load in loads(i):
            load.start()
    rim_loads = [pltpu.make_async_copy(src, dst, rim_sem.at[k]) for k, (src, dst) in enumerate(zip(rims_hbm, rim_refs))]
    for load in rim_loads:
        load.start()

    def arrive(i):
        for load in loads(i):
            load.wait()

    def use(i, rows, p, q, across, down):
        flat = p.shape
        c = v_ref[rows].reshape(flat).astype(f32)
        c = c * c * f32(1.0 / SCALE)
        a = c * (1.0 + 2.0 * e_ref[rows].reshape(flat).astype(f32))
        b = c * jnp.sqrt(1.0 + 2.0 * d_ref[rows].reshape(flat).astype(f32))
        for ref, value in ((a_ref, a), (b_ref, b), (c_ref, c)):
            ref[rows] = value.reshape((XT, ny, nz))
        update(0, i, rows, p, q, across, down, facts_ref, wave_ref, pb_ref, qb_ref, a, b, c, p_ref, q_ref)

    neighbours(p0_ref, q0_ref, dh_ref, dz_ref, high_ref, low_ref, use, arrive)
    for load in rim_loads:
        load.wait()
    terms = rim_terms(facts_ref, rim_refs, ds_ref, p_ref.shape)
    add_rims(terms, p_ref, q_ref, a_ref, b_ref, p_ref, q_ref)
    put_rims_of(facts_ref, p_ref, *send_refs)


def update(step, i, rows, p, q, across, down, facts_ref, wave_ref, pb_ref, qb_ref, a, b, c, po_ref, qo_ref):
    flat = p.shape
    pb, qb = pb_ref[rows].reshape(flat), qb_ref[rows].reshape(flat)
    block = (XT,) + po_ref.shape[1:]
    at_row = lax.broadcasted_iota(jnp.int32, flat, 0) == jnp.broadcast_to(facts_ref[2:3] - i * flat[0], flat)
    at_z = lax.broadcasted_iota(jnp.int32, flat, 1) == jnp.broadcast_to(facts_ref[3:4], flat)
    source = jnp.where(at_row & at_z, jnp.broadcast_to(wave_ref[step : step + 1], flat), 0.0)
    po_ref[rows] = (2.0 * p - pb + (a * across + b * down) + source).reshape(block)
    qo_ref[rows] = (2.0 * q - qb + (b * across + c * down)).reshape(block)


def inner_kernel(step, facts_ref, wave_ref, p_ref, pb_ref, q_ref, qb_ref, a_ref, b_ref, c_ref, dh_ref, dz_ref,
                 po_ref, qo_ref, high_ref, low_ref):
    def use(i, rows, p, q, across, down):
        a, b, c = (ref[rows].reshape(p.shape) for ref in (a_ref, b_ref, c_ref))
        update(step, i, rows, p, q, across, down, facts_ref, wave_ref, pb_ref, qb_ref, a, b, c, po_ref, qo_ref)

    neighbours(p_ref, q_ref, dh_ref, dz_ref, high_ref, low_ref, use)


def rim_kernel(n_rims, last, facts_ref, p_in, q_in, a_ref, b_ref, *refs):
    rim_refs, (ds_ref, p_ref, q_ref, *out_refs) = refs[:n_rims], refs[n_rims:]
    terms = rim_terms(facts_ref, rim_refs, ds_ref, p_ref.shape)
    add_rims(terms, p_in, q_in, a_ref, b_ref, p_ref, q_ref)
    if not last:
        put_rims_of(facts_ref, p_ref, *out_refs)
    else:
        p_out, q_out, sem = out_refs
        copies = [pltpu.make_async_copy(p_ref, p_out, sem.at[0]), pltpu.make_async_copy(q_ref, q_out, sem.at[1])]
        for copy in copies:
            copy.start()
        for copy in copies:
            copy.wait()


def call(kernel, name, scalars, arrays, out, scratch=(), aliases=None, hbm=(), hbm_out=0, smem_out=0):
    vmem = pl.BlockSpec(memory_space=pltpu.VMEM)
    smem = pl.BlockSpec(memory_space=pltpu.SMEM)
    anywhere = pl.BlockSpec(memory_space=pl.ANY)
    return pl.pallas_call(
        kernel,
        out_shape=out,
        in_specs=[smem] * len(scalars) + [vmem] * len(arrays) + [anywhere] * len(hbm),
        out_specs=[vmem] * (len(out) - hbm_out - smem_out) + [anywhere] * hbm_out + [smem] * smem_out,
        scratch_shapes=scratch,
        input_output_aliases=aliases or {},
        compiler_params=pltpu.CompilerParams(vmem_limit_bytes=VMEM_LIMIT),
        name=name,
    )(*in_hbm(*scalars), *arrays, *hbm)


def in_vmem(*arrays):
    return [pltpu.with_memory_space_constraint(a, pltpu.VMEM) for a in arrays]


def in_hbm(*arrays):
    return [pltpu.with_memory_space_constraint(a, pltpu.HBM) for a in arrays]


def on_device(velocity, epsilon, delta, anchors, sources, wavelet, p_now, p_prev, q_now, q_prev):
    p, pb, q, qb = p_now[0], p_prev[0], q_now[0], q_prev[0]
    nx, ny, nz = p.shape
    f32, bf16 = jnp.float32, jnp.bfloat16
    ids = jnp.stack([lax.axis_index(name) for name in ("shot", "gx", "gy")])
    block = pltpu.VMEM((nx, ny, nz), f32)
    x_rim, y_rim = (pltpu.VMEM(((REACH + 1) * n, nz), bf16) for n in (ny, nx))
    rim_shapes = [x_rim] * len(swaps(lax.axis_size("gx"))) + [y_rim] * len(swaps(lax.axis_size("gy")))
    padded = [pltpu.VMEM((nx + 2 * REACH, ny, nz), bf16)] * 2
    dz = jnp.asarray(depth_matrix(nz), bf16)
    dh = jnp.asarray(plane_matrix(ny), bf16)
    ds = jnp.asarray(side_matrix(nx), bf16)
    facts, waves, *index = call(
        functools.partial(facts_kernel, lax.axis_size("gx"), p.shape), "facts", [ids, anchors, sources, wavelet], [],
        [pltpu.VMEM((8, nz), jnp.int32), pltpu.VMEM((STEPS, nz), f32), *[jax.ShapeDtypeStruct((1,), jnp.int32)] * 2],
        smem_out=2,
    )
    edges = call(
        edge_kernel, "edges", [], in_vmem(facts), rim_shapes,
        [pltpu.VMEM((REACH, ny, nz), f32)] * 2 + [pltpu.VMEM((nx, 8, nz), f32)] * 2 + [pltpu.SemaphoreType.DMA((4,))],
        hbm=in_hbm(p),
    )
    rims = exchange(edges)
    windows, rims = model_windows(ids, anchors, (velocity, epsilon, delta), index, rims)
    p0, q0 = p, q
    p, q, a, b, c, *rims = call(
        functools.partial(first_kernel, len(rims)), "first", [ids, anchors], in_vmem(facts, waves, p0, q0, dh, dz, ds),
        [block] * 5 + rim_shapes, padded + [block] * 2 + [pltpu.VMEM((nx, ny, nz), bf16)] * 3 + rim_shapes
        + [pltpu.SemaphoreType.DMA((5, nx // XT)), pltpu.SemaphoreType.DMA((len(rims),))],
        hbm=in_hbm(pb, qb) + windows + in_hbm(*rims),
    )
    pb, qb = p0, q0
    for step in range(1, STEPS):
        rims = exchange(rims)
        p_new, q_new = call(
            functools.partial(inner_kernel, step), f"inner_{step}", [],
            in_vmem(facts, waves, p, pb, q, qb, a, b, c, dh, dz), [block] * 2, padded,
        )
        last = step == STEPS - 1
        whole = jax.ShapeDtypeStruct((nx, ny, nz), f32)
        out = call(
            functools.partial(rim_kernel, len(rims), last), f"rims_{step}", [], in_vmem(facts, p_new, q_new, a, b, *rims, ds),
            [block] * 2 + ([whole] * 2 if last else rim_shapes),
            [pltpu.SemaphoreType.DMA((2,))] if last else [],
            {1: 0, 2: 1},
            hbm_out=2 if last else 0,
        )
        pb, qb = p, q
        p, q, *rims = out
    return rims[0][None], rims[1][None]


def solution(mesh):
    model = P(("shot", "gx"), "gy", None)
    field = P("shot", "gx", "gy", None)
    return jax.shard_map(
        on_device,
        mesh=mesh,
        in_specs=(model, model, model, P(), P("shot", None), P("shot", None)) + (field,) * 4,
        out_specs=(field, field),
        check_vma=False,
    )
```

```python
import functools

import jax
import jax.numpy as jnp
import numpy as np
from jax import lax
from jax.experimental import pallas as pl
from jax.experimental.pallas import tpu as pltpu
from jax.sharding import PartitionSpec as P

STEPS = 4
REACH = 4
SCALE = 5040.0
CENTER = -14350.0
OUTER = (8064.0, -1008.0, 128.0, -9.0)
BUCKET = 4
XT = 8
VMEM_LIMIT = 16 * 1024 * 1024


def row_group(anchor, gx, n_gx, rows):
    period = n_gx * rows
    group = lax.div(anchor, period)
    cut = lax.rem(anchor, period) - gx * rows
    return lambda i: jnp.where(i < cut, group + 1, group)


def pick_kernel(n_gx, ids_ref, anchors_ref, field_ref, other_ref, send_ref, here_ref):
    rows = field_ref.shape[0]
    shot, gx = ids_ref[0], ids_ref[1]
    core = shot & 1
    far = row_group(anchors_ref[shot ^ 2], gx, n_gx, rows)
    own = row_group(anchors_ref[shot], gx, n_gx, rows)
    for i in range(rows):
        field, other = field_ref[i], other_ref[i]
        send_ref[i] = jnp.where(far(i) & 1 == core, field, other)
        here_ref[i] = jnp.where(own(i) & 1 == core, field, other)


def join_kernel(n_gx, whose, ids_ref, anchors_ref, *refs):
    *blocks, out_ref = refs
    rows = out_ref.shape[0]
    shot, gx = ids_ref[0], ids_ref[1]
    core, half = shot & 1, shot >> 1
    own = row_group(anchors_ref[shot ^ whose], gx, n_gx, rows)
    for i in range(rows):
        here, across = blocks[0][i], blocks[1][i]
        if len(blocks) == 4:
            mine = own(i) & 1 == core
            here, across = jnp.where(mine, here, blocks[2][i]), jnp.where(mine, across, blocks[3][i])
        out_ref[i] = jnp.where(own(i) >> 1 == half, here, across)


def facts_kernel(n_gx, shape, ids_ref, anchors_ref, sources_ref, wavelet_ref, facts_ref, waves_ref, *index_refs):
    nx, ny, nz = shape
    gx, gy = ids_ref[1], ids_ref[2]
    for k, index_ref in enumerate(index_refs):
        anchor = anchors_ref[ids_ref[0] ^ (2 * k)]
        turn = lax.rem(lax.div(anchor, nx), n_gx)
        rest = lax.rem(anchor, nx)
        bucket = jnp.where(rest > 0, lax.div(rest - 1, BUCKET) + 1, 0)
        index_ref[0] = turn * (nx // BUCKET + 1) + bucket
    lx, ly = sources_ref[0, 0] - gx * nx, sources_ref[0, 1] - gy * ny
    cell = jnp.where((lx >= 0) & (lx < nx) & (ly >= 0) & (ly < ny), lx * ny + ly, -1)
    for k, fact in enumerate((gx & 1, gy & 1, cell, sources_ref[0, 2])):
        facts_ref[k : k + 1] = jnp.full((1, nz), fact, jnp.int32)
    for k in range(STEPS):
        waves_ref[k : k + 1] = jnp.full((1, nz), wavelet_ref[0, k], jnp.float32)


def rotation_branches(n_gx, rows):
    def perm(block, by):
        by %= n_gx
        if by == 0:
            return block
        return lax.ppermute(block, "gx", [(i, (i - by) % n_gx) for i in range(n_gx)])

    def branch(turn, bucket):
        def aligned(block):
            moved = perm(block, turn)
            return jnp.concatenate([moved, jnp.zeros_like(moved[: BUCKET - 1])], 0)

        def split(block):
            k = BUCKET * (bucket - 1)
            return jnp.concatenate(
                [perm(block[k + 1 :], turn), perm(block[: k + BUCKET], turn + 1)], 0
            )

        return aligned if bucket == 0 else split

    return [branch(t, b) for t in range(n_gx) for b in range(rows // BUCKET + 1)]


def model_windows(ids, anchors, fields, index, rims):
    n_gx = lax.axis_size("gx")
    n_shot = lax.axis_size("shot")
    branches = rotation_branches(n_gx, fields[0].shape[0])
    beside = [(i, i ^ 1) for i in range(n_shot)]
    across = [(i, i ^ 2) for i in range(n_shot)]
    like = jax.ShapeDtypeStruct(fields[0].shape, fields[0].dtype)

    def turned(k, whose, *blocks):
        (block,) = call(
            functools.partial(join_kernel, n_gx, whose), f"join_{k}", [ids, anchors], in_vmem(*blocks), [like]
        )
        return lax.switch(index[whose // 2][0], branches, block)

    crossed = [lax.ppermute(fields[0], "shot", across)]
    others = [lax.ppermute(field, "shot", beside) for field in fields]
    sends, heres = [None], [None]
    for k in (1, 2):
        send, here = call(
            functools.partial(pick_kernel, n_gx), f"pick_{k}", [ids, anchors], in_vmem(fields[k], others[k]), [like] * 2
        )
        sends.append(send)
        heres.append(here)
    sends[1], sends[2], crossed[0], rims, index = lax.optimization_barrier((sends[1], sends[2], crossed[0], rims, index))
    crossed += [lax.ppermute(send, "shot", across) for send in sends[1:]]
    far_other = lax.ppermute(crossed[0], "shot", beside)
    windows = [turned(0, 2, fields[0], crossed[0], others[0], far_other)]
    crossed[1], windows[0] = lax.optimization_barrier((crossed[1], windows[0]))
    windows.append(turned(1, 0, heres[1], crossed[1]))
    crossed[2], windows[0], windows[1] = lax.optimization_barrier((crossed[2], windows[0], windows[1]))
    windows[0] = lax.ppermute(windows[0], "shot", across)
    windows.append(turned(2, 0, heres[2], crossed[2]))
    return windows, rims


def swaps(count):
    near = [(i, i ^ 1) for i in range(count)]
    off = [(i, i + 1) for i in range(1, count - 1, 2)]
    return [near] + [off + [(b, a) for a, b in off]] * bool(off)


def exchange(rims):
    sets = [("gx", pairs) for pairs in swaps(lax.axis_size("gx"))] + [("gy", pairs) for pairs in swaps(lax.axis_size("gy"))]
    return [lax.ppermute(rim, axis, pairs) for rim, (axis, pairs) in zip(rims, sets, strict=True)]


def depth_matrix(nz):
    out = np.zeros((nz, nz), np.float32)
    for k, weight in enumerate(OUTER, 1):
        out += weight * (np.eye(nz, k=k, dtype=np.float32) + np.eye(nz, k=-k, dtype=np.float32))
    return out


def plane_matrix(ny):
    out = np.zeros((XT, ny, XT + 2 * REACH, ny), np.float32)
    column = depth_matrix(ny)
    for x in range(XT):
        out[x, :, x + REACH, :] = column
        for k, weight in enumerate(OUTER, 1):
            for at in (x + REACH - k, x + REACH + k):
                out[x, np.arange(ny), at, np.arange(ny)] += weight
    return out.reshape(XT * ny, (XT + 2 * REACH) * ny)


def side_matrix(nx):
    out = np.zeros((nx, 16, 2, REACH + 1, nx), np.float32)
    x = np.arange(nx)
    for cell in range(REACH):
        for plane in range(REACH + 1):
            reach = cell + plane % REACH
            if reach < REACH:
                out[x, cell, 0, plane, x] = OUTER[reach]
                out[x, 15 - cell, 1, plane, x] = OUTER[reach]
    return out.reshape(nx * 16, 2 * (REACH + 1) * nx)


def split(values):
    high = values.astype(jnp.bfloat16)
    return high, (values - high.astype(jnp.float32)).astype(jnp.bfloat16)


def dot(a, b):
    return jnp.dot(a, b, preferred_element_type=jnp.float32)


def neighbours(p_ref, q_ref, dh_ref, dz_ref, high_ref, low_ref, use, before=None):
    nx, ny, nz = p_ref.shape
    flat = (XT * ny, nz)
    for ref in (high_ref, low_ref):
        ref[0:REACH] = jnp.zeros((REACH, ny, nz), jnp.bfloat16)
        ref[nx + REACH :] = jnp.zeros((REACH, ny, nz), jnp.bfloat16)

    def cut(i, _):
        x = i * XT
        high, low = split(p_ref[pl.ds(x, XT)])
        high_ref[pl.ds(x + REACH, XT)] = high
        low_ref[pl.ds(x + REACH, XT)] = low
        return _

    lax.fori_loop(0, nx // XT, cut, None)

    def tile(i, _):
        if before:
            before(i)
        x = i * XT
        rows = pl.ds(x, XT)
        p, q = p_ref[rows].reshape(flat), q_ref[rows].reshape(flat)
        window = pl.ds(x, XT + 2 * REACH)
        deep = ((XT + 2 * REACH) * ny, nz)
        both = jnp.concatenate([high_ref[window].reshape(deep), low_ref[window].reshape(deep)], 0)
        across = dot(jnp.concatenate([dh_ref[...]] * 2, 1), both)
        down = dot(jnp.concatenate(split(q), 1), jnp.concatenate([dz_ref[...]] * 2, 0))
        use(i, rows, p, q, across + (2 * CENTER) * p, down + CENTER * q)
        return _

    lax.fori_loop(0, nx // XT, tile, None)


def rim_terms(facts_ref, rim_refs, ds_ref, shape):
    nx, ny, nz = shape
    xa_ref, xb_ref, ya_ref, *yb_ref = rim_refs
    x_odd = jnp.broadcast_to(facts_ref[0:1], (ny, nz)) == 1
    below, above = [], []
    for d in range(REACH):
        xa, xb = (ref[d * ny : (d + 1) * ny].astype(jnp.float32) for ref in (xa_ref, xb_ref))
        if d == 0:
            xa, xb = (v + ref[REACH * ny :].astype(jnp.float32) for v, ref in ((xa, xa_ref), (xb, xb_ref)))
        below.append(jnp.where(x_odd, xa, xb))
        above.append(jnp.where(x_odd, xb, xa))
    near, far = [], []
    for i in range(REACH):
        near.append(sum(OUTER[i + d] * below[d] for d in range(REACH - i)))
        far.insert(0, sum(OUTER[i + d] * above[d] for d in range(REACH - i)))
    ya = ya_ref[...]
    y_odd = jnp.broadcast_to(facts_ref[1:2].astype(jnp.float32).astype(ya.dtype), ya.shape)
    low_side, high_side = ya * y_odd, ya * (1 - y_odd)
    if yb_ref:
        yb = yb_ref[0][...]
        low_side, high_side = low_side + yb * (1 - y_odd), high_side + yb * y_odd
    side = dot(ds_ref[...], jnp.concatenate([low_side, high_side], 0))
    return jnp.stack(near), jnp.stack(far), side.reshape(nx, 16, nz)


def put_rims(facts_ref, low_ref, high_ref, head_ref, tail_ref, sxa_ref, sxb_ref, sya_ref, *syb_ref):
    _, ny, nz = low_ref.shape
    nx, cells, _ = head_ref.shape
    x_odd = jnp.broadcast_to(facts_ref[0:1], (ny, nz)) == 1
    y_odd = jnp.broadcast_to(facts_ref[1:2], (nx, nz)) == 1
    for d in range(REACH):
        low, high = low_ref[d], high_ref[REACH - 1 - d]
        put_plane(d, sxa_ref, jnp.where(x_odd, low, high))
        put_plane(d, sxb_ref, jnp.where(x_odd, high, low))
        head, tail = head_ref[:, d, :], tail_ref[:, cells - 1 - d, :]
        put_plane(d, sya_ref, jnp.where(y_odd, head, tail))
        if syb_ref:
            put_plane(d, syb_ref[0], jnp.where(y_odd, tail, head))


def put_plane(d, ref, plane):
    high, low = split(plane)
    count = plane.shape[0]
    ref[d * count : (d + 1) * count] = high
    if d == 0:
        ref[REACH * count :] = low


def put_rims_of(facts_ref, p_ref, *rim_refs):
    nx, ny, _ = p_ref.shape
    low, high = p_ref.at[0:REACH], p_ref.at[nx - REACH : nx]
    put_rims(facts_ref, low, high, p_ref, p_ref, *rim_refs)


def edge_kernel(facts_ref, p_hbm, *refs):
    *rim_refs, low_ref, high_ref, head_ref, tail_ref, sem = refs
    nx, ny, _ = p_hbm.shape
    parts = (p_hbm.at[0:REACH], p_hbm.at[nx - REACH : nx], p_hbm.at[:, 0:8], p_hbm.at[:, ny - 8 : ny])
    held = (low_ref, high_ref, head_ref, tail_ref)
    copies = [pltpu.make_async_copy(src, dst, sem.at[k]) for k, (src, dst) in enumerate(zip(parts, held))]
    for copy in copies:
        copy.start()
    for copy in copies:
        copy.wait()
    put_rims(facts_ref, *held, *rim_refs)


def add_rims(terms, p_in, q_in, a_ref, b_ref, p_ref, q_ref):
    near, far, side = terms
    nx, ny, nz = p_ref.shape
    for rows, term in ((slice(0, REACH), near), (slice(nx - REACH, nx), far)):
        p_ref[rows] = p_in[rows] + a_ref[rows] * term
        q_ref[rows] = q_in[rows] + b_ref[rows] * term
    for cells, term in ((slice(0, 8), side[:, 0:8]), (slice(ny - 8, ny), side[:, 8:16])):
        p_ref[:, cells] += a_ref[:, cells] * term
        q_ref[:, cells] += b_ref[:, cells] * term


def first_kernel(n_rims, ids_ref, anchors_ref, facts_ref, wave_ref, p0_ref, q0_ref, dh_ref, dz_ref, ds_ref, *refs):
    sources, rims_hbm, refs = refs[:5], refs[5 : 5 + n_rims], refs[5 + n_rims :]
    p_ref, q_ref, a_ref, b_ref, c_ref = refs[:5]
    send_refs, refs = refs[5 : 5 + n_rims], refs[5 + n_rims :]
    high_ref, low_ref, pb_ref, qb_ref, v_ref, e_ref, d_ref = refs[:7]
    held, rim_refs, (sem, rim_sem) = refs[2:7], refs[7 : 7 + n_rims], refs[7 + n_rims :]
    nx, ny, nz = p_ref.shape
    f32 = jnp.float32

    def loads(i):
        out = []
        for k, (src, dst) in enumerate(zip(sources, held)):
            start = i * XT + (first if k >= 2 else 0)
            out.append(pltpu.make_async_copy(src.at[pl.ds(start, XT)], dst.at[pl.ds(i * XT, XT)], sem.at[k, i]))
        return out

    rest = lax.rem(anchors_ref[ids_ref[0]], nx)
    first = jnp.where(rest > 0, lax.rem(rest - 1, BUCKET), 0)
    for i in range(nx // XT):
        for load in loads(i):
            load.start()
    rim_loads = [pltpu.make_async_copy(src, dst, rim_sem.at[k]) for k, (src, dst) in enumerate(zip(rims_hbm, rim_refs))]
    for load in rim_loads:
        load.start()

    def arrive(i):
        for load in loads(i):
            load.wait()

    def use(i, rows, p, q, across, down):
        flat = p.shape
        c = v_ref[rows].reshape(flat).astype(f32)
        c = c * c * f32(1.0 / SCALE)
        a = c * (1.0 + 2.0 * e_ref[rows].reshape(flat).astype(f32))
        b = c * jnp.sqrt(1.0 + 2.0 * d_ref[rows].reshape(flat).astype(f32))
        for ref, value in ((a_ref, a), (b_ref, b), (c_ref, c)):
            ref[rows] = value.reshape((XT, ny, nz))
        update(0, i, rows, p, q, across, down, facts_ref, wave_ref, pb_ref, qb_ref, a, b, c, p_ref, q_ref)

    neighbours(p0_ref, q0_ref, dh_ref, dz_ref, high_ref, low_ref, use, arrive)
    for load in rim_loads:
        load.wait()
    terms = rim_terms(facts_ref, rim_refs, ds_ref, p_ref.shape)
    add_rims(terms, p_ref, q_ref, a_ref, b_ref, p_ref, q_ref)
    put_rims_of(facts_ref, p_ref, *send_refs)


def update(step, i, rows, p, q, across, down, facts_ref, wave_ref, pb_ref, qb_ref, a, b, c, po_ref, qo_ref):
    flat = p.shape
    pb, qb = pb_ref[rows].reshape(flat), qb_ref[rows].reshape(flat)
    block = (XT,) + po_ref.shape[1:]
    at_row = lax.broadcasted_iota(jnp.int32, flat, 0) == jnp.broadcast_to(facts_ref[2:3] - i * flat[0], flat)
    at_z = lax.broadcasted_iota(jnp.int32, flat, 1) == jnp.broadcast_to(facts_ref[3:4], flat)
    source = jnp.where(at_row & at_z, jnp.broadcast_to(wave_ref[step : step + 1], flat), 0.0)
    po_ref[rows] = (2.0 * p - pb + (a * across + b * down) + source).reshape(block)
    qo_ref[rows] = (2.0 * q - qb + (b * across + c * down)).reshape(block)


def inner_kernel(step, facts_ref, wave_ref, p_ref, pb_ref, q_ref, qb_ref, a_ref, b_ref, c_ref, dh_ref, dz_ref,
                 po_ref, qo_ref, high_ref, low_ref):
    def use(i, rows, p, q, across, down):
        a, b, c = (ref[rows].reshape(p.shape) for ref in (a_ref, b_ref, c_ref))
        update(step, i, rows, p, q, across, down, facts_ref, wave_ref, pb_ref, qb_ref, a, b, c, po_ref, qo_ref)

    neighbours(p_ref, q_ref, dh_ref, dz_ref, high_ref, low_ref, use)


def rim_kernel(n_rims, last, facts_ref, p_in, q_in, a_ref, b_ref, *refs):
    rim_refs, (ds_ref, p_ref, q_ref, *out_refs) = refs[:n_rims], refs[n_rims:]
    near, far, side = rim_terms(facts_ref, rim_refs, ds_ref, p_ref.shape)
    if not last:
        add_rims((near, far, side), p_in, q_in, a_ref, b_ref, p_ref, q_ref)
        put_rims_of(facts_ref, p_ref, *out_refs)
        return
    p_out, q_out, sem = out_refs
    nx, ny, _ = p_ref.shape
    for rows, term in ((slice(0, REACH), near), (slice(nx - REACH, nx), far)):
        p_ref[rows] = p_in[rows] + a_ref[rows] * term
        q_ref[rows] = q_in[rows] + b_ref[rows] * term
    copies = []
    for i in range(nx // XT):
        rows = slice(i * XT, (i + 1) * XT)
        for cells, term in ((slice(0, 8), side[rows, 0:8]), (slice(ny - 8, ny), side[rows, 8:16])):
            p_ref[rows, cells] += a_ref[rows, cells] * term
            q_ref[rows, cells] += b_ref[rows, cells] * term
        for k, (ref, out) in enumerate(((p_ref, p_out), (q_ref, q_out))):
            copies.append(pltpu.make_async_copy(ref.at[rows], out.at[rows], sem.at[k, i]))
            copies[-1].start()
    for copy in copies:
        copy.wait()


def call(kernel, name, scalars, arrays, out, scratch=(), aliases=None, hbm=(), hbm_out=0, smem_out=0):
    vmem = pl.BlockSpec(memory_space=pltpu.VMEM)
    smem = pl.BlockSpec(memory_space=pltpu.SMEM)
    anywhere = pl.BlockSpec(memory_space=pl.ANY)
    return pl.pallas_call(
        kernel,
        out_shape=out,
        in_specs=[smem] * len(scalars) + [vmem] * len(arrays) + [anywhere] * len(hbm),
        out_specs=[vmem] * (len(out) - hbm_out - smem_out) + [anywhere] * hbm_out + [smem] * smem_out,
        scratch_shapes=scratch,
        input_output_aliases=aliases or {},
        compiler_params=pltpu.CompilerParams(vmem_limit_bytes=VMEM_LIMIT),
        name=name,
    )(*in_hbm(*scalars), *arrays, *hbm)


def in_vmem(*arrays):
    return [pltpu.with_memory_space_constraint(a, pltpu.VMEM) for a in arrays]


def in_hbm(*arrays):
    return [pltpu.with_memory_space_constraint(a, pltpu.HBM) for a in arrays]


def on_device(velocity, epsilon, delta, anchors, sources, wavelet, p_now, p_prev, q_now, q_prev):
    p, pb, q, qb = p_now[0], p_prev[0], q_now[0], q_prev[0]
    nx, ny, nz = p.shape
    f32, bf16 = jnp.float32, jnp.bfloat16
    ids = jnp.stack([lax.axis_index(name) for name in ("shot", "gx", "gy")])
    block = pltpu.VMEM((nx, ny, nz), f32)
    x_rim, y_rim = (pltpu.VMEM(((REACH + 1) * n, nz), bf16) for n in (ny, nx))
    rim_shapes = [x_rim] * len(swaps(lax.axis_size("gx"))) + [y_rim] * len(swaps(lax.axis_size("gy")))
    padded = [pltpu.VMEM((nx + 2 * REACH, ny, nz), bf16)] * 2
    dz = jnp.asarray(depth_matrix(nz), bf16)
    dh = jnp.asarray(plane_matrix(ny), bf16)
    ds = jnp.asarray(side_matrix(nx), bf16)
    facts, waves, *index = call(
        functools.partial(facts_kernel, lax.axis_size("gx"), p.shape), "facts", [ids, anchors, sources, wavelet], [],
        [pltpu.VMEM((8, nz), jnp.int32), pltpu.VMEM((STEPS, nz), f32), *[jax.ShapeDtypeStruct((1,), jnp.int32)] * 2],
        smem_out=2,
    )
    edges = call(
        edge_kernel, "edges", [], in_vmem(facts), rim_shapes,
        [pltpu.VMEM((REACH, ny, nz), f32)] * 2 + [pltpu.VMEM((nx, 8, nz), f32)] * 2 + [pltpu.SemaphoreType.DMA((4,))],
        hbm=in_hbm(p),
    )
    rims = exchange(edges)
    windows, rims = model_windows(ids, anchors, (velocity, epsilon, delta), index, rims)
    p0, q0 = p, q
    p, q, a, b, c, *rims = call(
        functools.partial(first_kernel, len(rims)), "first", [ids, anchors], in_vmem(facts, waves, p0, q0, dh, dz, ds),
        [block] * 5 + rim_shapes, padded + [block] * 2 + [pltpu.VMEM((nx, ny, nz), bf16)] * 3 + rim_shapes
        + [pltpu.SemaphoreType.DMA((5, nx // XT)), pltpu.SemaphoreType.DMA((len(rims),))],
        hbm=in_hbm(pb, qb) + windows + in_hbm(*rims),
    )
    pb, qb = p0, q0
    for step in range(1, STEPS):
        rims = exchange(rims)
        p_new, q_new = call(
            functools.partial(inner_kernel, step), f"inner_{step}", [],
            in_vmem(facts, waves, p, pb, q, qb, a, b, c, dh, dz), [block] * 2, padded,
        )
        last = step == STEPS - 1
        whole = jax.ShapeDtypeStruct((nx, ny, nz), f32)
        out = call(
            functools.partial(rim_kernel, len(rims), last), f"rims_{step}", [], in_vmem(facts, p_new, q_new, a, b, *rims, ds),
            [block] * 2 + ([whole] * 2 if last else rim_shapes),
            [pltpu.SemaphoreType.DMA((2, nx // XT))] if last else [],
            {1: 0, 2: 1},
            hbm_out=2 if last else 0,
        )
        pb, qb = p, q
        p, q, *rims = out
    return rims[0][None], rims[1][None]


def solution(mesh):
    model = P(("shot", "gx"), "gy", None)
    field = P("shot", "gx", "gy", None)
    return jax.shard_map(
        on_device,
        mesh=mesh,
        in_specs=(model, model, model, P(), P("shot", None), P("shot", None)) + (field,) * 4,
        out_specs=(field, field),
        check_vma=False,
    )
```

```python
import functools

import jax
import jax.numpy as jnp
import numpy as np
from jax import lax
from jax.experimental import pallas as pl
from jax.experimental.pallas import tpu as pltpu
from jax.sharding import PartitionSpec as P

STEPS = 4
REACH = 4
SCALE = 5040.0
CENTER = -14350.0
OUTER = (8064.0, -1008.0, 128.0, -9.0)
BUCKET = 4
XT = 8
VMEM_LIMIT = 16 * 1024 * 1024


def row_group(anchor, gx, n_gx, rows):
    period = n_gx * rows
    group = lax.div(anchor, period)
    cut = lax.rem(anchor, period) - gx * rows
    return lambda i: jnp.where(i < cut, group + 1, group)


def pick_kernel(n_gx, ids_ref, anchors_ref, field_ref, other_ref, send_ref, here_ref):
    rows = field_ref.shape[0]
    shot, gx = ids_ref[0], ids_ref[1]
    core = shot & 1
    far = row_group(anchors_ref[shot ^ 2], gx, n_gx, rows)
    own = row_group(anchors_ref[shot], gx, n_gx, rows)
    for i in range(rows):
        field, other = field_ref[i], other_ref[i]
        send_ref[i] = jnp.where(far(i) & 1 == core, field, other)
        here_ref[i] = jnp.where(own(i) & 1 == core, field, other)


def join_kernel(n_gx, whose, ids_ref, anchors_ref, *refs):
    *blocks, out_ref = refs
    rows = out_ref.shape[0]
    shot, gx = ids_ref[0], ids_ref[1]
    core, half = shot & 1, shot >> 1
    own = row_group(anchors_ref[shot ^ whose], gx, n_gx, rows)
    for i in range(rows):
        here, across = blocks[0][i], blocks[1][i]
        if len(blocks) == 4:
            mine = own(i) & 1 == core
            here, across = jnp.where(mine, here, blocks[2][i]), jnp.where(mine, across, blocks[3][i])
        out_ref[i] = jnp.where(own(i) >> 1 == half, here, across)


def facts_kernel(n_gx, shape, ids_ref, anchors_ref, sources_ref, wavelet_ref, facts_ref, waves_ref, *index_refs):
    nx, ny, nz = shape
    gx, gy = ids_ref[1], ids_ref[2]
    for k, index_ref in enumerate(index_refs):
        anchor = anchors_ref[ids_ref[0] ^ (2 * k)]
        turn = lax.rem(lax.div(anchor, nx), n_gx)
        rest = lax.rem(anchor, nx)
        bucket = jnp.where(rest > 0, lax.div(rest - 1, BUCKET) + 1, 0)
        index_ref[0] = turn * (nx // BUCKET + 1) + bucket
    lx, ly = sources_ref[0, 0] - gx * nx, sources_ref[0, 1] - gy * ny
    cell = jnp.where((lx >= 0) & (lx < nx) & (ly >= 0) & (ly < ny), lx * ny + ly, -1)
    for k, fact in enumerate((gx & 1, gy & 1, cell, sources_ref[0, 2])):
        facts_ref[k : k + 1] = jnp.full((1, nz), fact, jnp.int32)
    for k in range(STEPS):
        waves_ref[k : k + 1] = jnp.full((1, nz), wavelet_ref[0, k], jnp.float32)


def rotation_branches(n_gx, rows):
    def perm(block, by):
        by %= n_gx
        if by == 0:
            return block
        return lax.ppermute(block, "gx", [(i, (i - by) % n_gx) for i in range(n_gx)])

    def branch(turn, bucket):
        def aligned(block):
            moved = perm(block, turn)
            return jnp.concatenate([moved, jnp.zeros_like(moved[: BUCKET - 1])], 0)

        def split(block):
            k = BUCKET * (bucket - 1)
            return jnp.concatenate(
                [perm(block[k + 1 :], turn), perm(block[: k + BUCKET], turn + 1)], 0
            )

        return aligned if bucket == 0 else split

    return [branch(t, b) for t in range(n_gx) for b in range(rows // BUCKET + 1)]


def model_windows(ids, anchors, fields, index, rims):
    n_gx = lax.axis_size("gx")
    n_shot = lax.axis_size("shot")
    branches = rotation_branches(n_gx, fields[0].shape[0])
    beside = [(i, i ^ 1) for i in range(n_shot)]
    across = [(i, i ^ 2) for i in range(n_shot)]
    like = jax.ShapeDtypeStruct(fields[0].shape, fields[0].dtype)

    def turned(k, whose, *blocks):
        (block,) = call(
            functools.partial(join_kernel, n_gx, whose), f"join_{k}", [ids, anchors], in_vmem(*blocks), [like]
        )
        return lax.switch(index[whose // 2][0], branches, block)

    crossed = [lax.ppermute(fields[0], "shot", across)]
    others = [lax.ppermute(field, "shot", beside) for field in fields]
    sends, heres = [None], [None]
    for k in (1, 2):
        send, here = call(
            functools.partial(pick_kernel, n_gx), f"pick_{k}", [ids, anchors], in_vmem(fields[k], others[k]), [like] * 2
        )
        sends.append(send)
        heres.append(here)
    sends[1], sends[2], crossed[0], rims, index = lax.optimization_barrier((sends[1], sends[2], crossed[0], rims, index))
    crossed += [lax.ppermute(send, "shot", across) for send in sends[1:]]
    far_other = lax.ppermute(crossed[0], "shot", beside)
    windows = [turned(0, 2, fields[0], crossed[0], others[0], far_other)]
    crossed[1], windows[0] = lax.optimization_barrier((crossed[1], windows[0]))
    windows.append(turned(1, 0, heres[1], crossed[1]))
    crossed[2], windows[0], windows[1] = lax.optimization_barrier((crossed[2], windows[0], windows[1]))
    windows[0] = lax.ppermute(windows[0], "shot", across)
    windows.append(turned(2, 0, heres[2], crossed[2]))
    return windows, rims


def swaps(count):
    near = [(i, i ^ 1) for i in range(count)]
    off = [(i, i + 1) for i in range(1, count - 1, 2)]
    return [near] + [off + [(b, a) for a, b in off]] * bool(off)


def exchange(rims):
    sets = [("gx", pairs) for pairs in swaps(lax.axis_size("gx"))] + [("gy", pairs) for pairs in swaps(lax.axis_size("gy"))]
    return [lax.ppermute(rim, axis, pairs) for rim, (axis, pairs) in zip(rims, sets, strict=True)]


def depth_matrix(nz):
    out = np.zeros((nz, nz), np.float32)
    for k, weight in enumerate(OUTER, 1):
        out += weight * (np.eye(nz, k=k, dtype=np.float32) + np.eye(nz, k=-k, dtype=np.float32))
    return out


def plane_matrix(ny):
    out = np.zeros((XT, ny, XT + 2 * REACH, ny), np.float32)
    column = depth_matrix(ny)
    for x in range(XT):
        out[x, :, x + REACH, :] = column
        for k, weight in enumerate(OUTER, 1):
            for at in (x + REACH - k, x + REACH + k):
                out[x, np.arange(ny), at, np.arange(ny)] += weight
    return out.reshape(XT * ny, (XT + 2 * REACH) * ny)


def side_matrix(nx):
    out = np.zeros((nx, 16, 2, REACH + 1, nx), np.float32)
    x = np.arange(nx)
    for cell in range(REACH):
        for plane in range(REACH + 1):
            reach = cell + plane % REACH
            if reach < REACH:
                out[x, cell, 0, plane, x] = OUTER[reach]
                out[x, 15 - cell, 1, plane, x] = OUTER[reach]
    return out.reshape(nx * 16, 2 * (REACH + 1) * nx)


def split(values):
    high = values.astype(jnp.bfloat16)
    return high, (values - high.astype(jnp.float32)).astype(jnp.bfloat16)


def dot(a, b):
    return jnp.dot(a, b, preferred_element_type=jnp.float32)


def neighbours(p_ref, q_ref, dh_ref, dz_ref, high_ref, low_ref, use, before=None, between=None):
    nx, ny, nz = p_ref.shape
    flat = (XT * ny, nz)
    for ref in (high_ref, low_ref):
        ref[0:REACH] = jnp.zeros((REACH, ny, nz), jnp.bfloat16)
        ref[nx + REACH :] = jnp.zeros((REACH, ny, nz), jnp.bfloat16)

    def cut(i, _):
        x = i * XT
        high, low = split(p_ref[pl.ds(x, XT)])
        high_ref[pl.ds(x + REACH, XT)] = high
        low_ref[pl.ds(x + REACH, XT)] = low
        return _

    lax.fori_loop(0, nx // XT, cut, None)
    if between:
        between()

    def tile(i, _):
        if before:
            before(i)
        x = i * XT
        rows = pl.ds(x, XT)
        p, q = p_ref[rows].reshape(flat), q_ref[rows].reshape(flat)
        window = pl.ds(x, XT + 2 * REACH)
        deep = ((XT + 2 * REACH) * ny, nz)
        both = jnp.concatenate([high_ref[window].reshape(deep), low_ref[window].reshape(deep)], 0)
        across = dot(jnp.concatenate([dh_ref[...]] * 2, 1), both)
        down = dot(jnp.concatenate(split(q), 1), jnp.concatenate([dz_ref[...]] * 2, 0))
        use(i, rows, p, q, across + (2 * CENTER) * p, down + CENTER * q)
        return _

    lax.fori_loop(0, nx // XT, tile, None)


def rim_terms(facts_ref, rim_refs, ds_ref, shape):
    nx, ny, nz = shape
    xa_ref, xb_ref, ya_ref, *yb_ref = rim_refs
    x_odd = jnp.broadcast_to(facts_ref[0:1], (ny, nz)) == 1
    below, above = [], []
    for d in range(REACH):
        xa, xb = (ref[d * ny : (d + 1) * ny].astype(jnp.float32) for ref in (xa_ref, xb_ref))
        if d == 0:
            xa, xb = (v + ref[REACH * ny :].astype(jnp.float32) for v, ref in ((xa, xa_ref), (xb, xb_ref)))
        below.append(jnp.where(x_odd, xa, xb))
        above.append(jnp.where(x_odd, xb, xa))
    near, far = [], []
    for i in range(REACH):
        near.append(sum(OUTER[i + d] * below[d] for d in range(REACH - i)))
        far.insert(0, sum(OUTER[i + d] * above[d] for d in range(REACH - i)))
    ya = ya_ref[...]
    y_odd = jnp.broadcast_to(facts_ref[1:2].astype(jnp.float32).astype(ya.dtype), ya.shape)
    low_side, high_side = ya * y_odd, ya * (1 - y_odd)
    if yb_ref:
        yb = yb_ref[0][...]
        low_side, high_side = low_side + yb * (1 - y_odd), high_side + yb * y_odd
    side = dot(ds_ref[...], jnp.concatenate([low_side, high_side], 0))
    return jnp.stack(near), jnp.stack(far), side.reshape(nx, 16, nz)


def put_rims(facts_ref, low_ref, high_ref, head_ref, tail_ref, sxa_ref, sxb_ref, sya_ref, *syb_ref):
    _, ny, nz = low_ref.shape
    nx, cells, _ = head_ref.shape
    x_odd = jnp.broadcast_to(facts_ref[0:1], (ny, nz)) == 1
    y_odd = jnp.broadcast_to(facts_ref[1:2], (nx, nz)) == 1
    for d in range(REACH):
        low, high = low_ref[d], high_ref[REACH - 1 - d]
        put_plane(d, sxa_ref, jnp.where(x_odd, low, high))
        put_plane(d, sxb_ref, jnp.where(x_odd, high, low))
        head, tail = head_ref[:, d, :], tail_ref[:, cells - 1 - d, :]
        put_plane(d, sya_ref, jnp.where(y_odd, head, tail))
        if syb_ref:
            put_plane(d, syb_ref[0], jnp.where(y_odd, tail, head))


def put_plane(d, ref, plane):
    high, low = split(plane)
    count = plane.shape[0]
    ref[d * count : (d + 1) * count] = high
    if d == 0:
        ref[REACH * count :] = low


def put_rims_of(facts_ref, p_ref, *rim_refs):
    nx, ny, _ = p_ref.shape
    low, high = p_ref.at[0:REACH], p_ref.at[nx - REACH : nx]
    put_rims(facts_ref, low, high, p_ref, p_ref, *rim_refs)


def edge_kernel(facts_ref, p_hbm, *refs):
    *rim_refs, low_ref, high_ref, head_ref, tail_ref, sem = refs
    nx, ny, _ = p_hbm.shape
    parts = (p_hbm.at[0:REACH], p_hbm.at[nx - REACH : nx], p_hbm.at[:, 0:8], p_hbm.at[:, ny - 8 : ny])
    held = (low_ref, high_ref, head_ref, tail_ref)
    copies = [pltpu.make_async_copy(src, dst, sem.at[k]) for k, (src, dst) in enumerate(zip(parts, held))]
    for copy in copies:
        copy.start()
    for copy in copies:
        copy.wait()
    put_rims(facts_ref, *held, *rim_refs)


def add_rims(terms, p_in, q_in, a_ref, b_ref, p_ref, q_ref):
    near, far, side = terms
    nx, ny, nz = p_ref.shape
    for rows, term in ((slice(0, REACH), near), (slice(nx - REACH, nx), far)):
        p_ref[rows] = p_in[rows] + a_ref[rows] * term
        q_ref[rows] = q_in[rows] + b_ref[rows] * term
    for cells, term in ((slice(0, 8), side[:, 0:8]), (slice(ny - 8, ny), side[:, 8:16])):
        p_ref[:, cells] += a_ref[:, cells] * term
        q_ref[:, cells] += b_ref[:, cells] * term


def first_kernel(n_rims, ids_ref, anchors_ref, facts_ref, wave_ref, p0_ref, q0_ref, dh_ref, dz_ref, ds_ref, *refs):
    sources, rims_hbm, refs = refs[:5], refs[5 : 5 + n_rims], refs[5 + n_rims :]
    p_ref, q_ref, a_ref, b_ref, c_ref = refs[:5]
    send_refs, refs = refs[5 : 5 + n_rims], refs[5 + n_rims :]
    high_ref, low_ref, pb_ref, qb_ref, v_ref, e_ref, d_ref = refs[:7]
    held, rim_refs, (sem, rim_sem) = refs[2:7], refs[7 : 7 + n_rims], refs[7 + n_rims :]
    nx, ny, nz = p_ref.shape
    f32 = jnp.float32

    def loads(i):
        out = []
        for k, (src, dst) in enumerate(zip(sources, held)):
            start = i * XT + (first if k >= 2 else 0)
            out.append(pltpu.make_async_copy(src.at[pl.ds(start, XT)], dst.at[pl.ds(i * XT, XT)], sem.at[k, i]))
        return out

    rest = lax.rem(anchors_ref[ids_ref[0]], nx)
    first = jnp.where(rest > 0, lax.rem(rest - 1, BUCKET), 0)
    rim_loads = [pltpu.make_async_copy(src, dst, rim_sem.at[k]) for k, (src, dst) in enumerate(zip(rims_hbm, rim_refs))]
    for load in rim_loads:
        load.start()
    for i in range(nx // XT):
        for load in loads(i):
            load.start()
    terms = []

    def sums():
        for load in rim_loads:
            load.wait()
        terms.extend(rim_terms(facts_ref, rim_refs, ds_ref, p_ref.shape))

    def arrive(i):
        for load in loads(i):
            load.wait()

    def use(i, rows, p, q, across, down):
        flat = p.shape
        c = v_ref[rows].reshape(flat).astype(f32)
        c = c * c * f32(1.0 / SCALE)
        a = c * (1.0 + 2.0 * e_ref[rows].reshape(flat).astype(f32))
        b = c * jnp.sqrt(1.0 + 2.0 * d_ref[rows].reshape(flat).astype(f32))
        for ref, value in ((a_ref, a), (b_ref, b), (c_ref, c)):
            ref[rows] = value.reshape((XT, ny, nz))
        update(0, i, rows, p, q, across, down, facts_ref, wave_ref, pb_ref, qb_ref, a, b, c, p_ref, q_ref)

    neighbours(p0_ref, q0_ref, dh_ref, dz_ref, high_ref, low_ref, use, arrive, sums)
    add_rims(terms, p_ref, q_ref, a_ref, b_ref, p_ref, q_ref)
    put_rims_of(facts_ref, p_ref, *send_refs)


def update(step, i, rows, p, q, across, down, facts_ref, wave_ref, pb_ref, qb_ref, a, b, c, po_ref, qo_ref):
    flat = p.shape
    pb, qb = pb_ref[rows].reshape(flat), qb_ref[rows].reshape(flat)
    block = (XT,) + po_ref.shape[1:]
    at_row = lax.broadcasted_iota(jnp.int32, flat, 0) == jnp.broadcast_to(facts_ref[2:3] - i * flat[0], flat)
    at_z = lax.broadcasted_iota(jnp.int32, flat, 1) == jnp.broadcast_to(facts_ref[3:4], flat)
    source = jnp.where(at_row & at_z, jnp.broadcast_to(wave_ref[step : step + 1], flat), 0.0)
    po_ref[rows] = (2.0 * p - pb + (a * across + b * down) + source).reshape(block)
    qo_ref[rows] = (2.0 * q - qb + (b * across + c * down)).reshape(block)


def inner_kernel(step, facts_ref, wave_ref, p_ref, pb_ref, q_ref, qb_ref, a_ref, b_ref, c_ref, dh_ref, dz_ref,
                 po_ref, qo_ref, high_ref, low_ref):
    def use(i, rows, p, q, across, down):
        a, b, c = (ref[rows].reshape(p.shape) for ref in (a_ref, b_ref, c_ref))
        update(step, i, rows, p, q, across, down, facts_ref, wave_ref, pb_ref, qb_ref, a, b, c, po_ref, qo_ref)

    neighbours(p_ref, q_ref, dh_ref, dz_ref, high_ref, low_ref, use)


def rim_kernel(n_rims, last, facts_ref, p_in, q_in, a_ref, b_ref, *refs):
    rim_refs, (ds_ref, p_ref, q_ref, *out_refs) = refs[:n_rims], refs[n_rims:]
    near, far, side = rim_terms(facts_ref, rim_refs, ds_ref, p_ref.shape)
    if not last:
        add_rims((near, far, side), p_in, q_in, a_ref, b_ref, p_ref, q_ref)
        put_rims_of(facts_ref, p_ref, *out_refs)
        return
    p_out, q_out, sem = out_refs
    nx, ny, _ = p_ref.shape
    for rows, term in ((slice(0, REACH), near), (slice(nx - REACH, nx), far)):
        p_ref[rows] = p_in[rows] + a_ref[rows] * term
        q_ref[rows] = q_in[rows] + b_ref[rows] * term
    copies = []
    for i in range(nx // XT):
        rows = slice(i * XT, (i + 1) * XT)
        for cells, term in ((slice(0, 8), side[rows, 0:8]), (slice(ny - 8, ny), side[rows, 8:16])):
            p_ref[rows, cells] += a_ref[rows, cells] * term
            q_ref[rows, cells] += b_ref[rows, cells] * term
        for k, (ref, out) in enumerate(((p_ref, p_out), (q_ref, q_out))):
            copies.append(pltpu.make_async_copy(ref.at[rows], out.at[rows], sem.at[k, i]))
            copies[-1].start()
    for copy in copies:
        copy.wait()


def call(kernel, name, scalars, arrays, out, scratch=(), aliases=None, hbm=(), hbm_out=0, smem_out=0):
    vmem = pl.BlockSpec(memory_space=pltpu.VMEM)
    smem = pl.BlockSpec(memory_space=pltpu.SMEM)
    anywhere = pl.BlockSpec(memory_space=pl.ANY)
    return pl.pallas_call(
        kernel,
        out_shape=out,
        in_specs=[smem] * len(scalars) + [vmem] * len(arrays) + [anywhere] * len(hbm),
        out_specs=[vmem] * (len(out) - hbm_out - smem_out) + [anywhere] * hbm_out + [smem] * smem_out,
        scratch_shapes=scratch,
        input_output_aliases=aliases or {},
        compiler_params=pltpu.CompilerParams(vmem_limit_bytes=VMEM_LIMIT),
        name=name,
    )(*in_hbm(*scalars), *arrays, *hbm)


def in_vmem(*arrays):
    return [pltpu.with_memory_space_constraint(a, pltpu.VMEM) for a in arrays]


def in_hbm(*arrays):
    return [pltpu.with_memory_space_constraint(a, pltpu.HBM) for a in arrays]


def on_device(velocity, epsilon, delta, anchors, sources, wavelet, p_now, p_prev, q_now, q_prev):
    p, pb, q, qb = p_now[0], p_prev[0], q_now[0], q_prev[0]
    nx, ny, nz = p.shape
    f32, bf16 = jnp.float32, jnp.bfloat16
    ids = jnp.stack([lax.axis_index(name) for name in ("shot", "gx", "gy")])
    block = pltpu.VMEM((nx, ny, nz), f32)
    x_rim, y_rim = (pltpu.VMEM(((REACH + 1) * n, nz), bf16) for n in (ny, nx))
    rim_shapes = [x_rim] * len(swaps(lax.axis_size("gx"))) + [y_rim] * len(swaps(lax.axis_size("gy")))
    padded = [pltpu.VMEM((nx + 2 * REACH, ny, nz), bf16)] * 2
    dz = jnp.asarray(depth_matrix(nz), bf16)
    dh = jnp.asarray(plane_matrix(ny), bf16)
    ds = jnp.asarray(side_matrix(nx), bf16)
    facts, waves, *index = call(
        functools.partial(facts_kernel, lax.axis_size("gx"), p.shape), "facts", [ids, anchors, sources, wavelet], [],
        [pltpu.VMEM((8, nz), jnp.int32), pltpu.VMEM((STEPS, nz), f32), *[jax.ShapeDtypeStruct((1,), jnp.int32)] * 2],
        smem_out=2,
    )
    edges = call(
        edge_kernel, "edges", [], in_vmem(facts), rim_shapes,
        [pltpu.VMEM((REACH, ny, nz), f32)] * 2 + [pltpu.VMEM((nx, 8, nz), f32)] * 2 + [pltpu.SemaphoreType.DMA((4,))],
        hbm=in_hbm(p),
    )
    rims = exchange(edges)
    windows, rims = model_windows(ids, anchors, (velocity, epsilon, delta), index, rims)
    p0, q0 = p, q
    p, q, a, b, c, *rims = call(
        functools.partial(first_kernel, len(rims)), "first", [ids, anchors], in_vmem(facts, waves, p0, q0, dh, dz, ds),
        [block] * 5 + rim_shapes, padded + [block] * 2 + [pltpu.VMEM((nx, ny, nz), bf16)] * 3 + rim_shapes
        + [pltpu.SemaphoreType.DMA((5, nx // XT)), pltpu.SemaphoreType.DMA((len(rims),))],
        hbm=in_hbm(pb, qb) + windows + in_hbm(*rims),
    )
    pb, qb = p0, q0
    for step in range(1, STEPS):
        rims = exchange(rims)
        p_new, q_new = call(
            functools.partial(inner_kernel, step), f"inner_{step}", [],
            in_vmem(facts, waves, p, pb, q, qb, a, b, c, dh, dz), [block] * 2, padded,
        )
        last = step == STEPS - 1
        whole = jax.ShapeDtypeStruct((nx, ny, nz), f32)
        out = call(
            functools.partial(rim_kernel, len(rims), last), f"rims_{step}", [], in_vmem(facts, p_new, q_new, a, b, *rims, ds),
            [block] * 2 + ([whole] * 2 if last else rim_shapes),
            [pltpu.SemaphoreType.DMA((2, nx // XT))] if last else [],
            {1: 0, 2: 1},
            hbm_out=2 if last else 0,
        )
        pb, qb = p, q
        p, q, *rims = out
    return rims[0][None], rims[1][None]


def solution(mesh):
    model = P(("shot", "gx"), "gy", None)
    field = P("shot", "gx", "gy", None)
    return jax.shard_map(
        on_device,
        mesh=mesh,
        in_specs=(model, model, model, P(), P("shot", None), P("shot", None)) + (field,) * 4,
        out_specs=(field, field),
        check_vma=False,
    )
```
